32 devices in a mesh: row: 8 (over z, core), col: 4 (over y, x).
Axes of the slice: x: 2, y: 2, z: 4, core: 2. Of those that a mesh axis runs over, the one named last changes fastest.
Arguments:
- sources: float32 [64, 16384], P(None, 'row'), may hold values from -8 to 8
- targets: float32 [64, 8192], P(None, 'col'), may hold values from -8 to 8
- source_mass: float32 [16384], P('row'), may hold values from 0.1 to 10
- target_mass: float32 [8192], P('col'), may hold values from 0.1 to 10
Outputs:
- source_potential: float32 [16384], P('row')
- target_potential: float32 [8192], P('col')
- source_map: float32 [64, 16384], P(None, 'row')
- target_map: float32 [64, 8192], P(None, 'col')
The draws below stay inside these ranges and needn't reach their ends.
All inputs are finite; a program needn't handle non-finite values.
Results may differ from the reference program's by a relative error of at most 0.0003.
Values sent between devices are 32-bit elements; how exact they have to be, the bound alone decides.
No kernel may reach another device: no remote copies, remote signals or barrier semaphores. Data moves between devices by JAX's collectives and lax.ppermute only.
A program may use at most 64 MiB of HBM per device.

```python
import math
import jax
import jax.numpy as jnp
from jax import lax

D = 64
ITERS = 3
NS = 16384
NT = 8192


def drawn_points(key, columns):
    points = jax.random.normal(key, (D, columns), jnp.float32) * 0.25
    return jnp.clip(points, -3.0, 3.0)


def draw_sources(key, part):
    return drawn_points(jax.random.fold_in(key, 11), NS)


def draw_targets(key, part):
    return drawn_points(jax.random.fold_in(key, 13), NT)


def levels(rng, dims, shards, smallest, high):
    factor_of, own = 1.0, jax.random.fold_in(rng, 6)
    for axis_at, shards_of in shards:
        draws = jnp.exp(jax.random.uniform(jax.random.fold_in(own, axis_at), (shards_of,), jnp.float32, smallest / len(shards), high / len(shards)))
        factor_of = factor_of * jnp.repeat(draws, dims[axis_at] // shards_of).reshape([-1 if axis == axis_at else 1 for axis in range(len(dims))])
    return factor_of


def setup_inputs(seed: int = 0) -> dict:
    seeds = jax.random.split(jax.random.key(seed), 5)
    sources = draw_sources(jax.random.fold_in(seeds[4], 71), 0)
    targets = draw_targets(jax.random.fold_in(seeds[4], 71), 0)
    source_mass = jnp.clip(jnp.exp(math.log(10.0) - 4.6051702 * jax.random.uniform(seeds[2], (NS,), jnp.float32) ** levels(seeds[2], (NS,), ((0, 8),), -0.2, 0.2)), 0.1, 10.0)
    target_mass = jnp.clip(jnp.exp(math.log(10.0) - 4.6051702 * jax.random.uniform(seeds[3], (NT,), jnp.float32) ** levels(seeds[3], (NT,), ((0, 4),), -0.2, 0.2)), 0.1, 10.0)
    return dict(sources=sources, targets=targets, source_mass=source_mass, target_mass=target_mass)


entropy_scale = 0.25
lowest_start = -1.0e30


def tile_sweep(sources, targets, src_term, tgt_term, with_maps):
    block_rows = min(512, sources.shape[1])
    count = sources.shape[1] // block_rows
    depth = sources.shape[0]
    width = targets.shape[1]
    src_norms = jnp.sum(sources * sources, axis=0)
    tgt_norms = jnp.sum(targets * targets, axis=0)

    def one_block(carry, block_index):
        col_peak, col_total, col_vector = carry
        start = (block_index * block_rows).astype(jnp.int32)
        src_block = lax.dynamic_slice_in_dim(sources, start, block_rows, 1)
        norm_block = lax.dynamic_slice_in_dim(src_norms, start, block_rows, 0)
        term_block = lax.dynamic_slice_in_dim(src_term, start, block_rows, 0)
        cross = lax.dot_general(src_block, targets, (((0,), (0,)), ((), ())), precision=lax.Precision.HIGHEST, preferred_element_type=jnp.float32)
        scores = (2.0 * cross - norm_block[:, None] - tgt_norms[None, :]) / entropy_scale
        row_scores = scores + tgt_term[None, :]
        row_peak = jnp.max(row_scores, axis=1)
        row_weights = jnp.exp(row_scores - row_peak[:, None])
        row_total = jnp.sum(row_weights, axis=1)
        col_scores = scores + term_block[:, None]
        new_peak = jnp.maximum(col_peak, jnp.max(col_scores, axis=0))
        col_weights = jnp.exp(col_scores - new_peak[None, :])
        decay = jnp.exp(col_peak - new_peak)
        col_total = col_total * decay + jnp.sum(col_weights, axis=0)
        if with_maps:
            row_vector = lax.dot_general(targets, row_weights, (((1,), (1,)), ((), ())), precision=lax.Precision.HIGHEST, preferred_element_type=jnp.float32)
            col_vector = col_vector * decay[None, :] + jnp.dot(src_block, col_weights, precision=lax.Precision.HIGHEST, preferred_element_type=jnp.float32)
            return (new_peak, col_total, col_vector), (row_peak, row_total, row_vector)
        return (new_peak, col_total, col_vector), (row_peak, row_total)

    start_carry = (jnp.full((width,), lowest_start, jnp.float32), jnp.zeros((width,), jnp.float32), jnp.zeros((depth, width), jnp.float32))
    final, stacked = lax.scan(one_block, start_carry, jnp.arange(count, dtype=jnp.int32))
    row_peak = stacked[0].reshape(-1)
    row_total = stacked[1].reshape(-1)
    if with_maps:
        row_vector = jnp.transpose(stacked[2], (1, 0, 2)).reshape(depth, -1)
        return (row_peak, row_total, row_vector), final
    return (row_peak, row_total), (final[0], final[1])


def reference(sources, targets, source_mass, target_mass):
    src_log = jnp.log(source_mass)
    tgt_log = jnp.log(target_mass)
    src_pot = jnp.zeros(source_mass.shape, jnp.float32)
    tgt_pot = jnp.zeros(target_mass.shape, jnp.float32)
    for sweep_index in range(ITERS):
        rows, cols = tile_sweep(sources, targets, src_pot / entropy_scale + src_log, tgt_pot / entropy_scale + tgt_log, False)
        src_next = 0.5 * (src_pot - entropy_scale * (rows[0] + jnp.log(rows[1])))
        tgt_next = 0.5 * (tgt_pot - entropy_scale * (cols[0] + jnp.log(cols[1])))
        src_pot, tgt_pot = src_next, tgt_next
    rows, cols = tile_sweep(sources, targets, src_pot / entropy_scale + src_log, tgt_pot / entropy_scale + tgt_log, True)
    source_map = rows[2] / rows[1][None, :]
    target_map = cols[2] / cols[1][None, :]
    return src_pot, tgt_pot, source_map, target_map
```

```python
import functools

import jax
import jax.numpy as jnp
from jax import lax
from jax.experimental import pallas as pl
from jax.experimental.pallas import tpu as pltpu
from jax.sharding import PartitionSpec as P

ITERS = 3
EPS = 0.25
LOG2E = 1.4426950408889634
LN2 = 0.6931471805599453
SHIFT = 85.0
SMALLEST = 2.0**-85
FACTOR_RANGE = 60.0 * LN2
LANES = 128
F32 = jnp.float32
BF16 = jnp.bfloat16
HIGH = lax.Precision.HIGHEST


def split2(a):
    a1 = a.astype(BF16).astype(F32)
    return a1, a - a1


def split3(a):
    a1, rest = split2(a)
    a2, rest = split2(rest)
    return a1, a2, rest


def spread(u, ub):
    for b in range(u.shape[0]):
        ub[b * LANES : (b + 1) * LANES, :] = jnp.broadcast_to(u[b : b + 1, :], (LANES, LANES)).T


def lane_sums(acc, out):
    for b in range(out.shape[0]):
        out[b : b + 1, :] = jnp.sum(acc[b * LANES : (b + 1) * LANES, :].T, axis=0, keepdims=True)


def fold(a):
    return jnp.sum(a.reshape(a.shape[0] // 8, 8, a.shape[1]), axis=0)


def build_operands(x_ref, y_ref, xa, ya):
    d, ns = x_ref.shape
    nt = y_ref.shape[1]
    y = y_ref[...]
    yn = jnp.sum(y * y, axis=0, keepdims=True) * (LOG2E / EPS)
    y1, y2, y3 = (part.astype(BF16) for part in split3(y * (2.0 * LOG2E / EPS)))
    for at, part in enumerate((y1, y2, y1, y2, y3, y1)):
        ya[at * d : (at + 1) * d, :] = part
    m1, m2, m3 = split3(SHIFT - yn)
    row = lax.broadcasted_iota(jnp.int32, (2 * d, nt), 0)
    tail = jnp.where(
        row == 0, m1, jnp.where(row == 1, m2, jnp.where(row == 2, m3, jnp.where(row < 6, 1.0, 0.0)))
    )
    ya[6 * d : 8 * d, :] = tail.astype(BF16)
    lane = lax.broadcasted_iota(jnp.int32, (LANES, 2 * d), 1)

    def block(b, _):
        at = pl.multiple_of(b * LANES, LANES)
        xb = x_ref[:, pl.ds(at, LANES)]
        both = jnp.concatenate([xb, xb], axis=0).T
        norm = jnp.sum(jnp.where(lane < d, both * both, 0.0), axis=1, keepdims=True) * (-LOG2E / EPS)
        x1, x2, x3 = split3(both)
        n1, n2, n3 = split3(norm)
        rows = pl.ds(at, LANES)
        xa[rows, 0 : 2 * d] = x1.astype(BF16)
        xa[rows, 2 * d : 4 * d] = x2.astype(BF16)
        xa[rows, 4 * d : 6 * d] = jnp.where(lane < d, x1, x3).astype(BF16)
        xa[rows, 6 * d : 8 * d] = jnp.where(
            lane < 3,
            1.0,
            jnp.where(lane == 3, n1, jnp.where(lane == 4, n2, jnp.where(lane == 5, n3, 0.0))),
        ).astype(BF16)
        return 0

    lax.fori_loop(0, ns // LANES, block, 0)


def as_row(ref):
    return jnp.concatenate([ref[b : b + 1, :] for b in range(ref.shape[0])], axis=1)


def put_row(row, ref):
    for b in range(ref.shape[0]):
        ref[b : b + 1, :] = row[:, b * LANES : (b + 1) * LANES]


def general_sweep(x_ref, y_ref, r_ref, t_ref, row_lse, col_lse, row_map, col_map, ub):
    d, ns = x_ref.shape
    nt = y_ref.shape[1]
    with_maps = row_map is not None
    spread(r_ref[...], ub)
    y = y_ref[...]
    yn = jnp.sum(y * y, axis=0, keepdims=True)
    t = as_row(t_ref)

    def block(b, carry):
        at = pl.multiple_of(b * LANES, LANES)
        xb = x_ref[:, pl.ds(at, LANES)]
        xt = xb.T
        xn = jnp.sum(xt * xt, axis=1, keepdims=True)
        cross = jnp.dot(xt, y, precision=HIGH, preferred_element_type=F32)
        scores = (2.0 * cross - xn - yn) / EPS
        row_scores = scores + t
        peak = jnp.max(row_scores, axis=1, keepdims=True)
        weights = jnp.exp(row_scores - peak)
        total = jnp.sum(weights, axis=1, keepdims=True)
        row_lse[pl.ds(b, 1), :] = jnp.broadcast_to(peak + jnp.log(total), (LANES, LANES)).T[0:1, :]
        if with_maps:
            vector = lax.dot_general(
                weights / total, y, (((1,), (1,)), ((), ())), precision=HIGH, preferred_element_type=F32
            )
            row_map[0:d, pl.ds(at, LANES)] = jnp.concatenate([vector, vector], axis=1).T[0:d, :]
        col_scores = scores + ub[pl.ds(at, LANES), 0:1]
        new_peak = jnp.maximum(carry[0], jnp.max(col_scores, axis=0, keepdims=True))
        decay = jnp.exp(carry[0] - new_peak)
        col_weights = jnp.exp(col_scores - new_peak)
        total = carry[1] * decay + jnp.sum(col_weights, axis=0, keepdims=True)
        if with_maps:
            col_map[0:d, :] = col_map[0:d, :] * decay + jnp.dot(
                xb, col_weights, precision=HIGH, preferred_element_type=F32
            )
        return new_peak, total

    if with_maps:
        col_map[0:d, :] = jnp.zeros((d, nt), F32)
    start = (jnp.full((1, nt), -1e30, F32), jnp.zeros((1, nt), F32))
    peak, total = lax.fori_loop(0, ns // LANES, block, start)
    put_row(peak + jnp.log(total), col_lse)
    if with_maps:
        col_map[0:d, :] = col_map[0:d, :] / total


def factors(term):
    top = jnp.max(term)
    return jnp.exp(term - top), top, top - jnp.min(term) <= FACTOR_RANGE


def finish(row_ref, col_ref, r_top, t_top, fine):
    rows, cols = row_ref[...], col_ref[...]
    fine = fine & (jnp.min(rows) >= SMALLEST) & (jnp.min(cols) >= SMALLEST)
    row_ref[...] = jnp.log(rows) + (t_top - SHIFT * LN2)
    col_ref[...] = jnp.log(cols) + (r_top - SHIFT * LN2)
    return fine


def form_kernel(x_ref, y_ref, a_ref, b_ref, k_ref, row_ref, col_ref, xa, ya, ub, acc, r_s, t_s, *, rows):
    ns, nt = x_ref.shape[1], y_ref.shape[1]
    r_s[...] = jnp.log(a_ref[...])
    t_s[...] = jnp.log(b_ref[...])
    u, r_top, u_fine = factors(r_s[...])
    v, t_top, v_fine = factors(t_s[...])
    build_operands(x_ref, y_ref, xa, ya)
    spread(u, ub)
    col_ref[...] = v
    acc[...] = jnp.zeros_like(acc)
    wide = 2 * LANES

    def block(cb, _):
        at = pl.multiple_of(cb * wide, wide)
        v0 = col_ref[pl.ds(cb * 2, 1), :]
        v1 = col_ref[pl.ds(cb * 2 + 1, 1), :]
        c0 = jnp.zeros((8, LANES), F32)
        c1 = jnp.zeros((8, LANES), F32)
        for r in range(0, ns, rows):
            z = jnp.dot(xa[r : r + rows, :], ya[:, pl.ds(at, wide)], preferred_element_type=F32)
            k = jnp.exp2(z)
            k_ref[r : r + rows, pl.ds(at, wide)] = k
            k0, k1 = k[:, :LANES], k[:, LANES:]
            acc[r : r + rows, :] += k0 * v0 + k1 * v1
            ur = ub[r : r + rows, :]
            c0 += fold(k0 * ur)
            c1 += fold(k1 * ur)
        col_ref[pl.ds(cb * 2, 1), :] = jnp.sum(c0, axis=0, keepdims=True)
        col_ref[pl.ds(cb * 2 + 1, 1), :] = jnp.sum(c1, axis=0, keepdims=True)
        return 0

    lax.fori_loop(0, nt // wide, block, 0)
    lane_sums(acc, row_ref)
    fine = finish(row_ref, col_ref, r_top, t_top, u_fine & v_fine)

    @pl.when(jnp.logical_not(fine))
    def _():
        general_sweep(x_ref, y_ref, r_s, t_s, row_ref, col_ref, None, None, ub)


def update(pot_ref, lse_ref, mass_ref, new_ref, term):
    new_ref[...] = 0.5 * (pot_ref[...] - EPS * lse_ref[...])
    term[...] = new_ref[...] / EPS + jnp.log(mass_ref[...])


def sums_kernel(
    k_ref, x_ref, y_ref, f_ref, g_ref, rl_ref, cl_ref, a_ref, b_ref,
    fn_ref, gn_ref, row_ref, col_ref, ub, acc, vs, r_s, t_s, *, rows,
):
    update(f_ref, rl_ref, a_ref, fn_ref, r_s)
    update(g_ref, cl_ref, b_ref, gn_ref, t_s)
    u, r_top, u_fine = factors(r_s[...])
    v, t_top, v_fine = factors(t_s[...])
    spread(u, ub)
    vs[...] = v
    ns, nt = k_ref.shape
    tiles = nt // LANES

    def block(rb, cs):
        at = pl.multiple_of(rb * rows, rows)
        ur = ub[pl.ds(at, rows), :]
        total = jnp.zeros((rows, LANES), F32)
        out = []
        for c in range(tiles):
            k = k_ref[pl.ds(at, rows), c * LANES : (c + 1) * LANES]
            total += k * vs[c : c + 1, :]
            out.append(cs[c] + fold(k * ur))
        acc[pl.ds(at, rows), :] = total
        return tuple(out)

    cs = lax.fori_loop(0, ns // rows, block, (jnp.zeros((8, LANES), F32),) * tiles)
    for c in range(tiles):
        col_ref[c : c + 1, :] = jnp.sum(cs[c], axis=0, keepdims=True)
    lane_sums(acc, row_ref)
    fine = finish(row_ref, col_ref, r_top, t_top, u_fine & v_fine)

    @pl.when(jnp.logical_not(fine))
    def _():
        general_sweep(x_ref, y_ref, r_s, t_s, row_ref, col_ref, None, None, ub)


def maps_kernel(
    k_ref, x_ref, y_ref, f_ref, g_ref, rl_ref, cl_ref, a_ref, b_ref,
    fn_ref, gn_ref, rowm_ref, colm_ref, row_s, col_s, ub, wy, xu, acc, cacc, r_s, t_s, *, rows,
):
    d = x_ref.shape[0]
    ns, nt = k_ref.shape
    update(f_ref, rl_ref, a_ref, fn_ref, r_s)
    update(g_ref, cl_ref, b_ref, gn_ref, t_s)
    u, r_top, u_fine = factors(r_s[...])
    v, t_top, v_fine = factors(t_s[...])
    lane = lax.broadcasted_iota(jnp.int32, (LANES, 2 * d), 1)
    sub = lax.broadcasted_iota(jnp.int32, (16, LANES), 0)
    for b in range(nt // LANES):
        at = slice(b * LANES, (b + 1) * LANES)
        vb = v[b : b + 1, :]
        yb = y_ref[:, at] * vb
        p1, p2 = split2(jnp.concatenate([yb, yb], axis=0).T)
        wy[at, 0 : 2 * d] = jnp.where(lane < d, p1, p2).astype(BF16)
        p1, p2 = split2(jnp.broadcast_to(vb, (2 * d, LANES)).T)
        wy[at, 2 * d : 4 * d] = jnp.where(lane == 0, p1, jnp.where(lane == 1, p2, 0.0)).astype(BF16)
    for b in range(ns // LANES):
        at = slice(b * LANES, (b + 1) * LANES)
        uv = u[b : b + 1, :]
        p1, p2 = split2(x_ref[:, at] * uv)
        xu[0:d, at] = p1.astype(BF16)
        xu[d : 2 * d, at] = p2.astype(BF16)
        p1, p2 = split2(jnp.broadcast_to(uv, (16, LANES)))
        xu[2 * d : 2 * d + 16, at] = jnp.where(sub == 0, p1, jnp.where(sub == 1, p2, 0.0)).astype(BF16)
    wide = 2 * LANES
    acc[...] = jnp.zeros_like(acc)

    def block(cb, _):
        at = pl.multiple_of(cb * wide, wide)
        w = wy[pl.ds(at, wide), :]
        ww = jnp.concatenate([w, w], axis=0)
        total = jnp.zeros((xu.shape[0], wide), F32)
        for r in range(0, ns, rows):
            k = k_ref[r : r + rows, pl.ds(at, wide)]
            k1 = k.astype(BF16)
            k2 = (k - k1.astype(F32)).astype(BF16)
            acc[r : r + rows, :] += jnp.dot(
                jnp.concatenate([k1, k2], axis=1), ww, preferred_element_type=F32
            )
            xr = xu[:, r : r + rows]
            total += jnp.dot(
                jnp.concatenate([xr, xr], axis=1),
                jnp.concatenate([k1, k2], axis=0),
                preferred_element_type=F32,
            )
        cacc[:, pl.ds(at, wide)] = total
        return 0

    lax.fori_loop(0, nt // wide, block, 0)
    for b in range(ns // LANES):
        at = slice(b * LANES, (b + 1) * LANES)
        num = acc[at, 0 : 2 * d].T
        den = acc[at, 2 * d : 4 * d].T
        den = den[0:1, :] + den[1:2, :]
        rowm_ref[0:d, at] = (num[0:d, :] + num[d : 2 * d, :]) / den
        row_s[b : b + 1, :] = den
    for b in range(nt // LANES):
        at = slice(b * LANES, (b + 1) * LANES)
        den = cacc[2 * d : 2 * d + 1, at] + cacc[2 * d + 1 : 2 * d + 2, at]
        colm_ref[0:d, at] = (cacc[0:d, at] + cacc[d : 2 * d, at]) / den
        col_s[b : b + 1, :] = den
    fine = finish(row_s, col_s, r_top, t_top, u_fine & v_fine)

    @pl.when(jnp.logical_not(fine))
    def _():
        general_sweep(x_ref, y_ref, r_s, t_s, row_s, col_s, rowm_ref, colm_ref, ub)

    for ref, lse in ((rowm_ref, row_s), (colm_ref, col_s)):
        for b in range(lse.shape[0]):
            ref[d : d + 8, b * LANES : (b + 1) * LANES] = jnp.broadcast_to(lse[b : b + 1, :], (8, LANES))


VM = pl.BlockSpec(memory_space=pltpu.VMEM)
PARAMS = pltpu.CompilerParams(vmem_limit_bytes=36 * 2**20)


def vector(n):
    return jax.ShapeDtypeStruct((n // LANES, LANES), F32)


def scratch(n):
    return pltpu.VMEM((n // LANES, LANES), F32)


def form(x, y, a, b):
    d, ns = x.shape
    nt = y.shape[1]
    return pl.pallas_call(
        functools.partial(form_kernel, rows=256),
        out_shape=(pltpu.VMEM((ns, nt), F32), vector(ns), vector(nt)),
        in_specs=[VM] * 4,
        out_specs=(VM,) * 3,
        scratch_shapes=[
            pltpu.VMEM((ns, 8 * d), BF16),
            pltpu.VMEM((8 * d, nt), BF16),
            pltpu.VMEM((ns, LANES), F32),
            pltpu.VMEM((ns, LANES), F32),
            scratch(ns),
            scratch(nt),
        ],
        compiler_params=PARAMS,
        name="form",
    )(x, y, a, b)


def sums(k, x, y, *vectors):
    ns, nt = k.shape
    return pl.pallas_call(
        functools.partial(sums_kernel, rows=64),
        out_shape=(vector(ns), vector(nt), vector(ns), vector(nt)),
        in_specs=[VM] * 9,
        out_specs=(VM,) * 4,
        scratch_shapes=[
            pltpu.VMEM((ns, LANES), F32),
            pltpu.VMEM((ns, LANES), F32),
            scratch(nt),
            scratch(ns),
            scratch(nt),
        ],
        compiler_params=PARAMS,
        name="sums",
    )(k, x, y, *vectors)


def maps(k, x, y, *vectors):
    d = x.shape[0]
    ns, nt = k.shape
    return pl.pallas_call(
        functools.partial(maps_kernel, rows=512),
        out_shape=(
            vector(ns),
            vector(nt),
            jax.ShapeDtypeStruct((d + 8, ns), F32),
            jax.ShapeDtypeStruct((d + 8, nt), F32),
        ),
        in_specs=[VM] * 9,
        out_specs=(VM,) * 4,
        scratch_shapes=[
            scratch(ns),
            scratch(nt),
            pltpu.VMEM((ns, LANES), F32),
            pltpu.VMEM((nt, 4 * d), BF16),
            pltpu.VMEM((2 * d + 16, ns), BF16),
            pltpu.VMEM((ns, 4 * d), F32),
            pltpu.VMEM((2 * d + 16, nt), F32),
            scratch(ns),
            scratch(nt),
        ],
        compiler_params=PARAMS,
        name="maps",
    )(k, x, y, *vectors)


def merged(first, second):
    peak = jnp.maximum(first, second)
    return peak + jnp.log(jnp.exp(first - peak) + jnp.exp(second - peak))


def lse_over(axis, part):
    n = lax.axis_size(axis)
    step = 1
    while step < n:
        part = merged(part, lax.ppermute(part, axis, [(i, i ^ step) for i in range(n)]))
        step *= 2
    return part


def weighed(parts):
    d = parts[0].shape[0] - 8
    peak = functools.reduce(jnp.maximum, [p[d : d + 1] for p in parts])
    weights = [jnp.exp(p[d : d + 1] - peak) for p in parts]
    total = sum(weights)
    return sum(p[:d] * w for p, w in zip(parts, weights)) / total, peak + jnp.log(total)


def piece(a, index, count):
    width = a.shape[1] // count
    return lax.dynamic_slice_in_dim(a, index * width, width, 1)


def map_over(axis, group, stride, part):
    n = lax.axis_size(axis)
    me = lax.axis_index(axis)
    place = (me // stride) % group

    def pairs(k):
        return [
            (i, i + (((i // stride) + k) % group - (i // stride) % group) * stride) for i in range(n)
        ]

    got = [piece(part, place, group)]
    for k in range(1, group):
        got.append(lax.ppermute(piece(part, (place + k) % group, group), axis, pairs(k)))
    own, _ = weighed(got)
    return gathered(axis, group, pairs, place, own)


def gathered(axis, group, pairs, place, own):
    width = own.shape[1]
    out = jnp.zeros((own.shape[0], width * group), F32)
    out = lax.dynamic_update_slice_in_dim(out, own, place * width, 1)
    for k in range(1, group):
        other = lax.ppermute(own, axis, pairs(k))
        out = lax.dynamic_update_slice_in_dim(out, other, ((place - k) % group) * width, 1)
    return out


def body(sources, targets, source_mass, target_mass):
    a = source_mass.reshape(-1, LANES)
    b = target_mass.reshape(-1, LANES)
    f = jnp.zeros_like(a)
    g = jnp.zeros_like(b)
    k, row_part, col_part = form(sources, targets, a, b)
    for sweep in range(ITERS):
        col_lse = lse_over("row", col_part)
        row_lse = lse_over("col", row_part)
        if sweep < ITERS - 1:
            f, g, row_part, col_part = sums(k, sources, targets, f, g, row_lse, col_lse, a, b)
        else:
            f, g, row_map, col_map = maps(k, sources, targets, f, g, row_lse, col_lse, a, b)
    rows = lax.axis_size("row")
    me = lax.axis_index("row")
    half = me % 2
    pair = [(i, i ^ 1) for i in range(rows)]
    mine = piece(col_map, half, 2)
    other = lax.ppermute(piece(col_map, 1 - half, 2), "row", pair)
    values, lse = weighed([mine, other])
    chip = jnp.concatenate([values, jnp.broadcast_to(lse, (8, lse.shape[1]))], axis=0)
    ours = map_over("row", rows // 2, 2, chip)
    theirs = lax.ppermute(ours, "row", pair)
    target_map = jnp.where(
        half == 0, jnp.concatenate([ours, theirs], axis=1), jnp.concatenate([theirs, ours], axis=1)
    )
    source_map = map_over("col", lax.axis_size("col"), 1, row_map)
    return f.reshape(-1), g.reshape(-1), source_map, target_map


def solution(mesh):
    in_specs = (P(None, "row"), P(None, "col"), P("row"), P("col"))
    out_specs = (P("row"), P("col"), P(None, "row"), P(None, "col"))
    return jax.shard_map(body, mesh=mesh, in_specs=in_specs, out_specs=out_specs, check_vma=False)
```

```python
import functools

import jax
import jax.numpy as jnp
from jax import lax
from jax.experimental import pallas as pl
from jax.experimental.pallas import tpu as pltpu
from jax.sharding import PartitionSpec as P

ITERS = 3
EPS = 0.25
LOG2E = 1.4426950408889634
LN2 = 0.6931471805599453
SHIFT = 85.0
SMALLEST = 2.0**-85
FACTOR_RANGE = 60.0 * LN2
LANES = 128
F32 = jnp.float32
BF16 = jnp.bfloat16
HIGH = lax.Precision.HIGHEST


def split2(a):
    a1 = a.astype(BF16).astype(F32)
    return a1, a - a1


def split3(a):
    a1, rest = split2(a)
    a2, rest = split2(rest)
    return a1, a2, rest


def spread(u, ub):
    for b in range(u.shape[0]):
        ub[b * LANES : (b + 1) * LANES, :] = jnp.broadcast_to(u[b : b + 1, :], (LANES, LANES)).T


def lane_sums(acc, out):
    for b in range(out.shape[0]):
        out[b : b + 1, :] = jnp.sum(acc[b * LANES : (b + 1) * LANES, :].T, axis=0, keepdims=True)


def fold(a):
    return jnp.sum(a.reshape(a.shape[0] // 8, 8, a.shape[1]), axis=0)


def build_operands(x_ref, y_ref, xa, ya):
    d, ns = x_ref.shape
    nt = y_ref.shape[1]
    y = y_ref[...]
    yn = jnp.sum(y * y, axis=0, keepdims=True) * (LOG2E / EPS)
    y1, y2, y3 = (part.astype(BF16) for part in split3(y * (2.0 * LOG2E / EPS)))
    for at, part in enumerate((y1, y2, y1, y2, y3, y1)):
        ya[at * d : (at + 1) * d, :] = part
    m1, m2, m3 = split3(SHIFT - yn)
    row = lax.broadcasted_iota(jnp.int32, (2 * d, nt), 0)
    tail = jnp.where(
        row == 0, m1, jnp.where(row == 1, m2, jnp.where(row == 2, m3, jnp.where(row < 6, 1.0, 0.0)))
    )
    ya[6 * d : 8 * d, :] = tail.astype(BF16)
    lane = lax.broadcasted_iota(jnp.int32, (LANES, 2 * d), 1)

    def block(b, _):
        at = pl.multiple_of(b * LANES, LANES)
        xb = x_ref[:, pl.ds(at, LANES)]
        both = jnp.concatenate([xb, xb], axis=0).T
        norm = jnp.sum(jnp.where(lane < d, both * both, 0.0), axis=1, keepdims=True) * (-LOG2E / EPS)
        x1, x2, x3 = split3(both)
        n1, n2, n3 = split3(norm)
        rows = pl.ds(at, LANES)
        xa[rows, 0 : 2 * d] = x1.astype(BF16)
        xa[rows, 2 * d : 4 * d] = x2.astype(BF16)
        xa[rows, 4 * d : 6 * d] = jnp.where(lane < d, x1, x3).astype(BF16)
        xa[rows, 6 * d : 8 * d] = jnp.where(
            lane < 3,
            1.0,
            jnp.where(lane == 3, n1, jnp.where(lane == 4, n2, jnp.where(lane == 5, n3, 0.0))),
        ).astype(BF16)
        return 0

    lax.fori_loop(0, ns // LANES, block, 0)


def as_row(ref):
    return jnp.concatenate([ref[b : b + 1, :] for b in range(ref.shape[0])], axis=1)


def put_row(row, ref):
    for b in range(ref.shape[0]):
        ref[b : b + 1, :] = row[:, b * LANES : (b + 1) * LANES]


def general_sweep(x_ref, y_ref, r_ref, t_ref, row_lse, col_lse, row_map, col_map, ub):
    d, ns = x_ref.shape
    nt = y_ref.shape[1]
    with_maps = row_map is not None
    spread(r_ref[...], ub)
    y = y_ref[...]
    yn = jnp.sum(y * y, axis=0, keepdims=True)
    t = as_row(t_ref)

    def block(b, carry):
        at = pl.multiple_of(b * LANES, LANES)
        xb = x_ref[:, pl.ds(at, LANES)]
        xt = xb.T
        xn = jnp.sum(xt * xt, axis=1, keepdims=True)
        cross = jnp.dot(xt, y, precision=HIGH, preferred_element_type=F32)
        scores = (2.0 * cross - xn - yn) / EPS
        row_scores = scores + t
        peak = jnp.max(row_scores, axis=1, keepdims=True)
        weights = jnp.exp(row_scores - peak)
        total = jnp.sum(weights, axis=1, keepdims=True)
        row_lse[pl.ds(b, 1), :] = jnp.broadcast_to(peak + jnp.log(total), (LANES, LANES)).T[0:1, :]
        if with_maps:
            vector = lax.dot_general(
                weights / total, y, (((1,), (1,)), ((), ())), precision=HIGH, preferred_element_type=F32
            )
            row_map[0:d, pl.ds(at, LANES)] = jnp.concatenate([vector, vector], axis=1).T[0:d, :]
        col_scores = scores + ub[pl.ds(at, LANES), 0:1]
        new_peak = jnp.maximum(carry[0], jnp.max(col_scores, axis=0, keepdims=True))
        decay = jnp.exp(carry[0] - new_peak)
        col_weights = jnp.exp(col_scores - new_peak)
        total = carry[1] * decay + jnp.sum(col_weights, axis=0, keepdims=True)
        if with_maps:
            col_map[0:d, :] = col_map[0:d, :] * decay + jnp.dot(
                xb, col_weights, precision=HIGH, preferred_element_type=F32
            )
        return new_peak, total

    if with_maps:
        col_map[0:d, :] = jnp.zeros((d, nt), F32)
    start = (jnp.full((1, nt), -1e30, F32), jnp.zeros((1, nt), F32))
    peak, total = lax.fori_loop(0, ns // LANES, block, start)
    put_row(peak + jnp.log(total), col_lse)
    if with_maps:
        col_map[0:d, :] = col_map[0:d, :] / total


def factors(term):
    top = jnp.max(term)
    return jnp.exp(term - top), top, top - jnp.min(term) <= FACTOR_RANGE


def finish(row_ref, col_ref, r_top, t_top, fine):
    rows, cols = row_ref[...], col_ref[...]
    fine = fine & (jnp.min(rows) >= SMALLEST) & (jnp.min(cols) >= SMALLEST)
    row_ref[...] = jnp.log(rows) + (t_top - SHIFT * LN2)
    col_ref[...] = jnp.log(cols) + (r_top - SHIFT * LN2)
    return fine


def form_kernel(x_ref, y_ref, a_ref, b_ref, k_ref, row_ref, col_ref, xa, ya, ub, acc, r_s, t_s, *, rows):
    ns, nt = x_ref.shape[1], y_ref.shape[1]
    r_s[...] = jnp.log(a_ref[...])
    t_s[...] = jnp.log(b_ref[...])
    u, r_top, u_fine = factors(r_s[...])
    v, t_top, v_fine = factors(t_s[...])
    build_operands(x_ref, y_ref, xa, ya)
    spread(u, ub)
    col_ref[...] = v
    acc[...] = jnp.zeros_like(acc)
    wide = 2 * LANES

    def block(cb, _):
        at = pl.multiple_of(cb * wide, wide)
        v0 = col_ref[pl.ds(cb * 2, 1), :]
        v1 = col_ref[pl.ds(cb * 2 + 1, 1), :]
        c0 = jnp.zeros((8, LANES), F32)
        c1 = jnp.zeros((8, LANES), F32)
        for r in range(0, ns, rows):
            z = jnp.dot(xa[r : r + rows, :], ya[:, pl.ds(at, wide)], preferred_element_type=F32)
            k = jnp.exp2(z)
            k_ref[r : r + rows, pl.ds(at, wide)] = k
            k0, k1 = k[:, :LANES], k[:, LANES:]
            acc[r : r + rows, :] += k0 * v0 + k1 * v1
            ur = ub[r : r + rows, :]
            c0 += fold(k0 * ur)
            c1 += fold(k1 * ur)
        col_ref[pl.ds(cb * 2, 1), :] = jnp.sum(c0, axis=0, keepdims=True)
        col_ref[pl.ds(cb * 2 + 1, 1), :] = jnp.sum(c1, axis=0, keepdims=True)
        return 0

    lax.fori_loop(0, nt // wide, block, 0)
    lane_sums(acc, row_ref)
    fine = finish(row_ref, col_ref, r_top, t_top, u_fine & v_fine)

    @pl.when(jnp.logical_not(fine))
    def _():
        general_sweep(x_ref, y_ref, r_s, t_s, row_ref, col_ref, None, None, ub)


def update(pot_ref, lse_ref, mass_ref, new_ref, term):
    new_ref[...] = 0.5 * (pot_ref[...] - EPS * lse_ref[...])
    term[...] = new_ref[...] / EPS + jnp.log(mass_ref[...])


def sums_kernel(
    k_ref, x_ref, y_ref, f_ref, g_ref, rl_ref, cl_ref, a_ref, b_ref,
    kept_ref, fn_ref, gn_ref, row_ref, col_ref, ub, acc, vs, r_s, t_s, *, rows,
):
    update(f_ref, rl_ref, a_ref, fn_ref, r_s)
    update(g_ref, cl_ref, b_ref, gn_ref, t_s)
    u, r_top, u_fine = factors(r_s[...])
    v, t_top, v_fine = factors(t_s[...])
    spread(u, ub)
    vs[...] = v
    ns, nt = k_ref.shape
    tiles = nt // LANES

    def block(rb, cs):
        at = pl.multiple_of(rb * rows, rows)
        ur = ub[pl.ds(at, rows), :]
        total = jnp.zeros((rows, LANES), F32)
        out = []
        for c in range(tiles):
            k = k_ref[pl.ds(at, rows), c * LANES : (c + 1) * LANES]
            total += k * vs[c : c + 1, :]
            out.append(cs[c] + fold(k * ur))
        acc[pl.ds(at, rows), :] = total
        return tuple(out)

    cs = lax.fori_loop(0, ns // rows, block, (jnp.zeros((8, LANES), F32),) * tiles)
    for c in range(tiles):
        col_ref[c : c + 1, :] = jnp.sum(cs[c], axis=0, keepdims=True)
    lane_sums(acc, row_ref)
    fine = finish(row_ref, col_ref, r_top, t_top, u_fine & v_fine)

    @pl.when(jnp.logical_not(fine))
    def _():
        general_sweep(x_ref, y_ref, r_s, t_s, row_ref, col_ref, None, None, ub)


def maps_kernel(
    k_ref, x_ref, y_ref, f_ref, g_ref, rl_ref, cl_ref, a_ref, b_ref,
    fn_ref, gn_ref, rowm_ref, colm_ref, row_s, col_s, ub, wy, xu, acc, cacc, r_s, t_s, *, rows,
):
    d = x_ref.shape[0]
    ns, nt = k_ref.shape
    update(f_ref, rl_ref, a_ref, fn_ref, r_s)
    update(g_ref, cl_ref, b_ref, gn_ref, t_s)
    u, r_top, u_fine = factors(r_s[...])
    v, t_top, v_fine = factors(t_s[...])
    lane = lax.broadcasted_iota(jnp.int32, (LANES, 2 * d), 1)
    sub = lax.broadcasted_iota(jnp.int32, (16, LANES), 0)
    for b in range(nt // LANES):
        at = slice(b * LANES, (b + 1) * LANES)
        vb = v[b : b + 1, :]
        yb = y_ref[:, at] * vb
        p1, p2 = split2(jnp.concatenate([yb, yb], axis=0).T)
        wy[at, 0 : 2 * d] = jnp.where(lane < d, p1, p2).astype(BF16)
        p1, p2 = split2(jnp.broadcast_to(vb, (2 * d, LANES)).T)
        wy[at, 2 * d : 4 * d] = jnp.where(lane == 0, p1, jnp.where(lane == 1, p2, 0.0)).astype(BF16)
    for b in range(ns // LANES):
        at = slice(b * LANES, (b + 1) * LANES)
        uv = u[b : b + 1, :]
        p1, p2 = split2(x_ref[:, at] * uv)
        xu[0:d, at] = p1.astype(BF16)
        xu[d : 2 * d, at] = p2.astype(BF16)
        p1, p2 = split2(jnp.broadcast_to(uv, (16, LANES)))
        xu[2 * d : 2 * d + 16, at] = jnp.where(sub == 0, p1, jnp.where(sub == 1, p2, 0.0)).astype(BF16)
    wide = 2 * LANES
    acc[...] = jnp.zeros_like(acc)

    def block(cb, _):
        at = pl.multiple_of(cb * wide, wide)
        w = wy[pl.ds(at, wide), :]
        ww = jnp.concatenate([w, w], axis=0)
        total = jnp.zeros((xu.shape[0], wide), F32)
        for r in range(0, ns, rows):
            k = k_ref[r : r + rows, pl.ds(at, wide)]
            k1 = k.astype(BF16)
            k2 = (k - k1.astype(F32)).astype(BF16)
            acc[r : r + rows, :] += jnp.dot(
                jnp.concatenate([k1, k2], axis=1), ww, preferred_element_type=F32
            )
            xr = xu[:, r : r + rows]
            total += jnp.dot(
                jnp.concatenate([xr, xr], axis=1),
                jnp.concatenate([k1, k2], axis=0),
                preferred_element_type=F32,
            )
        cacc[:, pl.ds(at, wide)] = total
        return 0

    lax.fori_loop(0, nt // wide, block, 0)
    for b in range(ns // LANES):
        at = slice(b * LANES, (b + 1) * LANES)
        num = acc[at, 0 : 2 * d].T
        den = acc[at, 2 * d : 4 * d].T
        den = den[0:1, :] + den[1:2, :]
        rowm_ref[0:d, at] = (num[0:d, :] + num[d : 2 * d, :]) / den
        row_s[b : b + 1, :] = den
    for b in range(nt // LANES):
        at = slice(b * LANES, (b + 1) * LANES)
        den = cacc[2 * d : 2 * d + 1, at] + cacc[2 * d + 1 : 2 * d + 2, at]
        colm_ref[0:d, at] = (cacc[0:d, at] + cacc[d : 2 * d, at]) / den
        col_s[b : b + 1, :] = den
    fine = finish(row_s, col_s, r_top, t_top, u_fine & v_fine)

    @pl.when(jnp.logical_not(fine))
    def _():
        general_sweep(x_ref, y_ref, r_s, t_s, row_s, col_s, rowm_ref, colm_ref, ub)

    for ref, lse in ((rowm_ref, row_s), (colm_ref, col_s)):
        for b in range(lse.shape[0]):
            ref[d : d + 8, b * LANES : (b + 1) * LANES] = jnp.broadcast_to(lse[b : b + 1, :], (8, LANES))


VM = pl.BlockSpec(memory_space=pltpu.VMEM)
PARAMS = pltpu.CompilerParams(vmem_limit_bytes=24 * 2**20)


def vector(n):
    return jax.ShapeDtypeStruct((n // LANES, LANES), F32)


def scratch(n):
    return pltpu.VMEM((n // LANES, LANES), F32)


def form(x, y, a, b):
    d, ns = x.shape
    nt = y.shape[1]
    return pl.pallas_call(
        functools.partial(form_kernel, rows=256),
        out_shape=(pltpu.VMEM((ns, nt), F32), vector(ns), vector(nt)),
        in_specs=[VM] * 4,
        out_specs=(VM,) * 3,
        scratch_shapes=[
            pltpu.VMEM((ns, 8 * d), BF16),
            pltpu.VMEM((8 * d, nt), BF16),
            pltpu.VMEM((ns, LANES), F32),
            pltpu.VMEM((ns, LANES), F32),
            scratch(ns),
            scratch(nt),
        ],
        compiler_params=PARAMS,
        name="form",
    )(x, y, a, b)


def sums(k, x, y, *vectors):
    ns, nt = k.shape
    return pl.pallas_call(
        functools.partial(sums_kernel, rows=64),
        out_shape=(pltpu.VMEM((ns, nt), F32), vector(ns), vector(nt), vector(ns), vector(nt)),
        in_specs=[VM] * 9,
        out_specs=(VM,) * 5,
        input_output_aliases={0: 0},
        scratch_shapes=[
            pltpu.VMEM((ns, LANES), F32),
            pltpu.VMEM((ns, LANES), F32),
            scratch(nt),
            scratch(ns),
            scratch(nt),
        ],
        compiler_params=PARAMS,
        name="sums",
    )(k, x, y, *vectors)


def maps(k, x, y, *vectors):
    d = x.shape[0]
    ns, nt = k.shape
    return pl.pallas_call(
        functools.partial(maps_kernel, rows=512),
        out_shape=(
            vector(ns),
            vector(nt),
            jax.ShapeDtypeStruct((d + 8, ns), F32),
            jax.ShapeDtypeStruct((d + 8, nt), F32),
        ),
        in_specs=[VM] * 9,
        out_specs=(VM,) * 4,
        scratch_shapes=[
            scratch(ns),
            scratch(nt),
            pltpu.VMEM((ns, LANES), F32),
            pltpu.VMEM((nt, 4 * d), BF16),
            pltpu.VMEM((2 * d + 16, ns), BF16),
            pltpu.VMEM((ns, 4 * d), F32),
            pltpu.VMEM((2 * d + 16, nt), F32),
            scratch(ns),
            scratch(nt),
        ],
        compiler_params=PARAMS,
        name="maps",
    )(k, x, y, *vectors)


def merged(first, second):
    peak = jnp.maximum(first, second)
    return peak + jnp.log(jnp.exp(first - peak) + jnp.exp(second - peak))


def lse_over(axis, part):
    n = lax.axis_size(axis)
    step = n // 2
    while step:
        part = merged(part, lax.ppermute(part, axis, [(i, i ^ step) for i in range(n)]))
        step //= 2
    return part


def weighed(parts):
    d = parts[0].shape[0] - 8
    peak = functools.reduce(jnp.maximum, [p[d : d + 1] for p in parts])
    weights = [jnp.exp(p[d : d + 1] - peak) for p in parts]
    total = sum(weights)
    return sum(p[:d] * w for p, w in zip(parts, weights)) / total, peak + jnp.log(total)


def pairs(n, group, stride, k):
    return [(i, i + (((i // stride) + k) % group - (i // stride) % group) * stride) for i in range(n)]


def places(index, group, stride, width):
    own = (index // stride) % group
    return [(own + k) % group * width for k in range(group)]


def piece(a, at, count):
    zero = jnp.zeros((), at.dtype)
    return lax.dynamic_slice(
        a, (zero, at), (a.shape[0], a.shape[1] // count), allow_negative_indices=False
    )


def put(a, part, at):
    zero = jnp.zeros((), at.dtype)
    return lax.dynamic_update_slice(a, part, (zero, at), allow_negative_indices=False)


def map_over(axis, place, stride, part):
    n, group = lax.axis_size(axis), len(place)
    got = [piece(part, place[0], group)]
    for k in range(1, group):
        got.append(lax.ppermute(piece(part, place[k], group), axis, pairs(n, group, stride, k)))
    own, _ = weighed(got)
    width = own.shape[1]
    out = jnp.zeros((own.shape[0], width * group), F32)
    out = put(out, own, place[0])
    for k in range(1, group):
        other = lax.ppermute(own, axis, pairs(n, group, stride, k))
        out = put(out, other, place[-k])
    return out


def body(sources, targets, source_mass, target_mass):
    rows, cols = lax.axis_size("row"), lax.axis_size("col")
    index = lax.axis_index("row")
    ns, nt = sources.shape[1], targets.shape[1]
    halves = places(index, 2, 1, nt // 2)
    row_places = places(index, rows // 2, 2, nt // rows)
    col_places = places(lax.axis_index("col"), cols, 1, ns // cols)
    sources, halves, row_places, col_places = lax.optimization_barrier(
        (sources, halves, row_places, col_places)
    )
    a = source_mass.reshape(-1, LANES)
    b = target_mass.reshape(-1, LANES)
    f = jnp.zeros_like(a)
    g = jnp.zeros_like(b)
    k, row_part, col_part = form(sources, targets, a, b)
    for sweep in range(ITERS):
        col_lse = lse_over("row", col_part)
        row_lse = lse_over("col", row_part)
        if sweep < ITERS - 1:
            k, f, g, row_part, col_part = sums(k, sources, targets, f, g, row_lse, col_lse, a, b)
        else:
            f, g, row_map, col_map = maps(k, sources, targets, f, g, row_lse, col_lse, a, b)
    pair = pairs(rows, 2, 1, 1)
    mine = piece(col_map, halves[0], 2)
    other = lax.ppermute(piece(col_map, halves[1], 2), "row", pair)
    values, lse = weighed([mine, other])
    chip = jnp.concatenate([values, jnp.broadcast_to(lse, (8, lse.shape[1]))], axis=0)
    ours = map_over("row", row_places, 2, chip)
    theirs = lax.ppermute(ours, "row", pair)
    target_map = jnp.where(
        halves[0] == 0, jnp.concatenate([ours, theirs], axis=1), jnp.concatenate([theirs, ours], axis=1)
    )
    source_map = map_over("col", col_places, 1, row_map)
    return f.reshape(-1), g.reshape(-1), source_map, target_map


def solution(mesh):
    in_specs = (P(None, "row"), P(None, "col"), P("row"), P("col"))
    out_specs = (P("row"), P("col"), P(None, "row"), P(None, "col"))
    return jax.shard_map(body, mesh=mesh, in_specs=in_specs, out_specs=out_specs, check_vma=False)
```

```python
import functools

import jax
import jax.numpy as jnp
from jax import lax
from jax.experimental import pallas as pl
from jax.experimental.pallas import tpu as pltpu
from jax.sharding import PartitionSpec as P

ITERS = 3
EPS = 0.25
LOG2E = 1.4426950408889634
LN2 = 0.6931471805599453
SHIFT = 85.0
SMALLEST = 2.0**-85
FACTOR_RANGE = 60.0 * LN2
LANES = 128
F32 = jnp.float32
BF16 = jnp.bfloat16
HIGH = lax.Precision.HIGHEST


def split2(a):
    a1 = a.astype(BF16).astype(F32)
    return a1, a - a1


def split3(a):
    a1, rest = split2(a)
    a2, rest = split2(rest)
    return a1, a2, rest


def spread(u, ub):
    for b in range(u.shape[0]):
        ub[b * LANES : (b + 1) * LANES, :] = jnp.broadcast_to(u[b : b + 1, :], (LANES, LANES)).T


def lane_sums(acc, out):
    for b in range(out.shape[0]):
        out[b : b + 1, :] = jnp.sum(acc[b * LANES : (b + 1) * LANES, :].T, axis=0, keepdims=True)


def fold(a):
    return jnp.sum(a.reshape(a.shape[0] // 8, 8, a.shape[1]), axis=0)


def build_operands(x_ref, y_ref, xa, ya):
    d, ns = x_ref.shape
    nt = y_ref.shape[1]
    wide = 2 * LANES
    sub = lax.broadcasted_iota(jnp.int32, (16, wide), 0)
    lane = lax.broadcasted_iota(jnp.int32, (LANES, 2 * d), 1)

    def tail(row, parts):
        out = jnp.zeros(row.shape, F32)
        for at, part in enumerate(parts):
            out = jnp.where(row == at, part, out)
        return out

    def target_block(b, _):
        cols = pl.ds(pl.multiple_of(b * wide, wide), wide)
        y = y_ref[:, cols]
        norm = split3(SHIFT - jnp.sum(y * y, axis=0, keepdims=True) * (LOG2E / EPS))
        y1, y2, y3 = (part.astype(BF16) for part in split3(y * (2.0 * LOG2E / EPS)))
        for at, part in enumerate((y1, y2, y1, y2, y3, y1)):
            ya[at * d : (at + 1) * d, cols] = part
        ya[6 * d : 6 * d + 16, cols] = tail(sub, norm + (1.0, 1.0, 1.0)).astype(BF16)
        ya[6 * d + 16 : 8 * d, cols] = jnp.zeros((2 * d - 16, wide), BF16)
        return 0

    lax.fori_loop(0, nt // wide, target_block, 0, unroll=4)

    def source_block(b, _):
        rows = pl.ds(pl.multiple_of(b * LANES, LANES), LANES)
        x = x_ref[:, rows]
        norm = split3(jnp.sum(x * x, axis=0, keepdims=True) * (-LOG2E / EPS))
        x1, x2, x3 = split3(jnp.concatenate([x, x], axis=0).T)
        xa[rows, 0 : 2 * d] = x1.astype(BF16)
        xa[rows, 2 * d : 4 * d] = x2.astype(BF16)
        xa[rows, 4 * d : 6 * d] = jnp.where(lane < d, x1, x3).astype(BF16)
        last = tail(sub[:8, :LANES], (1.0, 1.0, 1.0) + norm)
        last = jnp.concatenate([last, jnp.zeros((2 * d - 8, LANES), F32)], axis=0)
        xa[rows, 6 * d : 8 * d] = last.T.astype(BF16)
        return 0

    lax.fori_loop(0, ns // LANES, source_block, 0, unroll=4)


def as_row(ref):
    return jnp.concatenate([ref[b : b + 1, :] for b in range(ref.shape[0])], axis=1)


def put_row(row, ref):
    for b in range(ref.shape[0]):
        ref[b : b + 1, :] = row[:, b * LANES : (b + 1) * LANES]


def rows_sweep(x_ref, y_ref, t_ref, lse, out):
    d, ns = x_ref.shape
    y = y_ref[...]
    yn = jnp.sum(y * y, axis=0, keepdims=True)
    t = as_row(t_ref)

    def block(b, _):
        at = pl.multiple_of(b * LANES, LANES)
        xt = jnp.concatenate([x_ref[:, pl.ds(at, LANES)]] * 2, axis=0).T[:, 0:d]
        xn = jnp.sum(xt * xt, axis=1, keepdims=True)
        cross = jnp.dot(xt, y, precision=HIGH, preferred_element_type=F32)
        scores = (2.0 * cross - xn - yn) / EPS + t
        peak = jnp.max(scores, axis=1, keepdims=True)
        weights = jnp.exp(scores - peak)
        total = jnp.sum(weights, axis=1, keepdims=True)
        lse[pl.ds(b, 1), :] = jnp.broadcast_to(peak + jnp.log(total), (LANES, LANES)).T[0:1, :]
        if out is not None:
            vector = lax.dot_general(
                weights / total, y, (((1,), (1,)), ((), ())), precision=HIGH, preferred_element_type=F32
            )
            out[0:d, pl.ds(at, LANES)] = jnp.concatenate([vector, vector], axis=1).T[0:d, :]
        return 0

    lax.fori_loop(0, ns // LANES, block, 0)


def cols_sweep(x_ref, y_ref, r_ref, lse, out, ub):
    d, ns = x_ref.shape
    nt = y_ref.shape[1]
    spread(r_ref[...], ub)
    y = y_ref[...]
    yn = jnp.sum(y * y, axis=0, keepdims=True)

    def block(b, carry):
        at = pl.multiple_of(b * LANES, LANES)
        xb = x_ref[:, pl.ds(at, LANES)]
        xt = jnp.concatenate([xb, xb], axis=0).T[:, 0:d]
        xn = jnp.sum(xt * xt, axis=1, keepdims=True)
        cross = jnp.dot(xt, y, precision=HIGH, preferred_element_type=F32)
        scores = (2.0 * cross - xn - yn) / EPS + ub[pl.ds(at, LANES), 0:1]
        peak = jnp.maximum(carry[0], jnp.max(scores, axis=0, keepdims=True))
        decay = jnp.exp(carry[0] - peak)
        weights = jnp.exp(scores - peak)
        total = carry[1] * decay + jnp.sum(weights, axis=0, keepdims=True)
        if out is not None:
            out[0:d, :] = out[0:d, :] * decay + jnp.dot(
                xb, weights, precision=HIGH, preferred_element_type=F32
            )
        return peak, total

    if out is not None:
        out[0:d, :] = jnp.zeros((d, nt), F32)
    start = (jnp.full((1, nt), -1e30, F32), jnp.zeros((1, nt), F32))
    peak, total = lax.fori_loop(0, ns // LANES, block, start)
    put_row(peak + jnp.log(total), lse)
    if out is not None:
        out[0:d, :] = out[0:d, :] / total


def factors(term):
    top = jnp.max(term)
    return jnp.exp(term - top), top, top - jnp.min(term) <= FACTOR_RANGE


def finish(ref, top, fine):
    values = ref[...]
    ref[...] = jnp.log(values) + (top - SHIFT * LN2)
    return fine & (jnp.min(values) >= SMALLEST)


def fetch(pairs, sem):
    copies = [pltpu.make_async_copy(src, dst, sem.at[i]) for i, (src, dst) in enumerate(pairs)]
    for copy in copies:
        copy.start()
    for copy in copies:
        copy.wait()


def form_kernel(
    x_hbm, y_hbm, a_hbm, b_hbm, k_ref, row_ref, col_ref, x_ref, y_ref, xa, ya, ub, acc, r_s, t_s, sem, *, rows
):
    ns, nt = x_ref.shape[1], y_ref.shape[1]
    fetch(((x_hbm, x_ref), (y_hbm, y_ref), (a_hbm, r_s), (b_hbm, t_s)), sem)
    r_s[...] = jnp.log(r_s[...])
    t_s[...] = jnp.log(t_s[...])
    u, r_top, u_fine = factors(r_s[...])
    v, t_top, v_fine = factors(t_s[...])
    build_operands(x_ref, y_ref, xa, ya)
    spread(u, ub)
    col_ref[...] = v
    acc[...] = jnp.zeros_like(acc)
    tiles = 4 if nt % (4 * LANES) == 0 else 1
    wide = tiles * LANES

    def block(cb, _):
        at = pl.multiple_of(cb * wide, wide)
        vs = [col_ref[pl.ds(cb * tiles + t, 1), :] for t in range(tiles)]
        cs = [jnp.zeros((8, LANES), F32)] * tiles
        for r in range(0, ns, rows):
            z = jnp.dot(xa[r : r + rows, :], ya[:, pl.ds(at, wide)], preferred_element_type=F32)
            k = jnp.exp2(z)
            k_ref[r : r + rows, pl.ds(at, wide)] = k
            ur = ub[r : r + rows, :]
            total = acc[r : r + rows, :]
            for t in range(tiles):
                kt = k[:, t * LANES : (t + 1) * LANES]
                total += kt * vs[t]
                cs[t] += fold(kt * ur)
            acc[r : r + rows, :] = total
        for t in range(tiles):
            col_ref[pl.ds(cb * tiles + t, 1), :] = jnp.sum(cs[t], axis=0, keepdims=True)
        return 0

    lax.fori_loop(0, nt // wide, block, 0)
    lane_sums(acc, row_ref)
    rows_fine = finish(row_ref, t_top, v_fine)
    cols_fine = finish(col_ref, r_top, u_fine)

    @pl.when(jnp.logical_not(rows_fine))
    def _():
        rows_sweep(x_ref, y_ref, t_s, row_ref, None)

    @pl.when(jnp.logical_not(cols_fine))
    def _():
        cols_sweep(x_ref, y_ref, r_s, col_ref, None, ub)


def update(pot_ref, lse_ref, mass_ref, new_ref, term):
    new_ref[...] = 0.5 * (pot_ref[...] - EPS * lse_ref[...])
    term[...] = new_ref[...] / EPS + jnp.log(mass_ref[...])


def cols_kernel(k_ref, x_hbm, y_hbm, f_ref, rl_ref, a_ref, fn_ref, col_ref, ub, r_s, x_ref, y_ref, sem, *, rows):
    update(f_ref, rl_ref, a_ref, fn_ref, r_s)
    u, r_top, fine = factors(r_s[...])
    spread(u, ub)
    ns, nt = k_ref.shape
    tiles = nt // LANES

    def block(rb, cs):
        at = pl.ds(pl.multiple_of(rb * rows, rows), rows)
        ur = ub[at, :]
        return tuple(
            cs[c] + fold(k_ref[at, c * LANES : (c + 1) * LANES] * ur) for c in range(tiles)
        )

    cs = lax.fori_loop(0, ns // rows, block, (jnp.zeros((8, LANES), F32),) * tiles)
    for c in range(tiles):
        col_ref[c : c + 1, :] = jnp.sum(cs[c], axis=0, keepdims=True)
    fine = finish(col_ref, r_top, fine)

    @pl.when(jnp.logical_not(fine))
    def _():
        fetch(((x_hbm, x_ref), (y_hbm, y_ref)), sem)
        cols_sweep(x_ref, y_ref, r_s, col_ref, None, ub)


def rows_kernel(k_ref, x_hbm, y_hbm, g_ref, cl_ref, b_ref, gn_ref, row_ref, acc, vs, t_s, x_ref, y_ref, sem, *, rows):
    update(g_ref, cl_ref, b_ref, gn_ref, t_s)
    v, t_top, fine = factors(t_s[...])
    vs[...] = v
    ns, nt = k_ref.shape

    def block(rb, _):
        at = pl.ds(pl.multiple_of(rb * rows, rows), rows)
        total = jnp.zeros((rows, LANES), F32)
        for c in range(nt // LANES):
            total += k_ref[at, c * LANES : (c + 1) * LANES] * vs[c : c + 1, :]
        acc[at, :] = total
        return 0

    lax.fori_loop(0, ns // rows, block, 0)
    lane_sums(acc, row_ref)
    fine = finish(row_ref, t_top, fine)

    @pl.when(jnp.logical_not(fine))
    def _():
        fetch(((x_hbm, x_ref), (y_hbm, y_ref)), sem)
        rows_sweep(x_ref, y_ref, t_s, row_ref, None)


def weight_rows(out, lse):
    d = out.shape[0] - 8
    for b in range(lse.shape[0]):
        out[d : d + 8, b * LANES : (b + 1) * LANES] = jnp.broadcast_to(lse[b : b + 1, :], (8, LANES))


def parts_of(k):
    k1 = k.astype(BF16)
    return k1, (k - k1.astype(F32)).astype(BF16)


def cols_map_kernel(k_ref, x_ref, y_ref, f_ref, rl_ref, a_ref, fn_ref, out_ref, lse, ub, xu, cacc, r_s, *, rows):
    d = x_ref.shape[0]
    ns, nt = k_ref.shape
    update(f_ref, rl_ref, a_ref, fn_ref, r_s)
    u, r_top, fine = factors(r_s[...])
    sub = lax.broadcasted_iota(jnp.int32, (16, LANES), 0)
    for b in range(ns // LANES):
        at = slice(b * LANES, (b + 1) * LANES)
        ur = u[b : b + 1, :]
        p1, p2 = split2(x_ref[:, at] * ur)
        xu[0:d, at] = p1.astype(BF16)
        xu[d : 2 * d, at] = p2.astype(BF16)
        p1, p2 = split2(jnp.broadcast_to(ur, (16, LANES)))
        xu[2 * d : 2 * d + 16, at] = jnp.where(sub == 0, p1, jnp.where(sub == 1, p2, 0.0)).astype(BF16)
    wide = 2 * LANES

    def block(cb, _):
        at = pl.multiple_of(cb * wide, wide)
        total = jnp.zeros((xu.shape[0], wide), F32)
        for r in range(0, ns, rows):
            xr = xu[:, r : r + rows]
            total += jnp.dot(
                jnp.concatenate([xr, xr], axis=1),
                jnp.concatenate(parts_of(k_ref[r : r + rows, pl.ds(at, wide)]), axis=0),
                preferred_element_type=F32,
            )
        cacc[:, pl.ds(at, wide)] = total
        return 0

    lax.fori_loop(0, nt // wide, block, 0)
    for b in range(nt // LANES):
        at = slice(b * LANES, (b + 1) * LANES)
        den = cacc[2 * d : 2 * d + 1, at] + cacc[2 * d + 1 : 2 * d + 2, at]
        out_ref[0:d, at] = (cacc[0:d, at] + cacc[d : 2 * d, at]) / den
        lse[b : b + 1, :] = den
    fine = finish(lse, r_top, fine)

    @pl.when(jnp.logical_not(fine))
    def _():
        cols_sweep(x_ref, y_ref, r_s, lse, out_ref, ub)

    weight_rows(out_ref, lse)


def rows_map_kernel(k_ref, x_ref, y_ref, g_ref, cl_ref, b_ref, gn_ref, out_ref, lse, wy, acc, t_s, *, rows):
    d = x_ref.shape[0]
    ns, nt = k_ref.shape
    update(g_ref, cl_ref, b_ref, gn_ref, t_s)
    v, t_top, fine = factors(t_s[...])
    lane = lax.broadcasted_iota(jnp.int32, (LANES, 2 * d), 1)
    for b in range(nt // LANES):
        at = slice(b * LANES, (b + 1) * LANES)
        vr = v[b : b + 1, :]
        yb = y_ref[:, at] * vr
        p1, p2 = split2(jnp.concatenate([yb, yb], axis=0).T)
        wy[at, 0 : 2 * d] = jnp.where(lane < d, p1, p2).astype(BF16)
        p1, p2 = split2(jnp.broadcast_to(vr, (2 * d, LANES)).T)
        wy[at, 2 * d : 4 * d] = jnp.where(lane == 0, p1, jnp.where(lane == 1, p2, 0.0)).astype(BF16)
    wide = 2 * LANES
    acc[...] = jnp.zeros_like(acc)

    def block(cb, _):
        at = pl.multiple_of(cb * wide, wide)
        w = wy[pl.ds(at, wide), :]
        ww = jnp.concatenate([w, w], axis=0)
        for r in range(0, ns, rows):
            k = jnp.concatenate(parts_of(k_ref[r : r + rows, pl.ds(at, wide)]), axis=1)
            acc[r : r + rows, :] += jnp.dot(k, ww, preferred_element_type=F32)
        return 0

    lax.fori_loop(0, nt // wide, block, 0)
    for b in range(ns // LANES):
        at = slice(b * LANES, (b + 1) * LANES)
        num = acc[at, 0 : 2 * d].T
        den = acc[at, 2 * d : 4 * d].T
        den = den[0:1, :] + den[1:2, :]
        out_ref[0:d, at] = (num[0:d, :] + num[d : 2 * d, :]) / den
        lse[b : b + 1, :] = den
    fine = finish(lse, t_top, fine)

    @pl.when(jnp.logical_not(fine))
    def _():
        rows_sweep(x_ref, y_ref, t_s, lse, out_ref)

    weight_rows(out_ref, lse)


def merge_kernel(at_ref, whole, *refs, place):
    *others, out = refs
    width = out.shape[1]
    d = whole.shape[0] - 8
    for b in range(width // LANES):
        cols = slice(b * LANES, (b + 1) * LANES)
        at = pl.ds(pl.multiple_of(at_ref[place] + b * LANES, LANES), LANES)
        logs = [whole[d : d + 1, at]] + [other[d : d + 1, cols] for other in others]
        peak = functools.reduce(jnp.maximum, logs)
        weights = [jnp.exp(log - peak) for log in logs]
        total = functools.reduce(jnp.add, weights)
        values = whole[0:d, at] * (weights[0] / total)
        for other, weight in zip(others, weights[1:]):
            values += other[0:d, cols] * (weight / total)
        out[0:d, cols] = values
        if out.shape[0] > d:
            out[d:, cols] = jnp.broadcast_to(peak + jnp.log(total), (8, LANES))


def join_kernel(at_ref, ours, theirs, *refs):
    *pieces, col_out, row_out, sem = refs
    d = col_out.shape[0]
    count = ours.shape[0] // d
    copies = []

    def lay(src, out, place):
        at = pl.multiple_of(at_ref[3 + place], LANES)
        dst = out.at[:, pl.ds(at, src.shape[1])]
        copies.append(pltpu.make_async_copy(src, dst, sem.at[len(copies)]))
        copies[-1].start()

    for which, stack in enumerate((ours, theirs)):
        for k in range(count):
            lay(stack.at[k * d : (k + 1) * d, :], col_out, which * count + k)
    for k, piece_ref in enumerate(pieces):
        lay(piece_ref, row_out, 2 * count + k)
    for copy in copies:
        copy.wait()


VM = pl.BlockSpec(memory_space=pltpu.VMEM)
ANY = pl.BlockSpec(memory_space=pl.ANY)
PARAMS = pltpu.CompilerParams(vmem_limit_bytes=24 * 2**20)


def cost(flops, size):
    return pl.CostEstimate(flops=flops, bytes_accessed=size, transcendentals=0)


def vector(n):
    return jax.ShapeDtypeStruct((n // LANES, LANES), F32)


def scratch(n):
    return pltpu.VMEM((n // LANES, LANES), F32)


def form(x, y, a, b):
    d, ns = x.shape
    nt = y.shape[1]
    return pl.pallas_call(
        functools.partial(form_kernel, rows=256),
        out_shape=(pltpu.VMEM((ns, nt), F32), vector(ns), vector(nt)),
        in_specs=[ANY] * 4,
        out_specs=(VM,) * 3,
        scratch_shapes=[
            pltpu.VMEM((d, ns), F32),
            pltpu.VMEM((d, nt), F32),
            pltpu.VMEM((ns, 8 * d), BF16),
            pltpu.VMEM((8 * d, nt), BF16),
            pltpu.VMEM((ns, LANES), F32),
            pltpu.VMEM((ns, LANES), F32),
            scratch(ns),
            scratch(nt),
            pltpu.SemaphoreType.DMA((4,)),
        ],
        compiler_params=PARAMS,
        cost_estimate=cost(20 * d * ns * nt, 4 * ns * nt),
        name="form",
    )(x, y, a, b)


def sweep_scratch(d, ns, nt):
    return [pltpu.VMEM((d, ns), F32), pltpu.VMEM((d, nt), F32), pltpu.SemaphoreType.DMA((2,))]


def cols_sums(k, x, y, f, row_lse, a):
    ns, nt = k.shape
    return pl.pallas_call(
        functools.partial(cols_kernel, rows=64),
        out_shape=(vector(ns), vector(nt)),
        in_specs=[VM, ANY, ANY, VM, VM, VM],
        out_specs=(VM,) * 2,
        scratch_shapes=[pltpu.VMEM((ns, LANES), F32), scratch(ns)] + sweep_scratch(x.shape[0], ns, nt),
        compiler_params=PARAMS,
        cost_estimate=cost(2 * ns * nt, 2 * ns * nt),
        name="cols_sums",
    )(k, x, y, f, row_lse, a)


def rows_sums(k, x, y, g, col_lse, b):
    ns, nt = k.shape
    return pl.pallas_call(
        functools.partial(rows_kernel, rows=64),
        out_shape=(vector(nt), vector(ns)),
        in_specs=[VM, ANY, ANY, VM, VM, VM],
        out_specs=(VM,) * 2,
        scratch_shapes=[pltpu.VMEM((ns, LANES), F32), scratch(nt), scratch(nt)]
        + sweep_scratch(x.shape[0], ns, nt),
        compiler_params=PARAMS,
        cost_estimate=cost(2 * ns * nt, 2 * ns * nt),
        name="rows_sums",
    )(k, x, y, g, col_lse, b)


def cols_map(k, x, y, f, row_lse, a):
    d = x.shape[0]
    ns, nt = k.shape
    return pl.pallas_call(
        functools.partial(cols_map_kernel, rows=512),
        out_shape=(vector(ns), jax.ShapeDtypeStruct((d + 8, nt), F32)),
        in_specs=[VM] * 6,
        out_specs=(VM,) * 2,
        scratch_shapes=[
            scratch(nt),
            pltpu.VMEM((ns, LANES), F32),
            pltpu.VMEM((2 * d + 16, ns), BF16),
            pltpu.VMEM((2 * d + 16, nt), F32),
            scratch(ns),
        ],
        compiler_params=PARAMS,
        cost_estimate=cost(16 * d * ns * nt, 4 * ns * nt),
        name="cols_map",
    )(k, x, y, f, row_lse, a)


def rows_map(k, x, y, g, col_lse, b):
    d = x.shape[0]
    ns, nt = k.shape
    return pl.pallas_call(
        functools.partial(rows_map_kernel, rows=512),
        out_shape=(vector(nt), jax.ShapeDtypeStruct((d + 8, ns), F32)),
        in_specs=[VM] * 6,
        out_specs=(VM,) * 2,
        scratch_shapes=[
            scratch(ns),
            pltpu.VMEM((nt, 4 * d), BF16),
            pltpu.VMEM((ns, 4 * d), F32),
            scratch(nt),
        ],
        compiler_params=PARAMS,
        cost_estimate=cost(16 * d * ns * nt, 4 * ns * nt),
        name="rows_map",
    )(k, x, y, g, col_lse, b)


def merge(at, place, whole, others, keep):
    rows, width = others[0].shape
    return pl.pallas_call(
        functools.partial(merge_kernel, place=place),
        out_shape=jax.ShapeDtypeStruct((rows if keep else rows - 8, width), F32),
        in_specs=[pl.BlockSpec(memory_space=pltpu.SMEM)] + [VM] * (1 + len(others)),
        out_specs=VM,
        compiler_params=PARAMS,
        name="merge",
    )(at, whole, *others)


def join(at, ours, theirs, pieces):
    d, width = pieces[0].shape
    nt = 2 * ours.shape[0] // d * ours.shape[1]
    ns = width * len(pieces)
    return pl.pallas_call(
        join_kernel,
        out_shape=(jax.ShapeDtypeStruct((d, nt), F32), jax.ShapeDtypeStruct((d, ns), F32)),
        in_specs=[pl.BlockSpec(memory_space=pltpu.SMEM)] + [VM] * (2 + len(pieces)),
        out_specs=(ANY,) * 2,
        scratch_shapes=[pltpu.SemaphoreType.DMA((at.shape[0] - 3,))],
        compiler_params=PARAMS,
        name="join",
    )(at, ours, theirs, *pieces)


def merged(first, second):
    peak = jnp.maximum(first, second)
    return peak + jnp.log(jnp.exp(first - peak) + jnp.exp(second - peak))


def lse_over(axis, part):
    n = lax.axis_size(axis)
    step = n // 2
    while step:
        part = merged(part, lax.ppermute(part, axis, [(i, i ^ step) for i in range(n)]))
        step //= 2
    return part


def pairs(n, group, stride, k):
    return [(i, i + (((i // stride) + k) % group - (i // stride) % group) * stride) for i in range(n)]


def places(index, group, stride, width):
    own = (index // stride) % group
    return [(own + k) % group * width for k in range(group)]


def piece(a, at, count):
    zero = jnp.zeros((), at.dtype)
    return lax.dynamic_slice(
        a, (zero, at), (a.shape[0], a.shape[1] // count), allow_negative_indices=False
    )


def merged_piece(axis, place, stride, part, at, own):
    n, group = lax.axis_size(axis), len(place)
    got = [
        lax.ppermute(piece(part, place[k], group), axis, pairs(n, group, stride, k))
        for k in range(1, group)
    ]
    return merge(at, own, part, got, False)


def all_pieces(axis, group, stride, own):
    n = lax.axis_size(axis)
    return [own] + [lax.ppermute(own, axis, pairs(n, group, stride, k)) for k in range(1, group)]


def body(sources, targets, source_mass, target_mass):
    rows, cols = lax.axis_size("row"), lax.axis_size("col")
    ns, nt = sources.shape[1], targets.shape[1]
    index = lax.axis_index("row")
    halves = places(index, 2, 1, nt // 2)
    row_places = places(index, rows // 2, 2, nt // rows)
    col_places = places(lax.axis_index("col"), cols, 1, ns // cols)
    laid = [half + row_places[-k] for half in halves for k in range(rows // 2)]
    laid = [halves[0], row_places[0], col_places[0]] + laid + [col_places[-k] for k in range(cols)]
    laid = jnp.stack(laid)
    sources, halves, row_places, col_places, laid = lax.optimization_barrier(
        (sources, halves, row_places, col_places, laid)
    )
    x, y = sources, targets
    a = source_mass.reshape(-1, LANES)
    b = target_mass.reshape(-1, LANES)
    f = jnp.zeros_like(a)
    g = jnp.zeros_like(b)
    k, row_part, col_part = form(x, y, a, b)
    for sweep in range(ITERS):
        row_lse = lse_over("col", row_part)
        col_lse = lse_over("row", col_part)
        last = sweep == ITERS - 1
        f, col_part = (cols_map if last else cols_sums)(k, x, y, f, row_lse, a)
        g, row_part = (rows_map if last else rows_sums)(k, x, y, g, col_lse, b)
    pair = pairs(rows, 2, 1, 1)
    other = lax.ppermute(piece(col_part, halves[1], 2), "row", pair)
    chip = merge(laid, 0, col_part, [other], True)
    ours = merged_piece("row", row_places, 2, chip, laid, 1)
    ours = jnp.concatenate(all_pieces("row", rows // 2, 2, ours), axis=0)
    theirs = lax.ppermute(ours, "row", pair)
    own = merged_piece("col", col_places, 1, row_part, laid, 2)
    source_pieces = all_pieces("col", cols, 1, own)
    target_map, source_map = join(laid, ours, theirs, source_pieces)
    return f.reshape(-1), g.reshape(-1), source_map, target_map


def solution(mesh):
    in_specs = (P(None, "row"), P(None, "col"), P("row"), P("col"))
    out_specs = (P("row"), P("col"), P(None, "row"), P(None, "col"))
    return jax.shard_map(body, mesh=mesh, in_specs=in_specs, out_specs=out_specs, check_vma=False)
```

```python
import functools

import jax
import jax.numpy as jnp
from jax import lax
from jax.experimental import pallas as pl
from jax.experimental.pallas import tpu as pltpu
from jax.sharding import PartitionSpec as P

ITERS = 3
EPS = 0.25
LOG2E = 1.4426950408889634
LN2 = 0.6931471805599453
SHIFT = 85.0
SMALLEST = 2.0**-85
FACTOR_RANGE = 60.0 * LN2
LANES = 128
F32 = jnp.float32
BF16 = jnp.bfloat16
HIGH = lax.Precision.HIGHEST


def split2(a):
    a1 = a.astype(BF16).astype(F32)
    return a1, a - a1


def split3(a):
    a1, rest = split2(a)
    a2, rest = split2(rest)
    return a1, a2, rest


def spread(u, ub):
    for b in range(u.shape[0]):
        ub[b * LANES : (b + 1) * LANES, :] = jnp.broadcast_to(u[b : b + 1, :], (LANES, LANES)).T


def lane_sums(acc, out):
    for b in range(out.shape[0]):
        out[b : b + 1, :] = jnp.sum(acc[b * LANES : (b + 1) * LANES, :].T, axis=0, keepdims=True)


def fold(a):
    return jnp.sum(a.reshape(a.shape[0] // 8, 8, a.shape[1]), axis=0)


def build_operands(x_ref, y_ref, xa, ya):
    d, ns = x_ref.shape
    nt = y_ref.shape[1]
    wide = 2 * LANES
    sub = lax.broadcasted_iota(jnp.int32, (16, wide), 0)
    lane = lax.broadcasted_iota(jnp.int32, (LANES, 2 * d), 1)

    def tail(row, parts):
        out = jnp.zeros(row.shape, F32)
        for at, part in enumerate(parts):
            out = jnp.where(row == at, part, out)
        return out

    def target_block(b, _):
        cols = pl.ds(pl.multiple_of(b * wide, wide), wide)
        y = y_ref[:, cols]
        norm = split3(SHIFT - jnp.sum(y * y, axis=0, keepdims=True) * (LOG2E / EPS))
        y1, y2, y3 = (part.astype(BF16) for part in split3(y * (2.0 * LOG2E / EPS)))
        for at, part in enumerate((y1, y2, y1, y2, y3, y1)):
            ya[at * d : (at + 1) * d, cols] = part
        ya[6 * d : 6 * d + 16, cols] = tail(sub, norm + (1.0, 1.0, 1.0)).astype(BF16)
        ya[6 * d + 16 : 8 * d, cols] = jnp.zeros((2 * d - 16, wide), BF16)
        return 0

    lax.fori_loop(0, nt // wide, target_block, 0, unroll=4)

    def source_block(b, _):
        rows = pl.ds(pl.multiple_of(b * LANES, LANES), LANES)
        x = x_ref[:, rows]
        norm = split3(jnp.sum(x * x, axis=0, keepdims=True) * (-LOG2E / EPS))
        x1, x2, x3 = split3(jnp.concatenate([x, x], axis=0).T)
        xa[rows, 0 : 2 * d] = x1.astype(BF16)
        xa[rows, 2 * d : 4 * d] = x2.astype(BF16)
        xa[rows, 4 * d : 6 * d] = jnp.where(lane < d, x1, x3).astype(BF16)
        last = tail(sub[:8, :LANES], (1.0, 1.0, 1.0) + norm)
        last = jnp.concatenate([last, jnp.zeros((2 * d - 8, LANES), F32)], axis=0)
        xa[rows, 6 * d : 8 * d] = last.T.astype(BF16)
        return 0

    lax.fori_loop(0, ns // LANES, source_block, 0, unroll=4)


def as_row(ref):
    return jnp.concatenate([ref[b : b + 1, :] for b in range(ref.shape[0])], axis=1)


def put_row(row, ref):
    for b in range(ref.shape[0]):
        ref[b : b + 1, :] = row[:, b * LANES : (b + 1) * LANES]


def rows_sweep(x_ref, y_ref, t_ref, lse, out):
    d, ns = x_ref.shape
    y = y_ref[...]
    yn = jnp.sum(y * y, axis=0, keepdims=True)
    t = as_row(t_ref)

    def block(b, _):
        at = pl.multiple_of(b * LANES, LANES)
        xt = jnp.concatenate([x_ref[:, pl.ds(at, LANES)]] * 2, axis=0).T[:, 0:d]
        xn = jnp.sum(xt * xt, axis=1, keepdims=True)
        cross = jnp.dot(xt, y, precision=HIGH, preferred_element_type=F32)
        scores = (2.0 * cross - xn - yn) / EPS + t
        peak = jnp.max(scores, axis=1, keepdims=True)
        weights = jnp.exp(scores - peak)
        total = jnp.sum(weights, axis=1, keepdims=True)
        lse[pl.ds(b, 1), :] = jnp.broadcast_to(peak + jnp.log(total), (LANES, LANES)).T[0:1, :]
        if out is not None:
            vector = lax.dot_general(
                weights / total, y, (((1,), (1,)), ((), ())), precision=HIGH, preferred_element_type=F32
            )
            out[0:d, pl.ds(at, LANES)] = jnp.concatenate([vector, vector], axis=1).T[0:d, :]
        return 0

    lax.fori_loop(0, ns // LANES, block, 0)


def cols_sweep(x_ref, y_ref, r_ref, lse, out, ub):
    d, ns = x_ref.shape
    nt = y_ref.shape[1]
    spread(r_ref[...], ub)
    y = y_ref[...]
    yn = jnp.sum(y * y, axis=0, keepdims=True)

    def block(b, carry):
        at = pl.multiple_of(b * LANES, LANES)
        xb = x_ref[:, pl.ds(at, LANES)]
        xt = jnp.concatenate([xb, xb], axis=0).T[:, 0:d]
        xn = jnp.sum(xt * xt, axis=1, keepdims=True)
        cross = jnp.dot(xt, y, precision=HIGH, preferred_element_type=F32)
        scores = (2.0 * cross - xn - yn) / EPS + ub[pl.ds(at, LANES), 0:1]
        peak = jnp.maximum(carry[0], jnp.max(scores, axis=0, keepdims=True))
        decay = jnp.exp(carry[0] - peak)
        weights = jnp.exp(scores - peak)
        total = carry[1] * decay + jnp.sum(weights, axis=0, keepdims=True)
        if out is not None:
            out[0:d, :] = out[0:d, :] * decay + jnp.dot(
                xb, weights, precision=HIGH, preferred_element_type=F32
            )
        return peak, total

    if out is not None:
        out[0:d, :] = jnp.zeros((d, nt), F32)
    start = (jnp.full((1, nt), -1e30, F32), jnp.zeros((1, nt), F32))
    peak, total = lax.fori_loop(0, ns // LANES, block, start)
    put_row(peak + jnp.log(total), lse)
    if out is not None:
        out[0:d, :] = out[0:d, :] / total


def factors(term):
    top = jnp.max(term)
    return jnp.exp(term - top), top, top - jnp.min(term) <= FACTOR_RANGE


def finish(ref, top, fine):
    values = ref[...]
    ref[...] = jnp.log(values) + (top - SHIFT * LN2)
    return fine & (jnp.min(values) >= SMALLEST)


def fetch(pairs, sem):
    copies = [pltpu.make_async_copy(src, dst, sem.at[i]) for i, (src, dst) in enumerate(pairs)]
    for copy in copies:
        copy.start()
    for copy in copies:
        copy.wait()


def form_kernel(
    x_hbm, y_hbm, a_hbm, b_hbm, k_ref, x_ref, y_ref, row_ref, col_ref, xa, ya, ub, acc, r_s, t_s, sem, *, rows
):
    ns, nt = x_ref.shape[1], y_ref.shape[1]
    fetch(((x_hbm, x_ref), (y_hbm, y_ref), (a_hbm, r_s), (b_hbm, t_s)), sem)
    r_s[...] = jnp.log(r_s[...])
    t_s[...] = jnp.log(t_s[...])
    u, r_top, u_fine = factors(r_s[...])
    v, t_top, v_fine = factors(t_s[...])
    build_operands(x_ref, y_ref, xa, ya)
    spread(u, ub)
    col_ref[...] = v
    acc[...] = jnp.zeros_like(acc)
    tiles = 4 if nt % (4 * LANES) == 0 else 1
    wide = tiles * LANES

    def block(cb, _):
        at = pl.multiple_of(cb * wide, wide)
        vs = [col_ref[pl.ds(cb * tiles + t, 1), :] for t in range(tiles)]
        cs = [jnp.zeros((8, LANES), F32)] * tiles
        for r in range(0, ns, rows):
            z = jnp.dot(xa[r : r + rows, :], ya[:, pl.ds(at, wide)], preferred_element_type=F32)
            k = jnp.exp2(z)
            k_ref[r : r + rows, pl.ds(at, wide)] = k
            ur = ub[r : r + rows, :]
            total = acc[r : r + rows, :]
            for t in range(tiles):
                kt = k[:, t * LANES : (t + 1) * LANES]
                total += kt * vs[t]
                cs[t] += fold(kt * ur)
            acc[r : r + rows, :] = total
        for t in range(tiles):
            col_ref[pl.ds(cb * tiles + t, 1), :] = jnp.sum(cs[t], axis=0, keepdims=True)
        return 0

    lax.fori_loop(0, nt // wide, block, 0)
    lane_sums(acc, row_ref)
    rows_fine = finish(row_ref, t_top, v_fine)
    cols_fine = finish(col_ref, r_top, u_fine)

    @pl.when(jnp.logical_not(rows_fine))
    def _():
        rows_sweep(x_ref, y_ref, t_s, row_ref, None)

    @pl.when(jnp.logical_not(cols_fine))
    def _():
        cols_sweep(x_ref, y_ref, r_s, col_ref, None, ub)


def update(pot_ref, lse_ref, mass_ref, new_ref, term):
    new_ref[...] = 0.5 * (pot_ref[...] - EPS * lse_ref[...])
    term[...] = new_ref[...] / EPS + jnp.log(mass_ref[...])


def sums_kernel(
    k_ref, x_ref, y_ref, f_ref, g_ref, rl_ref, cl_ref, a_ref, b_ref,
    fn_ref, gn_ref, row_ref, col_ref, vs, r_s, t_s, ub,
):
    update(f_ref, rl_ref, a_ref, fn_ref, r_s)
    update(g_ref, cl_ref, b_ref, gn_ref, t_s)
    u, r_top, u_fine = factors(r_s[...])
    v, t_top, v_fine = factors(t_s[...])
    row_ref[...] = u
    vs[...] = v
    ns, nt = k_ref.shape
    tiles = nt // LANES

    def block(rb, cs):
        at = pl.ds(pl.multiple_of(rb * LANES, LANES), LANES)
        ur = jnp.broadcast_to(row_ref[pl.ds(rb, 1), :], (LANES, LANES)).T
        total = jnp.zeros((LANES, LANES), F32)
        out = []
        for c in range(tiles):
            k = k_ref[at, c * LANES : (c + 1) * LANES]
            total += k * vs[c : c + 1, :]
            out.append(cs[c] + fold(k * ur))
        row_ref[pl.ds(rb, 1), :] = jnp.sum(total.T, axis=0, keepdims=True)
        return tuple(out)

    cs = lax.fori_loop(0, ns // LANES, block, (jnp.zeros((8, LANES), F32),) * tiles, unroll=2)
    for c in range(tiles):
        col_ref[c : c + 1, :] = jnp.sum(cs[c], axis=0, keepdims=True)
    rows_fine = finish(row_ref, t_top, v_fine)
    cols_fine = finish(col_ref, r_top, u_fine)

    @pl.when(jnp.logical_not(rows_fine & cols_fine))
    def _():
        rows_sweep(x_ref, y_ref, t_s, row_ref, None)
        cols_sweep(x_ref, y_ref, r_s, col_ref, None, ub)


def weight_rows(out, lse):
    d = out.shape[0] - 8
    for b in range(lse.shape[0]):
        out[d : d + 8, b * LANES : (b + 1) * LANES] = jnp.broadcast_to(lse[b : b + 1, :], (8, LANES))


def parts_of(k):
    k1 = k.astype(BF16)
    return k1, (k - k1.astype(F32)).astype(BF16)


def maps_kernel(
    k_ref, x_ref, y_ref, f_ref, g_ref, rl_ref, cl_ref, a_ref, b_ref,
    fn_ref, gn_ref, rowm_ref, colm_ref, row_s, col_s, ub, wy, xu, acc, cacc, r_s, t_s, *, rows,
):
    d = x_ref.shape[0]
    ns, nt = k_ref.shape
    update(f_ref, rl_ref, a_ref, fn_ref, r_s)
    update(g_ref, cl_ref, b_ref, gn_ref, t_s)
    u, r_top, u_fine = factors(r_s[...])
    v, t_top, v_fine = factors(t_s[...])
    lane = lax.broadcasted_iota(jnp.int32, (LANES, 2 * d), 1)
    sub = lax.broadcasted_iota(jnp.int32, (16, LANES), 0)
    for b in range(nt // LANES):
        at = slice(b * LANES, (b + 1) * LANES)
        vb = v[b : b + 1, :]
        yb = y_ref[:, at] * vb
        p1, p2 = split2(jnp.concatenate([yb, yb], axis=0).T)
        wy[at, 0 : 2 * d] = jnp.where(lane < d, p1, p2).astype(BF16)
        p1, p2 = split2(jnp.broadcast_to(vb, (2 * d, LANES)).T)
        wy[at, 2 * d : 4 * d] = jnp.where(lane == 0, p1, jnp.where(lane == 1, p2, 0.0)).astype(BF16)
    for b in range(ns // LANES):
        at = slice(b * LANES, (b + 1) * LANES)
        uv = u[b : b + 1, :]
        p1, p2 = split2(x_ref[:, at] * uv)
        xu[0:d, at] = p1.astype(BF16)
        xu[d : 2 * d, at] = p2.astype(BF16)
        p1, p2 = split2(jnp.broadcast_to(uv, (16, LANES)))
        xu[2 * d : 2 * d + 16, at] = jnp.where(sub == 0, p1, jnp.where(sub == 1, p2, 0.0)).astype(BF16)
    wide = 2 * LANES
    acc[...] = jnp.zeros_like(acc)

    def block(cb, _):
        at = pl.multiple_of(cb * wide, wide)
        w = wy[pl.ds(at, wide), :]
        ww = jnp.concatenate([w, w], axis=0)
        total = jnp.zeros((xu.shape[0], wide), F32)
        for r in range(0, ns, rows):
            k = k_ref[r : r + rows, pl.ds(at, wide)]
            k1 = k.astype(BF16)
            k2 = (k - k1.astype(F32)).astype(BF16)
            acc[r : r + rows, :] += jnp.dot(
                jnp.concatenate([k1, k2], axis=1), ww, preferred_element_type=F32
            )
            xr = xu[:, r : r + rows]
            total += jnp.dot(
                jnp.concatenate([xr, xr], axis=1),
                jnp.concatenate([k1, k2], axis=0),
                preferred_element_type=F32,
            )
        cacc[:, pl.ds(at, wide)] = total
        return 0

    lax.fori_loop(0, nt // wide, block, 0)
    for b in range(ns // LANES):
        at = slice(b * LANES, (b + 1) * LANES)
        num = acc[at, 0 : 2 * d].T
        den = acc[at, 2 * d : 4 * d].T
        den = den[0:1, :] + den[1:2, :]
        rowm_ref[0:d, at] = (num[0:d, :] + num[d : 2 * d, :]) / den
        row_s[b : b + 1, :] = den
    for b in range(nt // LANES):
        at = slice(b * LANES, (b + 1) * LANES)
        den = cacc[2 * d : 2 * d + 1, at] + cacc[2 * d + 1 : 2 * d + 2, at]
        colm_ref[0:d, at] = (cacc[0:d, at] + cacc[d : 2 * d, at]) / den
        col_s[b : b + 1, :] = den
    rows_fine = finish(row_s, t_top, v_fine)
    cols_fine = finish(col_s, r_top, u_fine)

    @pl.when(jnp.logical_not(rows_fine & cols_fine))
    def _():
        rows_sweep(x_ref, y_ref, t_s, row_s, rowm_ref)
        cols_sweep(x_ref, y_ref, r_s, col_s, colm_ref, ub)

    weight_rows(rowm_ref, row_s)
    weight_rows(colm_ref, col_s)


def merge_kernel(at_ref, whole, *refs, place):
    *others, out = refs
    width = out.shape[1]
    d = whole.shape[0] - 8
    for b in range(width // LANES):
        cols = slice(b * LANES, (b + 1) * LANES)
        at = pl.ds(pl.multiple_of(at_ref[place] + b * LANES, LANES), LANES)
        logs = [whole[d : d + 1, at]] + [other[d : d + 1, cols] for other in others]
        peak = functools.reduce(jnp.maximum, logs)
        weights = [jnp.exp(log - peak) for log in logs]
        total = functools.reduce(jnp.add, weights)
        values = whole[0:d, at] * (weights[0] / total)
        for other, weight in zip(others, weights[1:]):
            values += other[0:d, cols] * (weight / total)
        out[0:d, cols] = values
        if out.shape[0] > d:
            out[d:, cols] = jnp.broadcast_to(peak + jnp.log(total), (8, LANES))


def join_kernel(at_ref, ours, theirs, *refs):
    *pieces, col_out, row_out, sem = refs
    d = col_out.shape[0]
    count = ours.shape[0] // d
    copies = []

    def lay(src, out, place):
        at = pl.multiple_of(at_ref[3 + place], LANES)
        dst = out.at[:, pl.ds(at, src.shape[1])]
        copies.append(pltpu.make_async_copy(src, dst, sem.at[len(copies)]))
        copies[-1].start()

    for which, stack in enumerate((ours, theirs)):
        for k in range(count):
            lay(stack.at[k * d : (k + 1) * d, :], col_out, which * count + k)
    for k, piece_ref in enumerate(pieces):
        lay(piece_ref, row_out, 2 * count + k)
    for copy in copies:
        copy.wait()


VM = pl.BlockSpec(memory_space=pltpu.VMEM)
ANY = pl.BlockSpec(memory_space=pltpu.HBM)
PARAMS = pltpu.CompilerParams(vmem_limit_bytes=24 * 2**20)
FULL = pltpu.CompilerParams(vmem_limit_bytes=46 * 2**20 + 3 * 2**18)


def cost(flops, size):
    return pl.CostEstimate(flops=flops, bytes_accessed=size, transcendentals=0)


def vector(n):
    return jax.ShapeDtypeStruct((n // LANES, LANES), F32)


def near(n):
    return pltpu.VMEM((n // LANES, LANES), F32)


def scratch(n):
    return pltpu.VMEM((n // LANES, LANES), F32)


def form(x, y, a, b):
    d, ns = x.shape
    nt = y.shape[1]
    return pl.pallas_call(
        functools.partial(form_kernel, rows=256),
        out_shape=(
            pltpu.VMEM((ns, nt), F32),
            pltpu.VMEM((d, ns), F32),
            pltpu.VMEM((d, nt), F32),
            near(ns),
            near(nt),
        ),
        in_specs=[ANY] * 4,
        out_specs=(VM,) * 5,
        scratch_shapes=[
            pltpu.VMEM((ns, 8 * d), BF16),
            pltpu.VMEM((8 * d, nt), BF16),
            pltpu.VMEM((ns, LANES), F32),
            pltpu.VMEM((ns, LANES), F32),
            scratch(ns),
            scratch(nt),
            pltpu.SemaphoreType.DMA((4,)),
        ],
        compiler_params=FULL,
        cost_estimate=cost(20 * d * ns * nt, 4 * ns * nt),
        name="form",
    )(x, y, a, b)


def sums(k, x, y, *vectors):
    ns, nt = k.shape
    return pl.pallas_call(
        sums_kernel,
        out_shape=(near(ns), near(nt), near(ns), near(nt)),
        in_specs=[VM] * 9,
        out_specs=(VM,) * 4,
        scratch_shapes=[scratch(nt), scratch(ns), scratch(nt), pltpu.VMEM((ns, LANES), F32)],
        compiler_params=PARAMS,
        cost_estimate=cost(4 * ns * nt, 4 * ns * nt),
        name="sums",
    )(k, x, y, *vectors)


def maps(k, x, y, *vectors):
    d = x.shape[0]
    ns, nt = k.shape
    return pl.pallas_call(
        functools.partial(maps_kernel, rows=512),
        out_shape=(
            vector(ns),
            vector(nt),
            jax.ShapeDtypeStruct((d + 8, ns), F32),
            jax.ShapeDtypeStruct((d + 8, nt), F32),
        ),
        in_specs=[VM] * 9,
        out_specs=(VM,) * 4,
        scratch_shapes=[
            scratch(ns),
            scratch(nt),
            pltpu.VMEM((ns, LANES), F32),
            pltpu.VMEM((nt, 4 * d), BF16),
            pltpu.VMEM((2 * d + 16, ns), BF16),
            pltpu.VMEM((ns, 4 * d), F32),
            pltpu.VMEM((2 * d + 16, nt), F32),
            scratch(ns),
            scratch(nt),
        ],
        compiler_params=PARAMS,
        cost_estimate=cost(32 * d * ns * nt, 4 * ns * nt),
        name="maps",
    )(k, x, y, *vectors)


def merge(at, place, whole, others, keep):
    rows, width = others[0].shape
    return pl.pallas_call(
        functools.partial(merge_kernel, place=place),
        out_shape=jax.ShapeDtypeStruct((rows if keep else rows - 8, width), F32),
        in_specs=[pl.BlockSpec(memory_space=pltpu.SMEM)] + [VM] * (1 + len(others)),
        out_specs=VM,
        compiler_params=PARAMS,
        name="merge",
    )(at, whole, *others)


def join(at, ours, theirs, pieces):
    d, width = pieces[0].shape
    nt = 2 * ours.shape[0] // d * ours.shape[1]
    ns = width * len(pieces)
    return pl.pallas_call(
        join_kernel,
        out_shape=(jax.ShapeDtypeStruct((d, nt), F32), jax.ShapeDtypeStruct((d, ns), F32)),
        in_specs=[pl.BlockSpec(memory_space=pltpu.SMEM)] + [VM] * (2 + len(pieces)),
        out_specs=(ANY,) * 2,
        scratch_shapes=[pltpu.SemaphoreType.DMA((at.shape[0] - 3,))],
        compiler_params=PARAMS,
        name="join",
    )(at, ours, theirs, *pieces)


def merged(first, second):
    peak = jnp.maximum(first, second)
    return peak + jnp.log(jnp.exp(first - peak) + jnp.exp(second - peak))


def lse_over(axis, part):
    n = lax.axis_size(axis)
    step = n // 2
    while step:
        part = merged(part, lax.ppermute(part, axis, [(i, i ^ step) for i in range(n)]))
        step //= 2
    return part


def partner(place, k, group):
    return place ^ k if group & (group - 1) == 0 else (place + k) % group


def source(place, k, group):
    return place ^ k if group & (group - 1) == 0 else (place - k) % group


def pairs(n, group, stride, k):
    out = []
    for i in range(n):
        place = (i // stride) % group
        out.append((i, i + (partner(place, k, group) - place) * stride))
    return out


def places(index, group, stride, width):
    own = (index // stride) % group
    return (
        [partner(own, k, group) * width for k in range(group)],
        [source(own, k, group) * width for k in range(group)],
    )


def piece(a, at, count):
    zero = jnp.zeros((), at.dtype)
    return lax.dynamic_slice(
        a, (zero, at), (a.shape[0], a.shape[1] // count), allow_negative_indices=False
    )


def pieces_of(axis, place, stride, part):
    n, group = lax.axis_size(axis), len(place)
    return [
        lax.ppermute(piece(part, place[k], group), axis, pairs(n, group, stride, k))
        for k in range(1, group)
    ]


def all_pieces(axis, group, stride, own):
    n = lax.axis_size(axis)
    return [own] + [lax.ppermute(own, axis, pairs(n, group, stride, k)) for k in range(1, group)]


def body(sources, targets, source_mass, target_mass):
    rows, cols = lax.axis_size("row"), lax.axis_size("col")
    ns, nt = sources.shape[1], targets.shape[1]
    index = lax.axis_index("row")
    halves, _ = places(index, 2, 1, nt // 2)
    row_places, row_sources = places(index, rows // 2, 2, nt // rows)
    col_places, col_sources = places(lax.axis_index("col"), cols, 1, ns // cols)
    laid = [halves[0], row_places[0], col_places[0]]
    laid += [half + at for half in halves for at in row_sources] + col_sources
    laid = jnp.stack(laid)
    sources, halves, row_places, col_places, laid = lax.optimization_barrier(
        (sources, halves, row_places, col_places, laid)
    )
    a = source_mass.reshape(-1, LANES)
    b = target_mass.reshape(-1, LANES)
    f = jnp.zeros_like(a)
    g = jnp.zeros_like(b)
    k, x, y, row_part, col_part = form(sources, targets, a, b)
    for sweep in range(ITERS):
        row_lse = lse_over("col", row_part)
        col_lse = lse_over("row", col_part)
        if sweep < ITERS - 1:
            f, g, row_part, col_part = sums(k, x, y, f, g, row_lse, col_lse, a, b)
    f, g, row_part, col_part = maps(k, x, y, f, g, row_lse, col_lse, a, b)
    pair = pairs(rows, 2, 1, 1)
    other = lax.ppermute(piece(col_part, halves[1], 2), "row", pair)
    chip = merge(laid, 0, col_part, [other], True)
    chip, row_part = lax.optimization_barrier((chip, row_part))
    parted = (pieces_of("row", row_places, 2, chip), pieces_of("col", col_places, 1, row_part))
    column_pieces, row_pieces = lax.optimization_barrier(parted)
    ours = merge(laid, 1, chip, column_pieces, False)
    own = merge(laid, 2, row_part, row_pieces, False)
    ours, own = lax.optimization_barrier((ours, own))
    whole = (all_pieces("row", rows // 2, 2, ours), all_pieces("col", cols, 1, own))
    column_pieces, source_pieces = lax.optimization_barrier(whole)
    ours = jnp.concatenate(column_pieces, axis=0)
    theirs = lax.ppermute(ours, "row", pair)
    target_map, source_map = join(laid, ours, theirs, source_pieces)
    return f.reshape(-1), g.reshape(-1), source_map, target_map


def solution(mesh):
    in_specs = (P(None, "row"), P(None, "col"), P("row"), P("col"))
    out_specs = (P("row"), P("col"), P(None, "row"), P(None, "col"))
    return jax.shard_map(body, mesh=mesh, in_specs=in_specs, out_specs=out_specs, check_vma=False)
```

```python
import functools

import jax
import jax.numpy as jnp
from jax import lax
from jax.experimental import pallas as pl
from jax.experimental.pallas import tpu as pltpu
from jax.sharding import PartitionSpec as P

ITERS = 3
EPS = 0.25
LOG2E = 1.4426950408889634
LN2 = 0.6931471805599453
SHIFT = 85.0
SMALLEST = 2.0**-85
FACTOR_RANGE = 60.0 * LN2
LANES = 128
F32 = jnp.float32
BF16 = jnp.bfloat16
HIGH = lax.Precision.HIGHEST


def split2(a):
    a1 = a.astype(BF16).astype(F32)
    return a1, a - a1


def split3(a):
    a1, rest = split2(a)
    a2, rest = split2(rest)
    return a1, a2, rest


def spread(u, ub):
    for b in range(u.shape[0]):
        ub[b * LANES : (b + 1) * LANES, :] = jnp.broadcast_to(u[b : b + 1, :], (LANES, LANES)).T


def lane_sums(acc, out):
    for b in range(out.shape[0]):
        out[b : b + 1, :] = jnp.sum(acc[b * LANES : (b + 1) * LANES, :].T, axis=0, keepdims=True)


def fold(a):
    return jnp.sum(a.reshape(a.shape[0] // 8, 8, a.shape[1]), axis=0)


def build_operands(x_ref, y_ref, xa, ya):
    d, ns = x_ref.shape
    nt = y_ref.shape[1]
    wide = 2 * LANES
    sub = lax.broadcasted_iota(jnp.int32, (16, wide), 0)
    lane = lax.broadcasted_iota(jnp.int32, (LANES, 2 * d), 1)

    def tail(row, parts):
        out = jnp.zeros(row.shape, F32)
        for at, part in enumerate(parts):
            out = jnp.where(row == at, part, out)
        return out

    def target_block(b, _):
        cols = pl.ds(pl.multiple_of(b * wide, wide), wide)
        y = y_ref[:, cols]
        norm = split3(SHIFT - jnp.sum(y * y, axis=0, keepdims=True) * (LOG2E / EPS))
        y1, y2, y3 = (part.astype(BF16) for part in split3(y * (2.0 * LOG2E / EPS)))
        for at, part in enumerate((y1, y2, y1, y2, y3, y1)):
            ya[at * d : (at + 1) * d, cols] = part
        ya[6 * d : 6 * d + 16, cols] = tail(sub, norm + (1.0, 1.0, 1.0)).astype(BF16)
        ya[6 * d + 16 : 8 * d, cols] = jnp.zeros((2 * d - 16, wide), BF16)
        return 0

    lax.fori_loop(0, nt // wide, target_block, 0, unroll=4)

    def source_block(b, _):
        rows = pl.ds(pl.multiple_of(b * LANES, LANES), LANES)
        x = x_ref[:, rows]
        norm = split3(jnp.sum(x * x, axis=0, keepdims=True) * (-LOG2E / EPS))
        x1, x2, x3 = split3(jnp.concatenate([x, x], axis=0).T)
        xa[rows, 0 : 2 * d] = x1.astype(BF16)
        xa[rows, 2 * d : 4 * d] = x2.astype(BF16)
        xa[rows, 4 * d : 6 * d] = jnp.where(lane < d, x1, x3).astype(BF16)
        last = tail(sub[:8, :LANES], (1.0, 1.0, 1.0) + norm)
        last = jnp.concatenate([last, jnp.zeros((2 * d - 8, LANES), F32)], axis=0)
        xa[rows, 6 * d : 8 * d] = last.T.astype(BF16)
        return 0

    lax.fori_loop(0, ns // LANES, source_block, 0, unroll=4)


def as_row(ref):
    return jnp.concatenate([ref[b : b + 1, :] for b in range(ref.shape[0])], axis=1)


def put_row(row, ref):
    for b in range(ref.shape[0]):
        ref[b : b + 1, :] = row[:, b * LANES : (b + 1) * LANES]


def rows_sweep(x_ref, y_ref, t_ref, lse, out):
    d, ns = x_ref.shape
    y = y_ref[...]
    yn = jnp.sum(y * y, axis=0, keepdims=True)
    t = as_row(t_ref)

    def block(b, _):
        at = pl.multiple_of(b * LANES, LANES)
        xt = jnp.concatenate([x_ref[:, pl.ds(at, LANES)]] * 2, axis=0).T[:, 0:d]
        xn = jnp.sum(xt * xt, axis=1, keepdims=True)
        cross = jnp.dot(xt, y, precision=HIGH, preferred_element_type=F32)
        scores = (2.0 * cross - xn - yn) / EPS + t
        peak = jnp.max(scores, axis=1, keepdims=True)
        weights = jnp.exp(scores - peak)
        total = jnp.sum(weights, axis=1, keepdims=True)
        lse[pl.ds(b, 1), :] = jnp.broadcast_to(peak + jnp.log(total), (LANES, LANES)).T[0:1, :]
        if out is not None:
            vector = lax.dot_general(
                weights / total, y, (((1,), (1,)), ((), ())), precision=HIGH, preferred_element_type=F32
            )
            out[0:d, pl.ds(at, LANES)] = jnp.concatenate([vector, vector], axis=1).T[0:d, :]
        return 0

    lax.fori_loop(0, ns // LANES, block, 0)


def cols_sweep(x_ref, y_ref, r_ref, lse, out, ub):
    d, ns = x_ref.shape
    nt = y_ref.shape[1]
    spread(r_ref[...], ub)
    y = y_ref[...]
    yn = jnp.sum(y * y, axis=0, keepdims=True)

    def block(b, carry):
        at = pl.multiple_of(b * LANES, LANES)
        xb = x_ref[:, pl.ds(at, LANES)]
        xt = jnp.concatenate([xb, xb], axis=0).T[:, 0:d]
        xn = jnp.sum(xt * xt, axis=1, keepdims=True)
        cross = jnp.dot(xt, y, precision=HIGH, preferred_element_type=F32)
        scores = (2.0 * cross - xn - yn) / EPS + ub[pl.ds(at, LANES), 0:1]
        peak = jnp.maximum(carry[0], jnp.max(scores, axis=0, keepdims=True))
        decay = jnp.exp(carry[0] - peak)
        weights = jnp.exp(scores - peak)
        total = carry[1] * decay + jnp.sum(weights, axis=0, keepdims=True)
        if out is not None:
            out[0:d, :] = out[0:d, :] * decay + jnp.dot(
                xb, weights, precision=HIGH, preferred_element_type=F32
            )
        return peak, total

    if out is not None:
        out[0:d, :] = jnp.zeros((d, nt), F32)
    start = (jnp.full((1, nt), -1e30, F32), jnp.zeros((1, nt), F32))
    peak, total = lax.fori_loop(0, ns // LANES, block, start)
    put_row(peak + jnp.log(total), lse)
    if out is not None:
        out[0:d, :] = out[0:d, :] / total


def factors(term):
    top = jnp.max(term)
    return jnp.exp(term - top), top, top - jnp.min(term) <= FACTOR_RANGE


def finish(ref, top, fine):
    values = ref[...]
    ref[...] = jnp.log(values) + (top - SHIFT * LN2)
    return fine & (jnp.min(values) >= SMALLEST)


def fetch(pairs, sem):
    copies = [pltpu.make_async_copy(src, dst, sem.at[i]) for i, (src, dst) in enumerate(pairs)]
    for copy in copies:
        copy.start()
    for copy in copies:
        copy.wait()


def form_kernel(
    x_hbm, y_hbm, a_hbm, b_hbm, k_ref, x_ref, y_ref, row_ref, col_ref, xa, ya, ub, acc, r_s, t_s, sem, *, rows
):
    ns, nt = x_ref.shape[1], y_ref.shape[1]
    fetch(((x_hbm, x_ref), (y_hbm, y_ref), (a_hbm, r_s), (b_hbm, t_s)), sem)
    r_s[...] = jnp.log(r_s[...])
    t_s[...] = jnp.log(t_s[...])
    u, r_top, u_fine = factors(r_s[...])
    v, t_top, v_fine = factors(t_s[...])
    build_operands(x_ref, y_ref, xa, ya)
    spread(u, ub)
    col_ref[...] = v
    acc[...] = jnp.zeros_like(acc)
    tiles = 4 if nt % (4 * LANES) == 0 else 1
    wide = tiles * LANES

    def block(cb, _):
        at = pl.multiple_of(cb * wide, wide)
        vs = [col_ref[pl.ds(cb * tiles + t, 1), :] for t in range(tiles)]
        cs = [jnp.zeros((8, LANES), F32)] * tiles
        for r in range(0, ns, rows):
            z = jnp.dot(xa[r : r + rows, :], ya[:, pl.ds(at, wide)], preferred_element_type=F32)
            k = jnp.exp2(z)
            k_ref[r : r + rows, pl.ds(at, wide)] = k
            ur = ub[r : r + rows, :]
            total = acc[r : r + rows, :]
            for t in range(tiles):
                kt = k[:, t * LANES : (t + 1) * LANES]
                total += kt * vs[t]
                cs[t] += fold(kt * ur)
            acc[r : r + rows, :] = total
        for t in range(tiles):
            col_ref[pl.ds(cb * tiles + t, 1), :] = jnp.sum(cs[t], axis=0, keepdims=True)
        return 0

    lax.fori_loop(0, nt // wide, block, 0)
    lane_sums(acc, row_ref)
    rows_fine = finish(row_ref, t_top, v_fine)
    cols_fine = finish(col_ref, r_top, u_fine)

    @pl.when(jnp.logical_not(rows_fine))
    def _():
        rows_sweep(x_ref, y_ref, t_s, row_ref, None)

    @pl.when(jnp.logical_not(cols_fine))
    def _():
        cols_sweep(x_ref, y_ref, r_s, col_ref, None, ub)


def update(pot_ref, lse_ref, mass_ref, new_ref, term):
    new_ref[...] = 0.5 * (pot_ref[...] - EPS * lse_ref[...])
    term[...] = new_ref[...] / EPS + jnp.log(mass_ref[...])


def sums_kernel(
    k_ref, x_ref, y_ref, f_ref, g_ref, rl_ref, cl_ref, a_ref, b_ref,
    fn_ref, gn_ref, row_ref, col_ref, vs, r_s, t_s, ub,
):
    update(f_ref, rl_ref, a_ref, fn_ref, r_s)
    update(g_ref, cl_ref, b_ref, gn_ref, t_s)
    u, r_top, u_fine = factors(r_s[...])
    v, t_top, v_fine = factors(t_s[...])
    row_ref[...] = u
    vs[...] = v
    ns, nt = k_ref.shape
    tiles = nt // LANES

    def block(rb, cs):
        at = pl.ds(pl.multiple_of(rb * LANES, LANES), LANES)
        ur = jnp.broadcast_to(row_ref[pl.ds(rb, 1), :], (LANES, LANES)).T
        total = jnp.zeros((LANES, LANES), F32)
        out = []
        for c in range(tiles):
            k = k_ref[at, c * LANES : (c + 1) * LANES]
            total += k * vs[c : c + 1, :]
            out.append(cs[c] + fold(k * ur))
        row_ref[pl.ds(rb, 1), :] = jnp.sum(total.T, axis=0, keepdims=True)
        return tuple(out)

    cs = lax.fori_loop(0, ns // LANES, block, (jnp.zeros((8, LANES), F32),) * tiles, unroll=2)
    for c in range(tiles):
        col_ref[c : c + 1, :] = jnp.sum(cs[c], axis=0, keepdims=True)
    rows_fine = finish(row_ref, t_top, v_fine)
    cols_fine = finish(col_ref, r_top, u_fine)

    @pl.when(jnp.logical_not(rows_fine & cols_fine))
    def _():
        rows_sweep(x_ref, y_ref, t_s, row_ref, None)
        cols_sweep(x_ref, y_ref, r_s, col_ref, None, ub)


def weight_rows(out, lse):
    d = out.shape[0] - 8
    for b in range(lse.shape[0]):
        out[d : d + 8, b * LANES : (b + 1) * LANES] = jnp.broadcast_to(lse[b : b + 1, :], (8, LANES))


def parts_of(k):
    k1 = k.astype(BF16)
    return k1, (k - k1.astype(F32)).astype(BF16)


def weighted_points(points, factor, out):
    d = points.shape[0]
    sub = lax.broadcasted_iota(jnp.int32, (16, LANES), 0)
    for b in range(factor.shape[0]):
        at = slice(b * LANES, (b + 1) * LANES)
        row = factor[b : b + 1, :]
        p1, p2 = split2(points[:, at] * row)
        out[0:d, at] = p1.astype(BF16)
        out[d : 2 * d, at] = p2.astype(BF16)
        p1, p2 = split2(jnp.broadcast_to(row, (16, LANES)))
        out[2 * d : 2 * d + 16, at] = jnp.where(sub == 0, p1, jnp.where(sub == 1, p2, 0.0)).astype(BF16)


def means(acc, out, total):
    d = out.shape[0] - 8
    for b in range(total.shape[0]):
        at = slice(b * LANES, (b + 1) * LANES)
        den = acc[2 * d : 2 * d + 1, at] + acc[2 * d + 1 : 2 * d + 2, at]
        out[0:d, at] = (acc[0:d, at] + acc[d : 2 * d, at]) * (1.0 / den)
        total[b : b + 1, :] = den


def maps_kernel(
    k_ref, x_ref, y_ref, f_ref, g_ref, rl_ref, cl_ref, a_ref, b_ref,
    fn_ref, gn_ref, rowm_ref, colm_ref, row_s, col_s, ub, yv, xu, racc, cacc, r_s, t_s, *, rows,
):
    ns, nt = k_ref.shape
    update(f_ref, rl_ref, a_ref, fn_ref, r_s)
    update(g_ref, cl_ref, b_ref, gn_ref, t_s)
    u, r_top, u_fine = factors(r_s[...])
    v, t_top, v_fine = factors(t_s[...])
    weighted_points(y_ref, v, yv)
    weighted_points(x_ref, u, xu)
    wide = 2 * LANES
    racc[...] = jnp.zeros_like(racc)

    def block(cb, _):
        at = pl.multiple_of(cb * wide, wide)
        yc = yv[:, pl.ds(at, wide)]
        yc = jnp.concatenate([yc, yc], axis=1)
        total = jnp.zeros((xu.shape[0], wide), F32)
        for r in range(0, ns, rows):
            k1, k2 = parts_of(k_ref[r : r + rows, pl.ds(at, wide)])
            xr = xu[:, r : r + rows]
            total += jnp.dot(
                jnp.concatenate([xr, xr], axis=1),
                jnp.concatenate([k1, k2], axis=0),
                preferred_element_type=F32,
            )
            racc[:, r : r + rows] += lax.dot_general(
                yc,
                jnp.concatenate([k1, k2], axis=1),
                (((1,), (1,)), ((), ())),
                preferred_element_type=F32,
            )
        cacc[:, pl.ds(at, wide)] = total
        return 0

    lax.fori_loop(0, nt // wide, block, 0)
    means(racc, rowm_ref, row_s)
    means(cacc, colm_ref, col_s)
    rows_fine = finish(row_s, t_top, v_fine)
    cols_fine = finish(col_s, r_top, u_fine)

    @pl.when(jnp.logical_not(rows_fine & cols_fine))
    def _():
        rows_sweep(x_ref, y_ref, t_s, row_s, rowm_ref)
        cols_sweep(x_ref, y_ref, r_s, col_s, colm_ref, ub)

    weight_rows(rowm_ref, row_s)
    weight_rows(colm_ref, col_s)


def merge_kernel(at_ref, whole, *refs, place):
    *others, out = refs
    width = out.shape[1]
    d = whole.shape[0] - 8
    for b in range(width // LANES):
        cols = slice(b * LANES, (b + 1) * LANES)
        at = pl.ds(pl.multiple_of(at_ref[place] + b * LANES, LANES), LANES)
        logs = [whole[d : d + 1, at]] + [other[d : d + 1, cols] for other in others]
        peak = functools.reduce(jnp.maximum, logs)
        weights = [jnp.exp(log - peak) for log in logs]
        total = functools.reduce(jnp.add, weights)
        values = whole[0:d, at] * (weights[0] / total)
        for other, weight in zip(others, weights[1:]):
            values += other[0:d, cols] * (weight / total)
        out[0:d, cols] = values
        if out.shape[0] > d:
            out[d:, cols] = jnp.broadcast_to(peak + jnp.log(total), (8, LANES))


def join_kernel(at_ref, ours, theirs, *refs):
    *pieces, col_out, row_out, sem = refs
    d = col_out.shape[0]
    count = ours.shape[0] // d
    copies = []

    def lay(src, out, place):
        at = pl.multiple_of(at_ref[3 + place], LANES)
        dst = out.at[:, pl.ds(at, src.shape[1])]
        copies.append(pltpu.make_async_copy(src, dst, sem.at[len(copies)]))
        copies[-1].start()

    for which, stack in enumerate((ours, theirs)):
        for k in range(count):
            lay(stack.at[k * d : (k + 1) * d, :], col_out, which * count + k)
    for k, piece_ref in enumerate(pieces):
        lay(piece_ref, row_out, 2 * count + k)
    for copy in copies:
        copy.wait()


VM = pl.BlockSpec(memory_space=pltpu.VMEM)
ANY = pl.BlockSpec(memory_space=pltpu.HBM)
PARAMS = pltpu.CompilerParams(vmem_limit_bytes=24 * 2**20)
FULL = pltpu.CompilerParams(vmem_limit_bytes=46 * 2**20 + 3 * 2**18)


def cost(flops, size):
    return pl.CostEstimate(flops=flops, bytes_accessed=size, transcendentals=0)


def vector(n):
    return jax.ShapeDtypeStruct((n // LANES, LANES), F32)


def near(n):
    return pltpu.VMEM((n // LANES, LANES), F32)


def scratch(n):
    return pltpu.VMEM((n // LANES, LANES), F32)


def form(x, y, a, b):
    d, ns = x.shape
    nt = y.shape[1]
    return pl.pallas_call(
        functools.partial(form_kernel, rows=256),
        out_shape=(
            pltpu.VMEM((ns, nt), F32),
            pltpu.VMEM((d, ns), F32),
            pltpu.VMEM((d, nt), F32),
            near(ns),
            near(nt),
        ),
        in_specs=[ANY] * 4,
        out_specs=(VM,) * 5,
        scratch_shapes=[
            pltpu.VMEM((ns, 8 * d), BF16),
            pltpu.VMEM((8 * d, nt), BF16),
            pltpu.VMEM((ns, LANES), F32),
            pltpu.VMEM((ns, LANES), F32),
            scratch(ns),
            scratch(nt),
            pltpu.SemaphoreType.DMA((4,)),
        ],
        compiler_params=FULL,
        cost_estimate=cost(20 * d * ns * nt, 4 * ns * nt),
        name="form",
    )(x, y, a, b)


def sums(k, x, y, *vectors):
    ns, nt = k.shape
    return pl.pallas_call(
        sums_kernel,
        out_shape=(near(ns), near(nt), near(ns), near(nt)),
        in_specs=[VM] * 9,
        out_specs=(VM,) * 4,
        scratch_shapes=[scratch(nt), scratch(ns), scratch(nt), pltpu.VMEM((ns, LANES), F32)],
        compiler_params=PARAMS,
        cost_estimate=cost(4 * ns * nt, 4 * ns * nt),
        name="sums",
    )(k, x, y, *vectors)


def maps(k, x, y, *vectors):
    d = x.shape[0]
    ns, nt = k.shape
    return pl.pallas_call(
        functools.partial(maps_kernel, rows=256),
        out_shape=(
            vector(ns),
            vector(nt),
            jax.ShapeDtypeStruct((d + 8, ns), F32),
            jax.ShapeDtypeStruct((d + 8, nt), F32),
        ),
        in_specs=[VM] * 9,
        out_specs=(VM,) * 4,
        scratch_shapes=[
            scratch(ns),
            scratch(nt),
            pltpu.VMEM((ns, LANES), F32),
            pltpu.VMEM((2 * d + 16, nt), BF16),
            pltpu.VMEM((2 * d + 16, ns), BF16),
            pltpu.VMEM((2 * d + 16, ns), F32),
            pltpu.VMEM((2 * d + 16, nt), F32),
            scratch(ns),
            scratch(nt),
        ],
        compiler_params=PARAMS,
        cost_estimate=cost(32 * d * ns * nt, 4 * ns * nt),
        name="maps",
    )(k, x, y, *vectors)


def merge(at, place, whole, others, keep):
    rows, width = others[0].shape
    return pl.pallas_call(
        functools.partial(merge_kernel, place=place),
        out_shape=jax.ShapeDtypeStruct((rows if keep else rows - 8, width), F32),
        in_specs=[pl.BlockSpec(memory_space=pltpu.SMEM)] + [VM] * (1 + len(others)),
        out_specs=VM,
        compiler_params=PARAMS,
        name="merge",
    )(at, whole, *others)


def join(at, ours, theirs, pieces):
    d, width = pieces[0].shape
    nt = 2 * ours.shape[0] // d * ours.shape[1]
    ns = width * len(pieces)
    return pl.pallas_call(
        join_kernel,
        out_shape=(jax.ShapeDtypeStruct((d, nt), F32), jax.ShapeDtypeStruct((d, ns), F32)),
        in_specs=[pl.BlockSpec(memory_space=pltpu.SMEM)] + [VM] * (2 + len(pieces)),
        out_specs=(ANY,) * 2,
        scratch_shapes=[pltpu.SemaphoreType.DMA((at.shape[0] - 3,))],
        compiler_params=PARAMS,
        name="join",
    )(at, ours, theirs, *pieces)


def merged(first, second):
    peak = jnp.maximum(first, second)
    return peak + jnp.log(jnp.exp(first - peak) + jnp.exp(second - peak))


def lse_over(axis, part):
    n = lax.axis_size(axis)
    step = n // 2
    while step:
        part = merged(part, lax.ppermute(part, axis, [(i, i ^ step) for i in range(n)]))
        step //= 2
    return part


def partner(place, k, group):
    return place ^ k if group & (group - 1) == 0 else (place + k) % group


def source(place, k, group):
    return place ^ k if group & (group - 1) == 0 else (place - k) % group


def pairs(n, group, stride, k):
    out = []
    for i in range(n):
        place = (i // stride) % group
        out.append((i, i + (partner(place, k, group) - place) * stride))
    return out


def places(index, group, stride, width):
    own = (index // stride) % group
    return (
        [partner(own, k, group) * width for k in range(group)],
        [source(own, k, group) * width for k in range(group)],
    )


def piece(a, at, count):
    zero = jnp.zeros((), at.dtype)
    return lax.dynamic_slice(
        a, (zero, at), (a.shape[0], a.shape[1] // count), allow_negative_indices=False
    )


def pieces_of(axis, place, stride, part):
    n, group = lax.axis_size(axis), len(place)
    return [
        lax.ppermute(piece(part, place[k], group), axis, pairs(n, group, stride, k))
        for k in range(1, group)
    ]


def all_pieces(axis, group, stride, own):
    n = lax.axis_size(axis)
    return [own] + [lax.ppermute(own, axis, pairs(n, group, stride, k)) for k in range(1, group)]


def body(sources, targets, source_mass, target_mass):
    rows, cols = lax.axis_size("row"), lax.axis_size("col")
    ns, nt = sources.shape[1], targets.shape[1]
    index = lax.axis_index("row")
    halves, _ = places(index, 2, 1, nt // 2)
    row_places, row_sources = places(index, rows // 2, 2, nt // rows)
    col_places, col_sources = places(lax.axis_index("col"), cols, 1, ns // cols)
    laid = [halves[0], row_places[0], col_places[0]]
    laid += [half + at for half in halves for at in row_sources] + col_sources
    laid = jnp.stack(laid)
    sources, halves, row_places, col_places, laid = lax.optimization_barrier(
        (sources, halves, row_places, col_places, laid)
    )
    a = source_mass.reshape(-1, LANES)
    b = target_mass.reshape(-1, LANES)
    f = jnp.zeros_like(a)
    g = jnp.zeros_like(b)
    k, x, y, row_part, col_part = form(sources, targets, a, b)
    for sweep in range(ITERS):
        row_lse = lse_over("col", row_part)
        col_lse = lse_over("row", col_part)
        if sweep < ITERS - 1:
            f, g, row_part, col_part = sums(k, x, y, f, g, row_lse, col_lse, a, b)
    f, g, row_part, col_part = maps(k, x, y, f, g, row_lse, col_lse, a, b)
    pair = pairs(rows, 2, 1, 1)
    other = lax.ppermute(piece(col_part, halves[1], 2), "row", pair)
    chip = merge(laid, 0, col_part, [other], True)
    parted = (pieces_of("row", row_places, 2, chip), pieces_of("col", col_places, 1, row_part))
    column_pieces, row_pieces = parted
    own = merge(laid, 2, row_part, row_pieces, False)
    column_pieces, own = lax.optimization_barrier((column_pieces, own))
    ours = merge(laid, 1, chip, column_pieces, False)
    whole = (all_pieces("row", rows // 2, 2, ours), all_pieces("col", cols, 1, own))
    column_pieces, source_pieces = lax.optimization_barrier(whole)
    ours = jnp.concatenate(column_pieces, axis=0)
    theirs = lax.ppermute(ours, "row", pair)
    target_map, source_map = join(laid, ours, theirs, source_pieces)
    return f.reshape(-1), g.reshape(-1), source_map, target_map


def solution(mesh):
    in_specs = (P(None, "row"), P(None, "col"), P("row"), P("col"))
    out_specs = (P("row"), P("col"), P(None, "row"), P(None, "col"))
    return jax.shard_map(body, mesh=mesh, in_specs=in_specs, out_specs=out_specs, check_vma=False)
```

```python
import functools

import jax
import jax.numpy as jnp
from jax import lax
from jax.experimental import pallas as pl
from jax.experimental.pallas import tpu as pltpu
from jax.sharding import PartitionSpec as P

ITERS = 3
EPS = 0.25
LOG2E = 1.4426950408889634
LN2 = 0.6931471805599453
SHIFT = 85.0
SMALLEST = 2.0**-85
FACTOR_RANGE = 60.0 * LN2
LANES = 128
F32 = jnp.float32
BF16 = jnp.bfloat16
HIGH = lax.Precision.HIGHEST


def split2(a):
    a1 = a.astype(BF16).astype(F32)
    return a1, a - a1


def split3(a):
    a1, rest = split2(a)
    a2, rest = split2(rest)
    return a1, a2, rest


def spread(u, ub):
    for b in range(u.shape[0]):
        ub[b * LANES : (b + 1) * LANES, :] = jnp.broadcast_to(u[b : b + 1, :], (LANES, LANES)).T


def lane_sums(acc, out):
    for b in range(out.shape[0]):
        out[b : b + 1, :] = jnp.sum(acc[b * LANES : (b + 1) * LANES, :].T, axis=0, keepdims=True)


def fold(a):
    return jnp.sum(a.reshape(a.shape[0] // 8, 8, a.shape[1]), axis=0)


def tail(row, parts):
    out = jnp.zeros(row.shape, F32)
    for at, part in enumerate(parts):
        out = jnp.where(row == at, part, out)
    return out


def targets_operand(y_ref, ya):
    d, nt = y_ref.shape
    wide = 2 * LANES
    sub = lax.broadcasted_iota(jnp.int32, (16, wide), 0)

    def block(b, _):
        cols = pl.ds(pl.multiple_of(b * wide, wide), wide)
        y = y_ref[:, cols]
        norm = split3(SHIFT - jnp.sum(y * y, axis=0, keepdims=True) * (LOG2E / EPS))
        y1, y2, y3 = (part.astype(BF16) for part in split3(y * (2.0 * LOG2E / EPS)))
        for at, part in enumerate((y1, y2, y1, y2, y3, y1)):
            ya[at * d : (at + 1) * d, cols] = part
        ya[6 * d : 6 * d + 16, cols] = tail(sub, norm + (1.0, 1.0, 1.0)).astype(BF16)
        ya[6 * d + 16 : 8 * d, cols] = jnp.zeros((2 * d - 16, wide), BF16)
        return 0

    lax.fori_loop(0, nt // wide, block, 0, unroll=4)


def sources_operand(x):
    d = x.shape[0]
    lane = lax.broadcasted_iota(jnp.int32, (LANES, 2 * d), 1)
    sub = lax.broadcasted_iota(jnp.int32, (8, LANES), 0)
    norm = split3(jnp.sum(x * x, axis=0, keepdims=True) * (-LOG2E / EPS))
    x1, x2, x3 = split3(jnp.concatenate([x, x], axis=0).T)
    last = tail(sub, (1.0, 1.0, 1.0) + norm)
    last = jnp.concatenate([last, jnp.zeros((2 * d - 8, LANES), F32)], axis=0).T
    parts = (x1, x2, jnp.where(lane < d, x1, x3), last)
    return jnp.concatenate([part.astype(BF16) for part in parts], axis=1)


def as_row(ref):
    return jnp.concatenate([ref[b : b + 1, :] for b in range(ref.shape[0])], axis=1)


def put_row(row, ref):
    for b in range(ref.shape[0]):
        ref[b : b + 1, :] = row[:, b * LANES : (b + 1) * LANES]


def rows_sweep(x_ref, y_ref, t_ref, lse, out):
    d, ns = x_ref.shape
    y = y_ref[...]
    yn = jnp.sum(y * y, axis=0, keepdims=True)
    t = as_row(t_ref)

    def block(b, _):
        at = pl.multiple_of(b * LANES, LANES)
        xt = jnp.concatenate([x_ref[:, pl.ds(at, LANES)]] * 2, axis=0).T[:, 0:d]
        xn = jnp.sum(xt * xt, axis=1, keepdims=True)
        cross = jnp.dot(xt, y, precision=HIGH, preferred_element_type=F32)
        scores = (2.0 * cross - xn - yn) / EPS + t
        peak = jnp.max(scores, axis=1, keepdims=True)
        weights = jnp.exp(scores - peak)
        total = jnp.sum(weights, axis=1, keepdims=True)
        lse[pl.ds(b, 1), :] = jnp.broadcast_to(peak + jnp.log(total), (LANES, LANES)).T[0:1, :]
        if out is not None:
            vector = lax.dot_general(
                weights / total, y, (((1,), (1,)), ((), ())), precision=HIGH, preferred_element_type=F32
            )
            out[0:d, pl.ds(at, LANES)] = jnp.concatenate([vector, vector], axis=1).T[0:d, :]
        return 0

    lax.fori_loop(0, ns // LANES, block, 0)


def cols_sweep(x_ref, y_ref, r_ref, lse, out, ub):
    d, ns = x_ref.shape
    nt = y_ref.shape[1]
    spread(r_ref[...], ub)
    y = y_ref[...]
    yn = jnp.sum(y * y, axis=0, keepdims=True)

    def block(b, carry):
        at = pl.multiple_of(b * LANES, LANES)
        xb = x_ref[:, pl.ds(at, LANES)]
        xt = jnp.concatenate([xb, xb], axis=0).T[:, 0:d]
        xn = jnp.sum(xt * xt, axis=1, keepdims=True)
        cross = jnp.dot(xt, y, precision=HIGH, preferred_element_type=F32)
        scores = (2.0 * cross - xn - yn) / EPS + ub[pl.ds(at, LANES), 0:1]
        peak = jnp.maximum(carry[0], jnp.max(scores, axis=0, keepdims=True))
        decay = jnp.exp(carry[0] - peak)
        weights = jnp.exp(scores - peak)
        total = carry[1] * decay + jnp.sum(weights, axis=0, keepdims=True)
        if out is not None:
            out[0:d, :] = out[0:d, :] * decay + jnp.dot(
                xb, weights, precision=HIGH, preferred_element_type=F32
            )
        return peak, total

    if out is not None:
        out[0:d, :] = jnp.zeros((d, nt), F32)
    start = (jnp.full((1, nt), -1e30, F32), jnp.zeros((1, nt), F32))
    peak, total = lax.fori_loop(0, ns // LANES, block, start)
    put_row(peak + jnp.log(total), lse)
    if out is not None:
        out[0:d, :] = out[0:d, :] / total


def factors(term):
    top = jnp.max(term)
    return jnp.exp(term - top), top, top - jnp.min(term) <= FACTOR_RANGE


def finish(ref, top, fine):
    values = ref[...]
    ref[...] = jnp.log(values) + (top - SHIFT * LN2)
    return fine & (jnp.min(values) >= SMALLEST)


def fetch(pairs, sem):
    copies = [pltpu.make_async_copy(src, dst, sem.at[i]) for i, (src, dst) in enumerate(pairs)]
    for copy in copies:
        copy.start()
    for copy in copies:
        copy.wait()


def form_kernel(
    x_hbm, y_hbm, a_hbm, b_hbm, k_ref, x_ref, y_ref, row_ref, col_ref, xa, ya, ub, r_s, t_s, vs, cs, sem, *, tiles
):
    ns, nt = x_ref.shape[1], y_ref.shape[1]
    fetch(((x_hbm, x_ref), (y_hbm, y_ref), (a_hbm, r_s), (b_hbm, t_s)), sem)
    r_s[...] = jnp.log(r_s[...])
    t_s[...] = jnp.log(t_s[...])
    u, r_top, u_fine = factors(r_s[...])
    v, t_top, v_fine = factors(t_s[...])
    row_ref[...] = u
    vs[...] = v
    targets_operand(y_ref, ya)
    cs[...] = jnp.zeros_like(cs)
    wide = tiles * LANES
    tall = xa.shape[1]

    def operand(rb, slot):
        for b in range(tall // LANES):
            at = pl.ds(pl.multiple_of(rb * tall + b * LANES, LANES), LANES)
            xa[slot, b * LANES : (b + 1) * LANES, :] = sources_operand(x_ref[:, at])

    def block(rb, slot):
        at = pl.ds(pl.multiple_of(rb * tall, tall), tall)
        lanes = tall // LANES
        ur = [
            jnp.broadcast_to(row_ref[pl.ds(rb * lanes + b, 1), :], (LANES, LANES)).T for b in range(lanes)
        ]
        ur = jnp.concatenate(ur, axis=0)
        total = jnp.zeros((tall, LANES), F32)
        for c in range(0, nt, wide):
            z = jnp.dot(xa[slot], ya[:, c : c + wide], preferred_element_type=F32)
            k = jnp.exp2(z)
            k_ref[at, c : c + wide] = k
            for t in range(tiles):
                kt = k[:, t * LANES : (t + 1) * LANES]
                total += kt * vs[c // LANES + t : c // LANES + t + 1, :]
                cs[:, c + t * LANES : c + (t + 1) * LANES] += fold(kt * ur)
        for b in range(lanes):
            part = total[b * LANES : (b + 1) * LANES, :]
            row_ref[pl.ds(rb * lanes + b, 1), :] = jnp.sum(part.T, axis=0, keepdims=True)

    count = ns // tall
    operand(0, 0)

    def two(pair, _):
        first = pair * 2
        operand(first + 1, 1)
        block(first, 0)
        operand(jnp.minimum(first + 2, count - 1), 0)
        block(first + 1, 1)
        return 0

    lax.fori_loop(0, count // 2, two, 0)
    put_row(jnp.sum(cs[...], axis=0, keepdims=True), col_ref)
    rows_fine = finish(row_ref, t_top, v_fine)
    cols_fine = finish(col_ref, r_top, u_fine)

    @pl.when(jnp.logical_not(rows_fine))
    def _():
        rows_sweep(x_ref, y_ref, t_s, row_ref, None)

    @pl.when(jnp.logical_not(cols_fine))
    def _():
        cols_sweep(x_ref, y_ref, r_s, col_ref, None, ub)


def update(pot_ref, lse_ref, mass_ref, new_ref, term):
    new_ref[...] = 0.5 * (pot_ref[...] - EPS * lse_ref[...])
    term[...] = new_ref[...] / EPS + jnp.log(mass_ref[...])


def sums_kernel(
    k_ref, x_ref, y_ref, f_ref, g_ref, rl_ref, cl_ref, a_ref, b_ref,
    fn_ref, gn_ref, row_ref, col_ref, vs, r_s, t_s, ub, cs,
):
    update(f_ref, rl_ref, a_ref, fn_ref, r_s)
    update(g_ref, cl_ref, b_ref, gn_ref, t_s)
    u, r_top, u_fine = factors(r_s[...])
    v, t_top, v_fine = factors(t_s[...])
    row_ref[...] = u
    vs[...] = v
    ns, nt = k_ref.shape
    tiles = nt // LANES

    def block(rb, _):
        at = pl.ds(pl.multiple_of(rb * LANES, LANES), LANES)
        ur = jnp.broadcast_to(row_ref[pl.ds(rb, 1), :], (LANES, LANES)).T
        total = jnp.zeros((LANES, LANES), F32)
        for c in range(tiles):
            k = k_ref[at, c * LANES : (c + 1) * LANES]
            total += k * vs[c : c + 1, :]
            cs[:, c * LANES : (c + 1) * LANES] += fold(k * ur)
        row_ref[pl.ds(rb, 1), :] = jnp.sum(total.T, axis=0, keepdims=True)
        return 0

    cs[...] = jnp.zeros_like(cs)
    lax.fori_loop(0, ns // LANES, block, 0, unroll=2)
    put_row(jnp.sum(cs[...], axis=0, keepdims=True), col_ref)
    rows_fine = finish(row_ref, t_top, v_fine)
    cols_fine = finish(col_ref, r_top, u_fine)

    @pl.when(jnp.logical_not(rows_fine & cols_fine))
    def _():
        rows_sweep(x_ref, y_ref, t_s, row_ref, None)
        cols_sweep(x_ref, y_ref, r_s, col_ref, None, ub)


def weight_rows(out, lse):
    d = out.shape[0] - 8
    for b in range(lse.shape[0]):
        out[d : d + 8, b * LANES : (b + 1) * LANES] = jnp.broadcast_to(lse[b : b + 1, :], (8, LANES))


def parts_of(k):
    k1 = k.astype(BF16)
    return k1, (k - k1.astype(F32)).astype(BF16)


def weighted_points(points, factor, out):
    d = points.shape[0]
    sub = lax.broadcasted_iota(jnp.int32, (16, LANES), 0)
    for b in range(factor.shape[0]):
        at = slice(b * LANES, (b + 1) * LANES)
        row = factor[b : b + 1, :]
        p1, p2 = split2(points[:, at] * row)
        out[0:d, at] = p1.astype(BF16)
        out[d : 2 * d, at] = p2.astype(BF16)
        p1, p2 = split2(jnp.broadcast_to(row, (16, LANES)))
        out[2 * d : 2 * d + 16, at] = jnp.where(sub == 0, p1, jnp.where(sub == 1, p2, 0.0)).astype(BF16)


def means(acc, out, total):
    d = out.shape[0] - 8
    for b in range(total.shape[0]):
        at = slice(b * LANES, (b + 1) * LANES)
        den = acc[2 * d : 2 * d + 1, at] + acc[2 * d + 1 : 2 * d + 2, at]
        out[0:d, at] = (acc[0:d, at] + acc[d : 2 * d, at]) * (1.0 / den)
        total[b : b + 1, :] = den


def maps_kernel(
    k_ref, x_ref, y_ref, f_ref, g_ref, rl_ref, cl_ref, a_ref, b_ref,
    fn_ref, gn_ref, rowm_ref, colm_ref, row_s, col_s, ub, yv, xu, racc, cacc, r_s, t_s, *, rows,
):
    ns, nt = k_ref.shape
    update(f_ref, rl_ref, a_ref, fn_ref, r_s)
    update(g_ref, cl_ref, b_ref, gn_ref, t_s)
    u, r_top, u_fine = factors(r_s[...])
    v, t_top, v_fine = factors(t_s[...])
    weighted_points(y_ref, v, yv)
    weighted_points(x_ref, u, xu)
    yc = jnp.concatenate([yv[...], yv[...]], axis=1)
    total = jnp.zeros(cacc.shape, F32)
    for r in range(0, ns, rows):
        k1, k2 = parts_of(k_ref[r : r + rows, :])
        xr = xu[:, r : r + rows]
        total += jnp.dot(
            jnp.concatenate([xr, xr], axis=1),
            jnp.concatenate([k1, k2], axis=0),
            preferred_element_type=F32,
        )
        racc[:, r : r + rows] = lax.dot_general(
            yc,
            jnp.concatenate([k1, k2], axis=1),
            (((1,), (1,)), ((), ())),
            preferred_element_type=F32,
        )
    cacc[...] = total
    means(racc, rowm_ref, row_s)
    means(cacc, colm_ref, col_s)
    rows_fine = finish(row_s, t_top, v_fine)
    cols_fine = finish(col_s, r_top, u_fine)

    @pl.when(jnp.logical_not(rows_fine & cols_fine))
    def _():
        rows_sweep(x_ref, y_ref, t_s, row_s, rowm_ref)
        cols_sweep(x_ref, y_ref, r_s, col_s, colm_ref, ub)

    weight_rows(rowm_ref, row_s)
    weight_rows(colm_ref, col_s)


def merge_kernel(at_ref, whole, *refs, place):
    *others, out = refs
    width = out.shape[1]
    d = whole.shape[0] - 8
    for b in range(width // LANES):
        cols = slice(b * LANES, (b + 1) * LANES)
        at = pl.ds(pl.multiple_of(at_ref[place] + b * LANES, LANES), LANES)
        logs = [whole[d : d + 1, at]] + [other[d : d + 1, cols] for other in others]
        peak = functools.reduce(jnp.maximum, logs)
        weights = [jnp.exp(log - peak) for log in logs]
        total = functools.reduce(jnp.add, weights)
        values = whole[0:d, at] * (weights[0] / total)
        for other, weight in zip(others, weights[1:]):
            values += other[0:d, cols] * (weight / total)
        out[0:d, cols] = values
        if out.shape[0] > d:
            out[d:, cols] = jnp.broadcast_to(peak + jnp.log(total), (8, LANES))


def join_kernel(at_ref, ours, theirs, *refs):
    *pieces, col_out, row_out, sem = refs
    d = col_out.shape[0]
    count = ours.shape[0] // d
    copies = []

    def lay(src, out, place):
        at = pl.multiple_of(at_ref[3 + place], LANES)
        dst = out.at[:, pl.ds(at, src.shape[1])]
        copies.append(pltpu.make_async_copy(src, dst, sem.at[len(copies)]))
        copies[-1].start()

    for which, stack in enumerate((ours, theirs)):
        for k in range(count):
            lay(stack.at[k * d : (k + 1) * d, :], col_out, which * count + k)
    for k, piece_ref in enumerate(pieces):
        lay(piece_ref, row_out, 2 * count + k)
    for copy in copies:
        copy.wait()


VM = pl.BlockSpec(memory_space=pltpu.VMEM)
ANY = pl.BlockSpec(memory_space=pltpu.HBM)
PARAMS = pltpu.CompilerParams(vmem_limit_bytes=24 * 2**20)
FULL = pltpu.CompilerParams(vmem_limit_bytes=46 * 2**20 + 3 * 2**18)


def cost(flops, size):
    return pl.CostEstimate(flops=flops, bytes_accessed=size, transcendentals=0)


def vector(n):
    return jax.ShapeDtypeStruct((n // LANES, LANES), F32)


def near(n):
    return pltpu.VMEM((n // LANES, LANES), F32)


def scratch(n):
    return pltpu.VMEM((n // LANES, LANES), F32)


def form(x, y, a, b):
    d, ns = x.shape
    nt = y.shape[1]
    return pl.pallas_call(
        functools.partial(form_kernel, tiles=4),
        out_shape=(
            pltpu.VMEM((ns, nt), F32),
            pltpu.VMEM((d, ns), F32),
            pltpu.VMEM((d, nt), F32),
            near(ns),
            near(nt),
        ),
        in_specs=[ANY] * 4,
        out_specs=(VM,) * 5,
        scratch_shapes=[
            pltpu.VMEM((2, 256, 8 * d), BF16),
            pltpu.VMEM((8 * d, nt), BF16),
            pltpu.VMEM((ns, LANES), F32),
            scratch(ns),
            scratch(nt),
            scratch(nt),
            pltpu.VMEM((8, nt), F32),
            pltpu.SemaphoreType.DMA((4,)),
        ],
        compiler_params=FULL,
        cost_estimate=cost(20 * d * ns * nt, 4 * ns * nt),
        name="form",
    )(x, y, a, b)


def sums(k, x, y, *vectors):
    ns, nt = k.shape
    return pl.pallas_call(
        sums_kernel,
        out_shape=(near(ns), near(nt), near(ns), near(nt)),
        in_specs=[VM] * 9,
        out_specs=(VM,) * 4,
        scratch_shapes=[
            scratch(nt),
            scratch(ns),
            scratch(nt),
            pltpu.VMEM((ns, LANES), F32),
            pltpu.VMEM((8, nt), F32),
        ],
        compiler_params=PARAMS,
        cost_estimate=cost(4 * ns * nt, 4 * ns * nt),
        name="sums",
    )(k, x, y, *vectors)


def maps(k, x, y, *vectors):
    d = x.shape[0]
    ns, nt = k.shape
    return pl.pallas_call(
        functools.partial(maps_kernel, rows=256),
        out_shape=(
            vector(ns),
            vector(nt),
            jax.ShapeDtypeStruct((d + 8, ns), F32),
            jax.ShapeDtypeStruct((d + 8, nt), F32),
        ),
        in_specs=[VM] * 9,
        out_specs=(VM,) * 4,
        scratch_shapes=[
            scratch(ns),
            scratch(nt),
            pltpu.VMEM((ns, LANES), F32),
            pltpu.VMEM((2 * d + 16, nt), BF16),
            pltpu.VMEM((2 * d + 16, ns), BF16),
            pltpu.VMEM((2 * d + 16, ns), F32),
            pltpu.VMEM((2 * d + 16, nt), F32),
            scratch(ns),
            scratch(nt),
        ],
        compiler_params=PARAMS,
        cost_estimate=cost(32 * d * ns * nt, 4 * ns * nt),
        name="maps",
    )(k, x, y, *vectors)


def merge(at, place, whole, others, keep):
    rows, width = others[0].shape
    return pl.pallas_call(
        functools.partial(merge_kernel, place=place),
        out_shape=jax.ShapeDtypeStruct((rows if keep else rows - 8, width), F32),
        in_specs=[pl.BlockSpec(memory_space=pltpu.SMEM)] + [VM] * (1 + len(others)),
        out_specs=VM,
        compiler_params=PARAMS,
        name="merge",
    )(at, whole, *others)


def join(at, ours, theirs, pieces):
    d, width = pieces[0].shape
    nt = 2 * ours.shape[0] // d * ours.shape[1]
    ns = width * len(pieces)
    return pl.pallas_call(
        join_kernel,
        out_shape=(jax.ShapeDtypeStruct((d, nt), F32), jax.ShapeDtypeStruct((d, ns), F32)),
        in_specs=[pl.BlockSpec(memory_space=pltpu.SMEM)] + [VM] * (2 + len(pieces)),
        out_specs=(ANY,) * 2,
        scratch_shapes=[pltpu.SemaphoreType.DMA((at.shape[0] - 3,))],
        compiler_params=PARAMS,
        name="join",
    )(at, ours, theirs, *pieces)


def merged(first, second):
    peak = jnp.maximum(first, second)
    return peak + jnp.log(jnp.exp(first - peak) + jnp.exp(second - peak))


def lse_over(axis, part):
    n = lax.axis_size(axis)
    step = n // 2
    while step:
        part = merged(part, lax.ppermute(part, axis, [(i, i ^ step) for i in range(n)]))
        step //= 2
    return part


def partner(place, k, group):
    return place ^ k if group & (group - 1) == 0 else (place + k) % group


def source(place, k, group):
    return place ^ k if group & (group - 1) == 0 else (place - k) % group


def pairs(n, group, stride, k):
    out = []
    for i in range(n):
        place = (i // stride) % group
        out.append((i, i + (partner(place, k, group) - place) * stride))
    return out


def places(index, group, stride, width):
    own = (index // stride) % group
    return (
        [partner(own, k, group) * width for k in range(group)],
        [source(own, k, group) * width for k in range(group)],
    )


def piece(a, at, count):
    zero = jnp.zeros((), at.dtype)
    return lax.dynamic_slice(
        a, (zero, at), (a.shape[0], a.shape[1] // count), allow_negative_indices=False
    )


def pieces_of(axis, place, stride, part):
    n, group = lax.axis_size(axis), len(place)
    return [
        lax.ppermute(piece(part, place[k], group), axis, pairs(n, group, stride, k))
        for k in range(1, group)
    ]


def all_pieces(axis, group, stride, own):
    n = lax.axis_size(axis)
    return [own] + [lax.ppermute(own, axis, pairs(n, group, stride, k)) for k in range(1, group)]


def body(sources, targets, source_mass, target_mass):
    rows, cols = lax.axis_size("row"), lax.axis_size("col")
    ns, nt = sources.shape[1], targets.shape[1]
    index = lax.axis_index("row")
    halves, _ = places(index, 2, 1, nt // 2)
    row_places, row_sources = places(index, rows // 2, 2, nt // rows)
    col_places, col_sources = places(lax.axis_index("col"), cols, 1, ns // cols)
    laid = [halves[0], row_places[0], col_places[0]]
    laid += [half + at for half in halves for at in row_sources] + col_sources
    laid = jnp.stack(laid)
    sources, halves, row_places, col_places, laid = lax.optimization_barrier(
        (sources, halves, row_places, col_places, laid)
    )
    a = source_mass.reshape(-1, LANES)
    b = target_mass.reshape(-1, LANES)
    f = jnp.zeros_like(a)
    g = jnp.zeros_like(b)
    k, x, y, row_part, col_part = form(sources, targets, a, b)
    for sweep in range(ITERS):
        row_lse = lse_over("col", row_part)
        col_lse = lse_over("row", col_part)
        if sweep < ITERS - 1:
            f, g, row_part, col_part = sums(k, x, y, f, g, row_lse, col_lse, a, b)
    f, g, row_part, col_part = maps(k, x, y, f, g, row_lse, col_lse, a, b)
    pair = pairs(rows, 2, 1, 1)
    other = lax.ppermute(piece(col_part, halves[1], 2), "row", pair)
    chip = merge(laid, 0, col_part, [other], True)
    parted = (pieces_of("row", row_places, 2, chip), pieces_of("col", col_places, 1, row_part))
    column_pieces, row_pieces = parted
    own = merge(laid, 2, row_part, row_pieces, False)
    column_pieces, own = lax.optimization_barrier((column_pieces, own))
    ours = merge(laid, 1, chip, column_pieces, False)
    whole = (all_pieces("row", rows // 2, 2, ours), all_pieces("col", cols, 1, own))
    column_pieces, source_pieces = lax.optimization_barrier(whole)
    ours = jnp.concatenate(column_pieces, axis=0)
    theirs = lax.ppermute(ours, "row", pair)
    target_map, source_map = join(laid, ours, theirs, source_pieces)
    return f.reshape(-1), g.reshape(-1), source_map, target_map


def solution(mesh):
    in_specs = (P(None, "row"), P(None, "col"), P("row"), P("col"))
    out_specs = (P("row"), P("col"), P(None, "row"), P(None, "col"))
    return jax.shard_map(body, mesh=mesh, in_specs=in_specs, out_specs=out_specs, check_vma=False)
```

```python
import functools

import jax
import jax.numpy as jnp
from jax import lax
from jax.experimental import pallas as pl
from jax.experimental.pallas import tpu as pltpu
from jax.sharding import PartitionSpec as P

ITERS = 3
EPS = 0.25
LOG2E = 1.4426950408889634
LN2 = 0.6931471805599453
SHIFT = 85.0
SMALLEST = 2.0**-85
FACTOR_RANGE = 60.0 * LN2
LANES = 128
F32 = jnp.float32
BF16 = jnp.bfloat16
HIGH = lax.Precision.HIGHEST


def split2(a):
    a1 = a.astype(BF16).astype(F32)
    return a1, a - a1


def split3(a):
    a1, rest = split2(a)
    a2, rest = split2(rest)
    return a1, a2, rest


def spread(u, ub):
    for b in range(u.shape[0]):
        ub[b * LANES : (b + 1) * LANES, :] = jnp.broadcast_to(u[b : b + 1, :], (LANES, LANES)).T


def lane_sums(acc, out):
    for b in range(out.shape[0]):
        out[b : b + 1, :] = jnp.sum(acc[b * LANES : (b + 1) * LANES, :].T, axis=0, keepdims=True)


def fold(a):
    return jnp.sum(a.reshape(a.shape[0] // 8, 8, a.shape[1]), axis=0)


def tail(row, parts):
    out = jnp.zeros(row.shape, F32)
    for at, part in enumerate(parts):
        out = jnp.where(row == at, part, out)
    return out


def targets_operand(y_ref, ya):
    d, nt = y_ref.shape
    wide = 2 * LANES
    sub = lax.broadcasted_iota(jnp.int32, (16, wide), 0)

    def block(b, _):
        cols = pl.ds(pl.multiple_of(b * wide, wide), wide)
        y = y_ref[:, cols]
        norm = split3(SHIFT - jnp.sum(y * y, axis=0, keepdims=True) * (LOG2E / EPS))
        y1, y2, y3 = (part.astype(BF16) for part in split3(y * (2.0 * LOG2E / EPS)))
        for at, part in enumerate((y1, y2, y1, y2, y3, y1)):
            ya[at * d : (at + 1) * d, cols] = part
        ya[6 * d : 6 * d + 16, cols] = tail(sub, norm + (1.0, 1.0, 1.0)).astype(BF16)
        ya[6 * d + 16 : 8 * d, cols] = jnp.zeros((2 * d - 16, wide), BF16)
        return 0

    lax.fori_loop(0, nt // wide, block, 0, unroll=4)


def sources_operand(x):
    d = x.shape[0]
    lane = lax.broadcasted_iota(jnp.int32, (LANES, 2 * d), 1)
    sub = lax.broadcasted_iota(jnp.int32, (8, LANES), 0)
    norm = split3(jnp.sum(x * x, axis=0, keepdims=True) * (-LOG2E / EPS))
    x1, x2, x3 = split3(jnp.concatenate([x, x], axis=0).T)
    last = tail(sub, (1.0, 1.0, 1.0) + norm)
    last = jnp.concatenate([last, jnp.zeros((2 * d - 8, LANES), F32)], axis=0).T
    parts = (x1, x2, jnp.where(lane < d, x1, x3), last)
    return jnp.concatenate([part.astype(BF16) for part in parts], axis=1)


def as_row(ref):
    return jnp.concatenate([ref[b : b + 1, :] for b in range(ref.shape[0])], axis=1)


def put_row(row, ref):
    for b in range(ref.shape[0]):
        ref[b : b + 1, :] = row[:, b * LANES : (b + 1) * LANES]


def rows_sweep(x_ref, y_ref, t_ref, lse, out):
    d, ns = x_ref.shape
    y = y_ref[...]
    yn = jnp.sum(y * y, axis=0, keepdims=True)
    t = as_row(t_ref)

    def block(b, _):
        at = pl.multiple_of(b * LANES, LANES)
        xt = jnp.concatenate([x_ref[:, pl.ds(at, LANES)]] * 2, axis=0).T[:, 0:d]
        xn = jnp.sum(xt * xt, axis=1, keepdims=True)
        cross = jnp.dot(xt, y, precision=HIGH, preferred_element_type=F32)
        scores = (2.0 * cross - xn - yn) / EPS + t
        peak = jnp.max(scores, axis=1, keepdims=True)
        weights = jnp.exp(scores - peak)
        total = jnp.sum(weights, axis=1, keepdims=True)
        lse[pl.ds(b, 1), :] = jnp.broadcast_to(peak + jnp.log(total), (LANES, LANES)).T[0:1, :]
        if out is not None:
            vector = lax.dot_general(
                weights / total, y, (((1,), (1,)), ((), ())), precision=HIGH, preferred_element_type=F32
            )
            out[0:d, pl.ds(at, LANES)] = jnp.concatenate([vector, vector], axis=1).T[0:d, :]
        return 0

    lax.fori_loop(0, ns // LANES, block, 0)


def cols_sweep(x_ref, y_ref, r_ref, lse, out, ub):
    d, ns = x_ref.shape
    nt = y_ref.shape[1]
    spread(r_ref[...], ub)
    y = y_ref[...]
    yn = jnp.sum(y * y, axis=0, keepdims=True)

    def block(b, carry):
        at = pl.multiple_of(b * LANES, LANES)
        xb = x_ref[:, pl.ds(at, LANES)]
        xt = jnp.concatenate([xb, xb], axis=0).T[:, 0:d]
        xn = jnp.sum(xt * xt, axis=1, keepdims=True)
        cross = jnp.dot(xt, y, precision=HIGH, preferred_element_type=F32)
        scores = (2.0 * cross - xn - yn) / EPS + ub[pl.ds(at, LANES), 0:1]
        peak = jnp.maximum(carry[0], jnp.max(scores, axis=0, keepdims=True))
        decay = jnp.exp(carry[0] - peak)
        weights = jnp.exp(scores - peak)
        total = carry[1] * decay + jnp.sum(weights, axis=0, keepdims=True)
        if out is not None:
            out[0:d, :] = out[0:d, :] * decay + jnp.dot(
                xb, weights, precision=HIGH, preferred_element_type=F32
            )
        return peak, total

    if out is not None:
        out[0:d, :] = jnp.zeros((d, nt), F32)
    start = (jnp.full((1, nt), -1e30, F32), jnp.zeros((1, nt), F32))
    peak, total = lax.fori_loop(0, ns // LANES, block, start)
    put_row(peak + jnp.log(total), lse)
    if out is not None:
        out[0:d, :] = out[0:d, :] / total


def factors(term):
    top = jnp.max(term)
    return jnp.exp(term - top), top, top - jnp.min(term) <= FACTOR_RANGE


def finish(ref, top, fine):
    values = ref[...]
    ref[...] = jnp.log(values) + (top - SHIFT * LN2)
    return fine & (jnp.min(values) >= SMALLEST)


def fetch(pairs, sem):
    copies = [pltpu.make_async_copy(src, dst, sem.at[i]) for i, (src, dst) in enumerate(pairs)]
    for copy in copies:
        copy.start()
    for copy in copies:
        copy.wait()


def form_kernel(
    x_hbm, y_hbm, a_hbm, b_hbm, k_ref, x_ref, y_ref, row_ref, col_ref, xa, ya, ub, r_s, t_s, vs, cs, sem, *, tiles
):
    ns, nt = x_ref.shape[1], y_ref.shape[1]
    fetch(((x_hbm, x_ref), (y_hbm, y_ref), (a_hbm, r_s), (b_hbm, t_s)), sem)
    r_s[...] = jnp.log(r_s[...])
    t_s[...] = jnp.log(t_s[...])
    u, r_top, u_fine = factors(r_s[...])
    v, t_top, v_fine = factors(t_s[...])
    row_ref[...] = u
    vs[...] = v
    targets_operand(y_ref, ya)
    cs[...] = jnp.zeros_like(cs)
    wide = tiles * LANES
    tall = xa.shape[1]

    def operand(rb, slot):
        for b in range(tall // LANES):
            at = pl.ds(pl.multiple_of(rb * tall + b * LANES, LANES), LANES)
            xa[slot, b * LANES : (b + 1) * LANES, :] = sources_operand(x_ref[:, at])

    def block(rb, slot):
        at = pl.ds(pl.multiple_of(rb * tall, tall), tall)
        lanes = tall // LANES
        ur = [
            jnp.broadcast_to(row_ref[pl.ds(rb * lanes + b, 1), :], (LANES, LANES)).T for b in range(lanes)
        ]
        ur = jnp.concatenate(ur, axis=0)
        total = jnp.zeros((tall, LANES), F32)
        for c in range(0, nt, wide):
            z = jnp.dot(xa[slot], ya[:, c : c + wide], preferred_element_type=F32)
            k = jnp.exp2(z)
            k_ref[at, c : c + wide] = k
            for t in range(tiles):
                kt = k[:, t * LANES : (t + 1) * LANES]
                total += kt * vs[c // LANES + t : c // LANES + t + 1, :]
                cs[:, c + t * LANES : c + (t + 1) * LANES] += fold(kt * ur)
        for b in range(lanes):
            part = total[b * LANES : (b + 1) * LANES, :]
            row_ref[pl.ds(rb * lanes + b, 1), :] = jnp.sum(part.T, axis=0, keepdims=True)

    count = ns // tall
    operand(0, 0)

    def two(pair, _):
        first = pair * 2
        operand(first + 1, 1)
        block(first, 0)
        operand(jnp.minimum(first + 2, count - 1), 0)
        block(first + 1, 1)
        return 0

    lax.fori_loop(0, count // 2, two, 0)
    put_row(jnp.sum(cs[...], axis=0, keepdims=True), col_ref)
    rows_fine = finish(row_ref, t_top, v_fine)
    cols_fine = finish(col_ref, r_top, u_fine)

    @pl.when(jnp.logical_not(rows_fine))
    def _():
        rows_sweep(x_ref, y_ref, t_s, row_ref, None)

    @pl.when(jnp.logical_not(cols_fine))
    def _():
        cols_sweep(x_ref, y_ref, r_s, col_ref, None, ub)


def update(pot_ref, lse_ref, mass_ref, new_ref, term):
    new_ref[...] = 0.5 * (pot_ref[...] - EPS * lse_ref[...])
    term[...] = new_ref[...] / EPS + jnp.log(mass_ref[...])


def sums_kernel(
    k_ref, x_ref, y_ref, f_ref, g_ref, rl_ref, cl_ref, a_ref, b_ref,
    fn_ref, gn_ref, row_ref, col_ref, vs, r_s, t_s, ub, cs,
):
    update(f_ref, rl_ref, a_ref, fn_ref, r_s)
    update(g_ref, cl_ref, b_ref, gn_ref, t_s)
    u, r_top, u_fine = factors(r_s[...])
    v, t_top, v_fine = factors(t_s[...])
    row_ref[...] = u
    vs[...] = v
    ns, nt = k_ref.shape
    tiles = nt // LANES

    def block(rb, _):
        at = pl.ds(pl.multiple_of(rb * LANES, LANES), LANES)
        ur = jnp.broadcast_to(row_ref[pl.ds(rb, 1), :], (LANES, LANES)).T
        total = jnp.zeros((LANES, LANES), F32)
        for c in range(tiles):
            k = k_ref[at, c * LANES : (c + 1) * LANES]
            total += k * vs[c : c + 1, :]
            cs[:, c * LANES : (c + 1) * LANES] += fold(k * ur)
        row_ref[pl.ds(rb, 1), :] = jnp.sum(total.T, axis=0, keepdims=True)
        return 0

    cs[...] = jnp.zeros_like(cs)
    lax.fori_loop(0, ns // LANES, block, 0, unroll=2)
    put_row(jnp.sum(cs[...], axis=0, keepdims=True), col_ref)
    rows_fine = finish(row_ref, t_top, v_fine)
    cols_fine = finish(col_ref, r_top, u_fine)

    @pl.when(jnp.logical_not(rows_fine & cols_fine))
    def _():
        rows_sweep(x_ref, y_ref, t_s, row_ref, None)
        cols_sweep(x_ref, y_ref, r_s, col_ref, None, ub)


def weight_rows(out, lse):
    d = out.shape[0] - 8
    for b in range(lse.shape[0]):
        out[d : d + 8, b * LANES : (b + 1) * LANES] = jnp.broadcast_to(lse[b : b + 1, :], (8, LANES))


def parts_of(k):
    k1 = k.astype(BF16)
    return k1, (k - k1.astype(F32)).astype(BF16)


def weighted_points(points, factor, out):
    d = points.shape[0]
    sub = lax.broadcasted_iota(jnp.int32, (16, LANES), 0)
    for b in range(factor.shape[0]):
        at = slice(b * LANES, (b + 1) * LANES)
        row = factor[b : b + 1, :]
        p1, p2 = split2(points[:, at] * row)
        out[0:d, at] = p1.astype(BF16)
        out[d : 2 * d, at] = p2.astype(BF16)
        p1, p2 = split2(jnp.broadcast_to(row, (16, LANES)))
        out[2 * d : 2 * d + 16, at] = jnp.where(sub == 0, p1, jnp.where(sub == 1, p2, 0.0)).astype(BF16)


def means(acc, out, total):
    d = out.shape[0] - 8
    for b in range(total.shape[0]):
        at = slice(b * LANES, (b + 1) * LANES)
        den = acc[2 * d : 2 * d + 1, at] + acc[2 * d + 1 : 2 * d + 2, at]
        out[0:d, at] = (acc[0:d, at] + acc[d : 2 * d, at]) * (1.0 / den)
        total[b : b + 1, :] = den


def maps_kernel(
    k_ref, x_ref, y_ref, f_ref, g_ref, rl_ref, cl_ref, a_ref, b_ref,
    fn_ref, gn_ref, rowm_ref, colm_ref, row_s, col_s, ub, yv, xu, racc, cacc, r_s, t_s, *, rows,
):
    ns, nt = k_ref.shape
    update(f_ref, rl_ref, a_ref, fn_ref, r_s)
    update(g_ref, cl_ref, b_ref, gn_ref, t_s)
    u, r_top, u_fine = factors(r_s[...])
    v, t_top, v_fine = factors(t_s[...])
    weighted_points(y_ref, v, yv)
    weighted_points(x_ref, u, xu)
    yc = jnp.concatenate([yv[...], yv[...]], axis=1)
    total = jnp.zeros(cacc.shape, F32)
    for r in range(0, ns, rows):
        k1, k2 = parts_of(k_ref[r : r + rows, :])
        xr = xu[:, r : r + rows]
        total += jnp.dot(
            jnp.concatenate([xr, xr], axis=1),
            jnp.concatenate([k1, k2], axis=0),
            preferred_element_type=F32,
        )
        racc[:, r : r + rows] = lax.dot_general(
            yc,
            jnp.concatenate([k1, k2], axis=1),
            (((1,), (1,)), ((), ())),
            preferred_element_type=F32,
        )
    cacc[...] = total
    means(racc, rowm_ref, row_s)
    means(cacc, colm_ref, col_s)
    rows_fine = finish(row_s, t_top, v_fine)
    cols_fine = finish(col_s, r_top, u_fine)

    @pl.when(jnp.logical_not(rows_fine & cols_fine))
    def _():
        rows_sweep(x_ref, y_ref, t_s, row_s, rowm_ref)
        cols_sweep(x_ref, y_ref, r_s, col_s, colm_ref, ub)

    weight_rows(rowm_ref, row_s)
    weight_rows(colm_ref, col_s)


def merge_kernel(at_ref, whole, *refs, place):
    *others, out = refs
    width = out.shape[1]
    d = whole.shape[0] - 8
    for b in range(width // LANES):
        cols = slice(b * LANES, (b + 1) * LANES)
        at = pl.ds(pl.multiple_of(at_ref[place] + b * LANES, LANES), LANES)
        logs = [whole[d : d + 1, at]] + [other[d : d + 1, cols] for other in others]
        peak = functools.reduce(jnp.maximum, logs)
        weights = [jnp.exp(log - peak) for log in logs]
        total = functools.reduce(jnp.add, weights)
        values = whole[0:d, at] * (weights[0] / total)
        for other, weight in zip(others, weights[1:]):
            values += other[0:d, cols] * (weight / total)
        out[0:d, cols] = values
        if out.shape[0] > d:
            out[d:, cols] = jnp.broadcast_to(peak + jnp.log(total), (8, LANES))


def lay(at_ref, pieces, outs, sem):
    copies = []
    for (src, place), out in zip(pieces, outs):
        at = pl.multiple_of(at_ref[place], LANES)
        dst = out.at[:, pl.ds(at, src.shape[1])]
        copies.append(pltpu.make_async_copy(src, dst, sem.at[len(copies)]))
        copies[-1].start()
    for copy in copies:
        copy.wait()


def join_kernel(at_ref, ours, *refs):
    *pieces, col_out, row_out, sem = refs
    d = col_out.shape[0]
    count = ours.shape[0] // d
    laid = [(ours.at[k * d : (k + 1) * d, :], 3 + k) for k in range(count)]
    laid += [(piece_ref, 3 + 2 * count + k) for k, piece_ref in enumerate(pieces)]
    lay(at_ref, laid, [col_out] * count + [row_out] * len(pieces), sem)


def rest_kernel(at_ref, theirs, _, col_out, sem):
    d = col_out.shape[0]
    count = theirs.shape[0] // d
    laid = [(theirs.at[k * d : (k + 1) * d, :], 3 + count + k) for k in range(count)]
    lay(at_ref, laid, [col_out] * count, sem)


VM = pl.BlockSpec(memory_space=pltpu.VMEM)
ANY = pl.BlockSpec(memory_space=pltpu.HBM)
PARAMS = pltpu.CompilerParams(vmem_limit_bytes=24 * 2**20)
FULL = pltpu.CompilerParams(vmem_limit_bytes=46 * 2**20 + 3 * 2**18)


def cost(flops, size):
    return pl.CostEstimate(flops=flops, bytes_accessed=size, transcendentals=0)


def vector(n):
    return jax.ShapeDtypeStruct((n // LANES, LANES), F32)


def near(n):
    return pltpu.VMEM((n // LANES, LANES), F32)


def scratch(n):
    return pltpu.VMEM((n // LANES, LANES), F32)


def form(x, y, a, b):
    d, ns = x.shape
    nt = y.shape[1]
    return pl.pallas_call(
        functools.partial(form_kernel, tiles=4),
        out_shape=(
            pltpu.VMEM((ns, nt), F32),
            pltpu.VMEM((d, ns), F32),
            pltpu.VMEM((d, nt), F32),
            near(ns),
            near(nt),
        ),
        in_specs=[ANY] * 4,
        out_specs=(VM,) * 5,
        scratch_shapes=[
            pltpu.VMEM((2, 256, 8 * d), BF16),
            pltpu.VMEM((8 * d, nt), BF16),
            pltpu.VMEM((ns, LANES), F32),
            scratch(ns),
            scratch(nt),
            scratch(nt),
            pltpu.VMEM((8, nt), F32),
            pltpu.SemaphoreType.DMA((4,)),
        ],
        compiler_params=FULL,
        cost_estimate=cost(20 * d * ns * nt, 4 * ns * nt),
        name="form",
    )(x, y, a, b)


def sums(k, x, y, *vectors):
    ns, nt = k.shape
    return pl.pallas_call(
        sums_kernel,
        out_shape=(near(ns), near(nt), near(ns), near(nt)),
        in_specs=[VM] * 9,
        out_specs=(VM,) * 4,
        scratch_shapes=[
            scratch(nt),
            scratch(ns),
            scratch(nt),
            pltpu.VMEM((ns, LANES), F32),
            pltpu.VMEM((8, nt), F32),
        ],
        compiler_params=PARAMS,
        cost_estimate=cost(4 * ns * nt, 4 * ns * nt),
        name="sums",
    )(k, x, y, *vectors)


def maps(k, x, y, *vectors):
    d = x.shape[0]
    ns, nt = k.shape
    return pl.pallas_call(
        functools.partial(maps_kernel, rows=256),
        out_shape=(
            vector(ns),
            vector(nt),
            jax.ShapeDtypeStruct((d + 8, ns), F32),
            jax.ShapeDtypeStruct((d + 8, nt), F32),
        ),
        in_specs=[VM] * 9,
        out_specs=(VM,) * 4,
        scratch_shapes=[
            scratch(ns),
            scratch(nt),
            pltpu.VMEM((ns, LANES), F32),
            pltpu.VMEM((2 * d + 16, nt), BF16),
            pltpu.VMEM((2 * d + 16, ns), BF16),
            pltpu.VMEM((2 * d + 16, ns), F32),
            pltpu.VMEM((2 * d + 16, nt), F32),
            scratch(ns),
            scratch(nt),
        ],
        compiler_params=PARAMS,
        cost_estimate=cost(32 * d * ns * nt, 4 * ns * nt),
        name="maps",
    )(k, x, y, *vectors)


def merge(at, place, whole, others, keep):
    rows, width = others[0].shape
    return pl.pallas_call(
        functools.partial(merge_kernel, place=place),
        out_shape=jax.ShapeDtypeStruct((rows if keep else rows - 8, width), F32),
        in_specs=[pl.BlockSpec(memory_space=pltpu.SMEM)] + [VM] * (1 + len(others)),
        out_specs=VM,
        compiler_params=PARAMS,
        name="merge",
    )(at, whole, *others)


def join(at, ours, pieces):
    d, width = pieces[0].shape
    count = ours.shape[0] // d
    smem = pl.BlockSpec(memory_space=pltpu.SMEM)
    return pl.pallas_call(
        join_kernel,
        out_shape=(
            jax.ShapeDtypeStruct((d, 2 * count * ours.shape[1]), F32),
            jax.ShapeDtypeStruct((d, width * len(pieces)), F32),
        ),
        in_specs=[smem] + [VM] * (1 + len(pieces)),
        out_specs=(ANY,) * 2,
        scratch_shapes=[pltpu.SemaphoreType.DMA((count + len(pieces),))],
        compiler_params=PARAMS,
        cost_estimate=cost(0, 2**20),
        name="join",
    )(at, ours, *pieces)


def rest(at, theirs, col):
    count = theirs.shape[0] // col.shape[0]
    return pl.pallas_call(
        rest_kernel,
        out_shape=jax.ShapeDtypeStruct(col.shape, F32),
        in_specs=[pl.BlockSpec(memory_space=pltpu.SMEM), VM, ANY],
        out_specs=ANY,
        scratch_shapes=[pltpu.SemaphoreType.DMA((count,))],
        input_output_aliases={2: 0},
        compiler_params=PARAMS,
        name="rest",
    )(at, theirs, col)


def merged(first, second):
    peak = jnp.maximum(first, second)
    return peak + jnp.log(jnp.exp(first - peak) + jnp.exp(second - peak))


def lse_over(axis, part):
    n = lax.axis_size(axis)
    step = n // 2
    while step:
        part = merged(part, lax.ppermute(part, axis, [(i, i ^ step) for i in range(n)]))
        step //= 2
    return part


def partner(place, k, group):
    return place ^ k if group & (group - 1) == 0 else (place + k) % group


def source(place, k, group):
    return place ^ k if group & (group - 1) == 0 else (place - k) % group


def pairs(n, group, stride, k):
    out = []
    for i in range(n):
        place = (i // stride) % group
        out.append((i, i + (partner(place, k, group) - place) * stride))
    return out


def places(index, group, stride, width):
    own = (index // stride) % group
    return (
        [partner(own, k, group) * width for k in range(group)],
        [source(own, k, group) * width for k in range(group)],
    )


def piece(a, at, count):
    zero = jnp.zeros((), at.dtype)
    return lax.dynamic_slice(
        a, (zero, at), (a.shape[0], a.shape[1] // count), allow_negative_indices=False
    )


def pieces_of(axis, place, stride, part):
    n, group = lax.axis_size(axis), len(place)
    return [
        lax.ppermute(piece(part, place[k], group), axis, pairs(n, group, stride, k))
        for k in range(1, group)
    ]


def all_pieces(axis, group, stride, own):
    n = lax.axis_size(axis)
    return [own] + [lax.ppermute(own, axis, pairs(n, group, stride, k)) for k in range(1, group)]


def body(sources, targets, source_mass, target_mass):
    rows, cols = lax.axis_size("row"), lax.axis_size("col")
    ns, nt = sources.shape[1], targets.shape[1]
    index = lax.axis_index("row")
    halves, _ = places(index, 2, 1, nt // 2)
    row_places, row_sources = places(index, rows // 2, 2, nt // rows)
    col_places, col_sources = places(lax.axis_index("col"), cols, 1, ns // cols)
    laid = [halves[0], row_places[0], col_places[0]]
    laid += [half + at for half in halves for at in row_sources] + col_sources
    laid = jnp.stack(laid)
    sources, halves, row_places, col_places, laid = lax.optimization_barrier(
        (sources, halves, row_places, col_places, laid)
    )
    a = source_mass.reshape(-1, LANES)
    b = target_mass.reshape(-1, LANES)
    f = jnp.zeros_like(a)
    g = jnp.zeros_like(b)
    k, x, y, row_part, col_part = form(sources, targets, a, b)
    for sweep in range(ITERS):
        row_lse = lse_over("col", row_part)
        col_lse = lse_over("row", col_part)
        if sweep < ITERS - 1:
            f, g, row_part, col_part = sums(k, x, y, f, g, row_lse, col_lse, a, b)
    f, g, row_part, col_part = maps(k, x, y, f, g, row_lse, col_lse, a, b)
    pair = pairs(rows, 2, 1, 1)
    other = lax.ppermute(piece(col_part, halves[1], 2), "row", pair)
    chip = merge(laid, 0, col_part, [other], True)
    parted = (pieces_of("row", row_places, 2, chip), pieces_of("col", col_places, 1, row_part))
    column_pieces, row_pieces = parted
    own = merge(laid, 2, row_part, row_pieces, False)
    column_pieces, own = lax.optimization_barrier((column_pieces, own))
    ours = merge(laid, 1, chip, column_pieces, False)
    whole = (all_pieces("row", rows // 2, 2, ours), all_pieces("col", cols, 1, own))
    column_pieces, source_pieces = lax.optimization_barrier(whole)
    ours = jnp.concatenate(column_pieces, axis=0)
    theirs = lax.ppermute(ours, "row", pair)
    target_map, source_map = join(laid, ours, source_pieces)
    target_map = rest(laid, theirs, target_map)
    return f.reshape(-1), g.reshape(-1), source_map, target_map


def solution(mesh):
    in_specs = (P(None, "row"), P(None, "col"), P("row"), P("col"))
    out_specs = (P("row"), P("col"), P(None, "row"), P(None, "col"))
    return jax.shard_map(body, mesh=mesh, in_specs=in_specs, out_specs=out_specs, check_vma=False)
```

```python
import functools

import jax
import jax.numpy as jnp
from jax import lax
from jax.experimental import pallas as pl
from jax.experimental.pallas import tpu as pltpu
from jax.sharding import PartitionSpec as P

ITERS = 3
EPS = 0.25
LOG2E = 1.4426950408889634
LN2 = 0.6931471805599453
SHIFT = 85.0
SMALLEST = 2.0**-85
FACTOR_RANGE = 60.0 * LN2
LANES = 128
F32 = jnp.float32
BF16 = jnp.bfloat16
HIGH = lax.Precision.HIGHEST


def split2(a):
    a1 = a.astype(BF16).astype(F32)
    return a1, a - a1


def split3(a):
    a1, rest = split2(a)
    a2, rest = split2(rest)
    return a1, a2, rest


def spread(u, ub):
    for b in range(u.shape[0]):
        ub[b * LANES : (b + 1) * LANES, :] = jnp.broadcast_to(u[b : b + 1, :], (LANES, LANES)).T


def lane_sums(acc, out):
    for b in range(out.shape[0]):
        out[b : b + 1, :] = jnp.sum(acc[b * LANES : (b + 1) * LANES, :].T, axis=0, keepdims=True)


def fold(a):
    return jnp.sum(a.reshape(a.shape[0] // 8, 8, a.shape[1]), axis=0)


def tail(row, parts):
    out = jnp.zeros(row.shape, F32)
    for at, part in enumerate(parts):
        out = jnp.where(row == at, part, out)
    return out


def targets_operand(y_ref, ya):
    d, nt = y_ref.shape
    wide = 2 * LANES
    sub = lax.broadcasted_iota(jnp.int32, (16, wide), 0)

    def block(b, _):
        cols = pl.ds(pl.multiple_of(b * wide, wide), wide)
        y = y_ref[:, cols]
        norm = split3(SHIFT - jnp.sum(y * y, axis=0, keepdims=True) * (LOG2E / EPS))
        y1, y2, y3 = (part.astype(BF16) for part in split3(y * (2.0 * LOG2E / EPS)))
        for at, part in enumerate((y1, y2, y1, y2, y3, y1)):
            ya[at * d : (at + 1) * d, cols] = part
        ya[6 * d : 6 * d + 16, cols] = tail(sub, norm + (1.0, 1.0, 1.0)).astype(BF16)
        ya[6 * d + 16 : 8 * d, cols] = jnp.zeros((2 * d - 16, wide), BF16)
        return 0

    lax.fori_loop(0, nt // wide, block, 0, unroll=4)


def sources_operand(x):
    d = x.shape[0]
    lane = lax.broadcasted_iota(jnp.int32, (LANES, 2 * d), 1)
    sub = lax.broadcasted_iota(jnp.int32, (8, LANES), 0)
    norm = split3(jnp.sum(x * x, axis=0, keepdims=True) * (-LOG2E / EPS))
    x1, x2, x3 = split3(jnp.concatenate([x, x], axis=0).T)
    last = tail(sub, (1.0, 1.0, 1.0) + norm)
    last = jnp.concatenate([last, jnp.zeros((2 * d - 8, LANES), F32)], axis=0).T
    parts = (x1, x2, jnp.where(lane < d, x1, x3), last)
    return jnp.concatenate([part.astype(BF16) for part in parts], axis=1)


def as_row(ref):
    return jnp.concatenate([ref[b : b + 1, :] for b in range(ref.shape[0])], axis=1)


def put_row(row, ref):
    for b in range(ref.shape[0]):
        ref[b : b + 1, :] = row[:, b * LANES : (b + 1) * LANES]


def rows_sweep(x_ref, y_ref, t_ref, lse, out):
    d, ns = x_ref.shape
    y = y_ref[...]
    yn = jnp.sum(y * y, axis=0, keepdims=True)
    t = as_row(t_ref)

    def block(b, _):
        at = pl.multiple_of(b * LANES, LANES)
        xt = jnp.concatenate([x_ref[:, pl.ds(at, LANES)]] * 2, axis=0).T[:, 0:d]
        xn = jnp.sum(xt * xt, axis=1, keepdims=True)
        cross = jnp.dot(xt, y, precision=HIGH, preferred_element_type=F32)
        scores = (2.0 * cross - xn - yn) / EPS + t
        peak = jnp.max(scores, axis=1, keepdims=True)
        weights = jnp.exp(scores - peak)
        total = jnp.sum(weights, axis=1, keepdims=True)
        lse[pl.ds(b, 1), :] = jnp.broadcast_to(peak + jnp.log(total), (LANES, LANES)).T[0:1, :]
        if out is not None:
            vector = lax.dot_general(
                weights / total, y, (((1,), (1,)), ((), ())), precision=HIGH, preferred_element_type=F32
            )
            out[0:d, pl.ds(at, LANES)] = jnp.concatenate([vector, vector], axis=1).T[0:d, :]
        return 0

    lax.fori_loop(0, ns // LANES, block, 0)


def cols_sweep(x_ref, y_ref, r_ref, lse, out, ub):
    d, ns = x_ref.shape
    nt = y_ref.shape[1]
    spread(r_ref[...], ub)
    y = y_ref[...]
    yn = jnp.sum(y * y, axis=0, keepdims=True)

    def block(b, carry):
        at = pl.multiple_of(b * LANES, LANES)
        xb = x_ref[:, pl.ds(at, LANES)]
        xt = jnp.concatenate([xb, xb], axis=0).T[:, 0:d]
        xn = jnp.sum(xt * xt, axis=1, keepdims=True)
        cross = jnp.dot(xt, y, precision=HIGH, preferred_element_type=F32)
        scores = (2.0 * cross - xn - yn) / EPS + ub[pl.ds(at, LANES), 0:1]
        peak = jnp.maximum(carry[0], jnp.max(scores, axis=0, keepdims=True))
        decay = jnp.exp(carry[0] - peak)
        weights = jnp.exp(scores - peak)
        total = carry[1] * decay + jnp.sum(weights, axis=0, keepdims=True)
        if out is not None:
            out[0:d, :] = out[0:d, :] * decay + jnp.dot(
                xb, weights, precision=HIGH, preferred_element_type=F32
            )
        return peak, total

    if out is not None:
        out[0:d, :] = jnp.zeros((d, nt), F32)
    start = (jnp.full((1, nt), -1e30, F32), jnp.zeros((1, nt), F32))
    peak, total = lax.fori_loop(0, ns // LANES, block, start)
    put_row(peak + jnp.log(total), lse)
    if out is not None:
        out[0:d, :] = out[0:d, :] / total


def factors(term):
    top = jnp.max(term)
    return jnp.exp(term - top), top, top - jnp.min(term) <= FACTOR_RANGE


def finish(ref, top, fine):
    values = ref[...]
    ref[...] = jnp.log(values) + (top - SHIFT * LN2)
    return fine & (jnp.min(values) >= SMALLEST)


def fetch(pairs, sem):
    copies = [pltpu.make_async_copy(src, dst, sem.at[i]) for i, (src, dst) in enumerate(pairs)]
    for copy in copies:
        copy.start()
    return copies


def form_kernel(
    x_hbm, y_hbm, a_hbm, b_hbm, k_ref, x_ref, y_ref, row_ref, col_ref, xa, ya, ub, r_s, t_s, vs, cs, sem, *, tiles
):
    ns, nt = x_ref.shape[1], y_ref.shape[1]
    targets, *others = fetch(((y_hbm, y_ref), (x_hbm, x_ref), (a_hbm, r_s), (b_hbm, t_s)), sem)
    cs[...] = jnp.zeros_like(cs)
    targets.wait()
    targets_operand(y_ref, ya)
    for copy in others:
        copy.wait()
    r_s[...] = jnp.log(r_s[...])
    t_s[...] = jnp.log(t_s[...])
    u, r_top, u_fine = factors(r_s[...])
    v, t_top, v_fine = factors(t_s[...])
    row_ref[...] = u
    vs[...] = v
    wide = tiles * LANES
    tall = xa.shape[1]

    def operand(rb, slot):
        for b in range(tall // LANES):
            at = pl.ds(pl.multiple_of(rb * tall + b * LANES, LANES), LANES)
            xa[slot, b * LANES : (b + 1) * LANES, :] = sources_operand(x_ref[:, at])

    def block(rb, slot):
        at = pl.ds(pl.multiple_of(rb * tall, tall), tall)
        lanes = tall // LANES
        ur = [
            jnp.broadcast_to(row_ref[pl.ds(rb * lanes + b, 1), :], (LANES, LANES)).T for b in range(lanes)
        ]
        ur = jnp.concatenate(ur, axis=0)
        total = jnp.zeros((tall, LANES), F32)
        for c in range(0, nt, wide):
            z = jnp.dot(xa[slot], ya[:, c : c + wide], preferred_element_type=F32)
            k = jnp.exp2(z)
            k_ref[at, c : c + wide] = k
            for t in range(tiles):
                kt = k[:, t * LANES : (t + 1) * LANES]
                total += kt * vs[c // LANES + t : c // LANES + t + 1, :]
                cs[:, c + t * LANES : c + (t + 1) * LANES] += fold(kt * ur)
        for b in range(lanes):
            part = total[b * LANES : (b + 1) * LANES, :]
            row_ref[pl.ds(rb * lanes + b, 1), :] = jnp.sum(part.T, axis=0, keepdims=True)

    count = ns // tall
    operand(0, 0)

    def two(pair, _):
        first = pair * 2
        operand(first + 1, 1)
        block(first, 0)
        operand(jnp.minimum(first + 2, count - 1), 0)
        block(first + 1, 1)
        return 0

    lax.fori_loop(0, count // 2, two, 0)
    put_row(jnp.sum(cs[...], axis=0, keepdims=True), col_ref)
    rows_fine = finish(row_ref, t_top, v_fine)
    cols_fine = finish(col_ref, r_top, u_fine)

    @pl.when(jnp.logical_not(rows_fine))
    def _():
        rows_sweep(x_ref, y_ref, t_s, row_ref, None)

    @pl.when(jnp.logical_not(cols_fine))
    def _():
        cols_sweep(x_ref, y_ref, r_s, col_ref, None, ub)


def update(pot_ref, lse_ref, mass_ref, new_ref, term):
    new_ref[...] = 0.5 * (pot_ref[...] - EPS * lse_ref[...])
    term[...] = new_ref[...] / EPS + jnp.log(mass_ref[...])


def sums_kernel(
    k_ref, x_ref, y_ref, f_ref, g_ref, rl_ref, cl_ref, a_ref, b_ref,
    fn_ref, gn_ref, row_ref, col_ref, vs, r_s, t_s, ub, cs,
):
    update(f_ref, rl_ref, a_ref, fn_ref, r_s)
    update(g_ref, cl_ref, b_ref, gn_ref, t_s)
    u, r_top, u_fine = factors(r_s[...])
    v, t_top, v_fine = factors(t_s[...])
    row_ref[...] = u
    vs[...] = v
    ns, nt = k_ref.shape
    tiles = nt // LANES

    def block(rb, _):
        at = pl.ds(pl.multiple_of(rb * LANES, LANES), LANES)
        ur = jnp.broadcast_to(row_ref[pl.ds(rb, 1), :], (LANES, LANES)).T
        total = jnp.zeros((LANES, LANES), F32)
        for c in range(tiles):
            k = k_ref[at, c * LANES : (c + 1) * LANES]
            total += k * vs[c : c + 1, :]
            cs[:, c * LANES : (c + 1) * LANES] += fold(k * ur)
        row_ref[pl.ds(rb, 1), :] = jnp.sum(total.T, axis=0, keepdims=True)
        return 0

    cs[...] = jnp.zeros_like(cs)
    lax.fori_loop(0, ns // LANES, block, 0, unroll=2)
    put_row(jnp.sum(cs[...], axis=0, keepdims=True), col_ref)
    rows_fine = finish(row_ref, t_top, v_fine)
    cols_fine = finish(col_ref, r_top, u_fine)

    @pl.when(jnp.logical_not(rows_fine & cols_fine))
    def _():
        rows_sweep(x_ref, y_ref, t_s, row_ref, None)
        cols_sweep(x_ref, y_ref, r_s, col_ref, None, ub)


def weight_rows(out, lse):
    d = out.shape[0] - 8
    for b in range(lse.shape[0]):
        out[d : d + 8, b * LANES : (b + 1) * LANES] = jnp.broadcast_to(lse[b : b + 1, :], (8, LANES))


def parts_of(k):
    k1 = k.astype(BF16)
    return k1, (k - k1.astype(F32)).astype(BF16)


def weighted_points(points, factor, out):
    d = points.shape[0]
    sub = lax.broadcasted_iota(jnp.int32, (16, LANES), 0)
    for b in range(factor.shape[0]):
        at = slice(b * LANES, (b + 1) * LANES)
        row = factor[b : b + 1, :]
        p1, p2 = split2(points[:, at] * row)
        out[0:d, at] = p1.astype(BF16)
        out[d : 2 * d, at] = p2.astype(BF16)
        p1, p2 = split2(jnp.broadcast_to(row, (16, LANES)))
        out[2 * d : 2 * d + 16, at] = jnp.where(sub == 0, p1, jnp.where(sub == 1, p2, 0.0)).astype(BF16)


def means(acc, out, total):
    d = out.shape[0] - 8
    for b in range(total.shape[0]):
        at = slice(b * LANES, (b + 1) * LANES)
        den = acc[2 * d : 2 * d + 1, at] + acc[2 * d + 1 : 2 * d + 2, at]
        out[0:d, at] = (acc[0:d, at] + acc[d : 2 * d, at]) * (1.0 / den)
        total[b : b + 1, :] = den


def maps_kernel(
    k_ref, x_ref, y_ref, f_ref, g_ref, rl_ref, cl_ref, a_ref, b_ref,
    fn_ref, gn_ref, rowm_ref, colm_ref, row_s, col_s, ub, yv, xu, racc, cacc, r_s, t_s, *, rows,
):
    ns, nt = k_ref.shape
    update(f_ref, rl_ref, a_ref, fn_ref, r_s)
    update(g_ref, cl_ref, b_ref, gn_ref, t_s)
    u, r_top, u_fine = factors(r_s[...])
    v, t_top, v_fine = factors(t_s[...])
    weighted_points(y_ref, v, yv)
    weighted_points(x_ref, u, xu)
    yc = jnp.concatenate([yv[...], yv[...]], axis=1)
    total = jnp.zeros(cacc.shape, F32)
    for r in range(0, ns, rows):
        k1, k2 = parts_of(k_ref[r : r + rows, :])
        xr = xu[:, r : r + rows]
        total += jnp.dot(
            jnp.concatenate([xr, xr], axis=1),
            jnp.concatenate([k1, k2], axis=0),
            preferred_element_type=F32,
        )
        racc[:, r : r + rows] = lax.dot_general(
            yc,
            jnp.concatenate([k1, k2], axis=1),
            (((1,), (1,)), ((), ())),
            preferred_element_type=F32,
        )
    cacc[...] = total
    means(racc, rowm_ref, row_s)
    means(cacc, colm_ref, col_s)
    rows_fine = finish(row_s, t_top, v_fine)
    cols_fine = finish(col_s, r_top, u_fine)

    @pl.when(jnp.logical_not(rows_fine & cols_fine))
    def _():
        rows_sweep(x_ref, y_ref, t_s, row_s, rowm_ref)
        cols_sweep(x_ref, y_ref, r_s, col_s, colm_ref, ub)

    weight_rows(rowm_ref, row_s)
    weight_rows(colm_ref, col_s)


def merge_kernel(at_ref, whole, *refs, place):
    *others, out = refs
    width = out.shape[1]
    d = whole.shape[0] - 8
    for b in range(width // LANES):
        cols = slice(b * LANES, (b + 1) * LANES)
        at = pl.ds(pl.multiple_of(at_ref[place] + b * LANES, LANES), LANES)
        logs = [whole[d : d + 1, at]] + [other[d : d + 1, cols] for other in others]
        peak = functools.reduce(jnp.maximum, logs)
        weights = [jnp.exp(log - peak) for log in logs]
        total = functools.reduce(jnp.add, weights)
        values = whole[0:d, at] * (weights[0] / total)
        for other, weight in zip(others, weights[1:]):
            values += other[0:d, cols] * (weight / total)
        out[0:d, cols] = values
        if out.shape[0] > d:
            out[d:, cols] = jnp.broadcast_to(peak + jnp.log(total), (8, LANES))


def lay(at_ref, pieces, outs, sem):
    copies = []
    for (src, place), out in zip(pieces, outs):
        at = pl.multiple_of(at_ref[place], LANES)
        dst = out.at[:, pl.ds(at, src.shape[1])]
        copies.append(pltpu.make_async_copy(src, dst, sem.at[len(copies)]))
        copies[-1].start()
    for copy in copies:
        copy.wait()


def join_kernel(at_ref, ours, *refs):
    *pieces, col_out, row_out, sem = refs
    d = col_out.shape[0]
    count = ours.shape[0] // d
    laid = [(ours.at[k * d : (k + 1) * d, :], 3 + k) for k in range(count)]
    laid += [(piece_ref, 3 + 2 * count + k) for k, piece_ref in enumerate(pieces)]
    lay(at_ref, laid, [col_out] * count + [row_out] * len(pieces), sem)


def rest_kernel(at_ref, theirs, _, col_out, sem):
    d = col_out.shape[0]
    count = theirs.shape[0] // d
    laid = [(theirs.at[k * d : (k + 1) * d, :], 3 + count + k) for k in range(count)]
    lay(at_ref, laid, [col_out] * count, sem)


VM = pl.BlockSpec(memory_space=pltpu.VMEM)
ANY = pl.BlockSpec(memory_space=pltpu.HBM)
PARAMS = pltpu.CompilerParams(vmem_limit_bytes=24 * 2**20)
FULL = pltpu.CompilerParams(vmem_limit_bytes=46 * 2**20 + 3 * 2**18)


def cost(flops, size):
    return pl.CostEstimate(flops=flops, bytes_accessed=size, transcendentals=0)


def vector(n):
    return jax.ShapeDtypeStruct((n // LANES, LANES), F32)


def near(n):
    return pltpu.VMEM((n // LANES, LANES), F32)


def scratch(n):
    return pltpu.VMEM((n // LANES, LANES), F32)


def form(x, y, a, b):
    d, ns = x.shape
    nt = y.shape[1]
    return pl.pallas_call(
        functools.partial(form_kernel, tiles=4),
        out_shape=(
            pltpu.VMEM((ns, nt), F32),
            pltpu.VMEM((d, ns), F32),
            pltpu.VMEM((d, nt), F32),
            near(ns),
            near(nt),
        ),
        in_specs=[ANY] * 4,
        out_specs=(VM,) * 5,
        scratch_shapes=[
            pltpu.VMEM((2, 256, 8 * d), BF16),
            pltpu.VMEM((8 * d, nt), BF16),
            pltpu.VMEM((ns, LANES), F32),
            scratch(ns),
            scratch(nt),
            scratch(nt),
            pltpu.VMEM((8, nt), F32),
            pltpu.SemaphoreType.DMA((4,)),
        ],
        compiler_params=FULL,
        cost_estimate=cost(20 * d * ns * nt, 4 * ns * nt),
        name="form",
    )(x, y, a, b)


def sums(k, x, y, *vectors):
    ns, nt = k.shape
    return pl.pallas_call(
        sums_kernel,
        out_shape=(near(ns), near(nt), near(ns), near(nt)),
        in_specs=[VM] * 9,
        out_specs=(VM,) * 4,
        scratch_shapes=[
            scratch(nt),
            scratch(ns),
            scratch(nt),
            pltpu.VMEM((ns, LANES), F32),
            pltpu.VMEM((8, nt), F32),
        ],
        compiler_params=PARAMS,
        cost_estimate=cost(4 * ns * nt, 4 * ns * nt),
        name="sums",
    )(k, x, y, *vectors)


def maps(k, x, y, *vectors):
    d = x.shape[0]
    ns, nt = k.shape
    return pl.pallas_call(
        functools.partial(maps_kernel, rows=256),
        out_shape=(
            vector(ns),
            vector(nt),
            jax.ShapeDtypeStruct((d + 8, ns), F32),
            jax.ShapeDtypeStruct((d + 8, nt), F32),
        ),
        in_specs=[VM] * 9,
        out_specs=(VM,) * 4,
        scratch_shapes=[
            scratch(ns),
            scratch(nt),
            pltpu.VMEM((ns, LANES), F32),
            pltpu.VMEM((2 * d + 16, nt), BF16),
            pltpu.VMEM((2 * d + 16, ns), BF16),
            pltpu.VMEM((2 * d + 16, ns), F32),
            pltpu.VMEM((2 * d + 16, nt), F32),
            scratch(ns),
            scratch(nt),
        ],
        compiler_params=PARAMS,
        cost_estimate=cost(32 * d * ns * nt, 4 * ns * nt),
        name="maps",
    )(k, x, y, *vectors)


def merge(at, place, whole, others, keep):
    rows, width = others[0].shape
    return pl.pallas_call(
        functools.partial(merge_kernel, place=place),
        out_shape=jax.ShapeDtypeStruct((rows if keep else rows - 8, width), F32),
        in_specs=[pl.BlockSpec(memory_space=pltpu.SMEM)] + [VM] * (1 + len(others)),
        out_specs=VM,
        compiler_params=PARAMS,
        name="merge",
    )(at, whole, *others)


def join(at, ours, pieces):
    d, width = pieces[0].shape
    count = ours.shape[0] // d
    smem = pl.BlockSpec(memory_space=pltpu.SMEM)
    return pl.pallas_call(
        join_kernel,
        out_shape=(
            jax.ShapeDtypeStruct((d, 2 * count * ours.shape[1]), F32),
            jax.ShapeDtypeStruct((d, width * len(pieces)), F32),
        ),
        in_specs=[smem] + [VM] * (1 + len(pieces)),
        out_specs=(ANY,) * 2,
        scratch_shapes=[pltpu.SemaphoreType.DMA((count + len(pieces),))],
        compiler_params=PARAMS,
        cost_estimate=cost(0, 2**20),
        name="join",
    )(at, ours, *pieces)


def rest(at, theirs, col):
    count = theirs.shape[0] // col.shape[0]
    return pl.pallas_call(
        rest_kernel,
        out_shape=jax.ShapeDtypeStruct(col.shape, F32),
        in_specs=[pl.BlockSpec(memory_space=pltpu.SMEM), VM, ANY],
        out_specs=ANY,
        scratch_shapes=[pltpu.SemaphoreType.DMA((count,))],
        input_output_aliases={2: 0},
        compiler_params=PARAMS,
        name="rest",
    )(at, theirs, col)


def merged(first, second):
    peak = jnp.maximum(first, second)
    return peak + jnp.log(jnp.exp(first - peak) + jnp.exp(second - peak))


def lse_over(axis, part):
    n = lax.axis_size(axis)
    step = n // 2
    while step:
        part = merged(part, lax.ppermute(part, axis, [(i, i ^ step) for i in range(n)]))
        step //= 2
    return part


def partner(place, k, group):
    return place ^ k if group & (group - 1) == 0 else (place + k) % group


def source(place, k, group):
    return place ^ k if group & (group - 1) == 0 else (place - k) % group


def pairs(n, group, stride, k):
    out = []
    for i in range(n):
        place = (i // stride) % group
        out.append((i, i + (partner(place, k, group) - place) * stride))
    return out


def places(index, group, stride, width):
    own = (index // stride) % group
    return (
        [partner(own, k, group) * width for k in range(group)],
        [source(own, k, group) * width for k in range(group)],
    )


def piece(a, at, count):
    zero = jnp.zeros((), at.dtype)
    return lax.dynamic_slice(
        a, (zero, at), (a.shape[0], a.shape[1] // count), allow_negative_indices=False
    )


def pieces_of(axis, place, stride, part):
    n, group = lax.axis_size(axis), len(place)
    return [
        lax.ppermute(piece(part, place[k], group), axis, pairs(n, group, stride, k))
        for k in range(1, group)
    ]


def all_pieces(axis, group, stride, own):
    n = lax.axis_size(axis)
    return [own] + [lax.ppermute(own, axis, pairs(n, group, stride, k)) for k in range(1, group)]


def body(sources, targets, source_mass, target_mass):
    rows, cols = lax.axis_size("row"), lax.axis_size("col")
    ns, nt = sources.shape[1], targets.shape[1]
    index = lax.axis_index("row")
    halves, _ = places(index, 2, 1, nt // 2)
    row_places, row_sources = places(index, rows // 2, 2, nt // rows)
    col_places, col_sources = places(lax.axis_index("col"), cols, 1, ns // cols)
    laid = [halves[0], row_places[0], col_places[0]]
    laid += [half + at for half in halves for at in row_sources] + col_sources
    laid = jnp.stack(laid)
    sources, halves, row_places, col_places, laid = lax.optimization_barrier(
        (sources, halves, row_places, col_places, laid)
    )
    a = source_mass.reshape(-1, LANES)
    b = target_mass.reshape(-1, LANES)
    f = jnp.zeros_like(a)
    g = jnp.zeros_like(b)
    k, x, y, row_part, col_part = form(sources, targets, a, b)
    for sweep in range(ITERS):
        row_lse = lse_over("col", row_part)
        col_lse = lse_over("row", col_part)
        if sweep < ITERS - 1:
            f, g, row_part, col_part = sums(k, x, y, f, g, row_lse, col_lse, a, b)
    f, g, row_part, col_part = maps(k, x, y, f, g, row_lse, col_lse, a, b)
    pair = pairs(rows, 2, 1, 1)
    other = lax.ppermute(piece(col_part, halves[1], 2), "row", pair)
    chip = merge(laid, 0, col_part, [other], True)
    parted = (pieces_of("row", row_places, 2, chip), pieces_of("col", col_places, 1, row_part))
    column_pieces, row_pieces = parted
    own = merge(laid, 2, row_part, row_pieces, False)
    column_pieces, own = lax.optimization_barrier((column_pieces, own))
    ours = merge(laid, 1, chip, column_pieces, False)
    whole = (all_pieces("row", rows // 2, 2, ours), all_pieces("col", cols, 1, own))
    column_pieces, source_pieces = lax.optimization_barrier(whole)
    ours = jnp.concatenate(column_pieces, axis=0)
    theirs = lax.ppermute(ours, "row", pair)
    target_map, source_map = join(laid, ours, source_pieces)
    target_map = rest(laid, theirs, target_map)
    return f.reshape(-1), g.reshape(-1), source_map, target_map


def solution(mesh):
    in_specs = (P(None, "row"), P(None, "col"), P("row"), P("col"))
    out_specs = (P("row"), P("col"), P(None, "row"), P(None, "col"))
    return jax.shard_map(body, mesh=mesh, in_specs=in_specs, out_specs=out_specs, check_vma=False)
```
